32 devices in a mesh: dp: 8 (over z, x), blk: 4 (over y, core).
Axes of the slice: x: 2, y: 2, z: 4, core: 2. Of those that a mesh axis runs over, the one named last changes fastest.
Arguments:
- entity_table: float32 [65536, 400], P(('dp', 'blk')), may hold values from -1.8 to 1.8
- adagrad_sum: float32 [65536], P(('dp', 'blk')), may hold values from 0.0001 to 0.001
- relations: float32 [7424, 400], replicated, may hold values from -1.8 to 1.8
- owner_map: int32 [65536], replicated, may hold values from 0 to 65535, as said below
- head_ids: int32 [4096], P(('dp', 'blk')), may hold values from 0 to 65535, as said below
- rel_ids: int32 [4096], P(('dp', 'blk')), may hold values from 0 to 7423
- tail_ids: int32 [4096], P(('dp', 'blk')), may hold values from 0 to 65535, as said below
- neg_ids: int32 [16384], P(('dp', 'blk')), may hold values from 0 to 65535, as said below
Outputs:
- new_table: float32 [65536, 400], P(('dp', 'blk'))
- new_sum: float32 [65536], P(('dp', 'blk'))
The draws below stay inside these ranges and needn't reach their ends.
Inputs may be any that keep to these rules, and one draw needn't show every extreme that they name: `owner_map`: A permutation: every storage position appears once. The owner of position p is device p // 2048. `head_ids`: among the 128 heads, 128 tails and 512 negatives of one device taken together, at most 48 are stored on any one owner; in every draw 4 owners receive exactly 48 from every device. `tail_ids`: counted together with the heads and negatives of the same device, as stated for head_ids. `neg_ids`: counted together with the heads and tails of the same device, as stated for head_ids.
All inputs are finite; a program needn't handle non-finite values.
Results may differ from the reference program's by a relative error of at most 0.00005.
Values sent between devices are 32-bit elements; how exact they have to be, the bound alone decides.
No kernel may reach another device: no remote copies, remote signals or barrier semaphores. Data moves between devices by JAX's collectives and lax.ppermute only.
A program may use at most 128 MiB of HBM per device.

```python
import math
import jax
import jax.numpy as jnp
from jax import lax

DIM = 400
NREL = 7424
NEG = 512
ROWS_DEV = 2048
EDGES_DEV = 128
ENTITIES = 65536
EDGES = 4096
CAP = 48
NHOT = 4
N_DP = 8
N_BLK = 4


def draw_owner_map(key, part):
    return jax.random.permutation(jax.random.fold_in(key, 11), ENTITIES).astype(jnp.int32)


def request_layout(key):
    owner_total = ENTITIES // ROWS_DEV
    slot_total = owner_total * CAP
    request_total = 2 * EDGES_DEV + NEG
    placement = draw_owner_map(key, 0)
    inverse = jnp.argsort(placement).astype(jnp.int32)
    hot_owner = jax.random.permutation(jax.random.fold_in(key, 12), owner_total)[:NHOT]
    hot_flag = jnp.zeros((owner_total,), jnp.int32).at[hot_owner].set(1)
    slot_index = jnp.arange(slot_total, dtype=jnp.int32)
    slot_owner = slot_index // CAP
    device_keys = jax.random.split(jax.random.fold_in(key, 13), owner_total)

    def per_device(dev_key):
        jitter = jax.random.randint(jax.random.fold_in(dev_key, 1), (slot_total,), 0, 65536)
        ranking = (jitter + 131072 * hot_flag[slot_owner]) * slot_total + slot_index
        chosen = lax.top_k(ranking, request_total)[1].astype(jnp.int32)
        owner_of = chosen // CAP
        local_row = jax.random.randint(jax.random.fold_in(dev_key, 2), (request_total,), 0, ROWS_DEV)
        positions = owner_of * ROWS_DEV + local_row
        shuffle = jax.random.permutation(jax.random.fold_in(dev_key, 3), request_total)
        return inverse[positions[shuffle]]
    return jax.vmap(per_device)(device_keys).astype(jnp.int32)


def draw_head_ids(key, part):
    return request_layout(key)[:, :EDGES_DEV].reshape(-1)


def draw_tail_ids(key, part):
    return request_layout(key)[:, EDGES_DEV:2 * EDGES_DEV].reshape(-1)


def draw_neg_ids(key, part):
    return request_layout(key)[:, 2 * EDGES_DEV:].reshape(-1)


def set_ends(array, key, least, top_value):
    longest = array.shape.index(max(array.shape))
    spots = []
    for shift in (0, 1):
        where = [jax.random.randint(jax.random.fold_in(key, axis), (), 0, length) for axis, length in enumerate(array.shape)]
        where[longest] = (where[longest] + shift) % array.shape[longest]
        spots.append(tuple(where))
    return array.at[spots[0]].set(least).at[spots[1]].set(top_value)


def level_of(key, shape, pieces, least, top_value):
    level = 1.0
    for axis_at, blocks in pieces:
        heights = jax.random.uniform(jax.random.fold_in(jax.random.fold_in(key, 6), axis_at), (blocks,), jnp.float32, least / len(pieces), top_value / len(pieces))
        level = level * jnp.repeat(jnp.exp(heights), shape[axis_at] // blocks).reshape((-1,) + (1,) * (len(shape) - 1 - axis_at))
    return level


def bell_draw(own_key, shape, scale, reach, cuts=(), held_as=jnp.bfloat16):
    result = jax.random.normal(own_key, shape, jnp.float32) * scale
    if len(cuts) > 0:
        result = level_of(own_key, shape, cuts, -0.22, 0.18) * result
    return jnp.clip(result, min=-reach, max=reach).astype(held_as)


def setup_inputs(seed: int = 0) -> dict:
    streams_of = jax.random.split(jax.random.key(seed), 9)
    entity_table = bell_draw(streams_of[0], (ENTITIES, DIM), 0.3, 1.8, ((0, 32),), jnp.float32)
    adagrad_sum = jnp.clip(jnp.exp(math.log(0.001) - 2.3025852 * jax.random.uniform(streams_of[1], (ENTITIES,), jnp.float32) ** level_of(streams_of[1], (ENTITIES,), ((0, 32),), -0.2, 0.2)), 0.0001, 0.001)
    relations = bell_draw(streams_of[2], (NREL, DIM), 0.3, 1.8, (), jnp.float32)
    owner_map = draw_owner_map(jax.random.fold_in(streams_of[8], 71), 0)
    head_ids = draw_head_ids(jax.random.fold_in(streams_of[8], 71), 0)
    rel_ids = set_ends(jax.random.randint(streams_of[5], (EDGES,), 0, NREL), jax.random.fold_in(streams_of[5], 1), 0, NREL - 1).astype(jnp.int32)
    tail_ids = draw_tail_ids(jax.random.fold_in(streams_of[8], 71), 0)
    neg_ids = draw_neg_ids(jax.random.fold_in(streams_of[8], 71), 0)
    return dict(entity_table=entity_table, adagrad_sum=adagrad_sum, relations=relations, owner_map=owner_map, head_ids=head_ids, rel_ids=rel_ids, tail_ids=tail_ids, neg_ids=neg_ids)


MARGIN = 10.0
EPSILON = 1e-05
LEARNING_RATE = 0.1

def negative_terms(queries, neg_block, weight):
    query_sq = lax.optimization_barrier(jnp.sum(queries * queries, axis=1))
    block_sq = lax.optimization_barrier(jnp.sum(neg_block * neg_block, axis=1))
    inner_prod = jnp.dot(queries, neg_block.T, precision=lax.Precision.HIGHEST, preferred_element_type=jnp.float32)
    distance = jnp.sqrt(query_sq[:, None] + block_sq[None, :] - 2.0 * inner_prod + EPSILON)
    coefficient = -jax.nn.sigmoid(MARGIN - distance) / (weight * distance)
    grad_query = queries * lax.optimization_barrier(jnp.sum(coefficient, axis=1))[:, None] - jnp.dot(coefficient, neg_block, precision=lax.Precision.HIGHEST, preferred_element_type=jnp.float32)
    grad_block = neg_block * lax.optimization_barrier(jnp.sum(coefficient, axis=0))[:, None] - jnp.dot(coefficient.T, queries, precision=lax.Precision.HIGHEST, preferred_element_type=jnp.float32)
    return (grad_query, grad_block)

def reference(entity_table, adagrad_sum, relations, owner_map, head_ids, rel_ids, tail_ids, neg_ids):
    head_pos = owner_map[head_ids]
    tail_pos = owner_map[tail_ids]
    neg_pos = owner_map[neg_ids]
    queries = entity_table[head_pos] + relations[rel_ids]
    residue = queries - entity_table[tail_pos]
    pos_dist = jnp.sqrt(lax.optimization_barrier(jnp.sum(residue * residue, axis=1)) + EPSILON)
    grad_pos = (jax.nn.sigmoid(pos_dist - MARGIN) / pos_dist)[:, None] * residue
    weight = float(N_BLK * NEG)
    grouped_queries = queries.reshape(N_DP, N_BLK * EDGES_DEV, DIM)
    grouped_negs = entity_table[neg_pos].reshape(N_DP, N_BLK * NEG, DIM)

    def per_group(paired):
        return negative_terms(paired[0], paired[1], weight)
    grad_neg, block_grad = lax.map(per_group, (grouped_queries, grouped_negs))
    summed = jnp.zeros_like(entity_table)
    summed = summed.at[head_pos].add(grad_pos + grad_neg.reshape(-1, DIM))
    summed = summed.at[tail_pos].add(-grad_pos)
    summed = summed.at[neg_pos].add(block_grad.reshape(-1, DIM))
    new_sum = adagrad_sum + lax.optimization_barrier(jnp.mean(summed * summed, axis=1))
    new_table = entity_table - LEARNING_RATE * summed / jnp.sqrt(new_sum)[:, None]
    return (new_table, new_sum)
```

```python
import functools

import jax
import jax.numpy as jnp
from jax import lax
from jax.experimental import pallas as pl
from jax.experimental.pallas import tpu as pltpu
from jax.sharding import PartitionSpec as P

MARGIN = 10.0
EPSILON = 1e-05
LEARNING_RATE = 0.1
LANES = 128
SUBLANES = 8
VMEM_BYTES = 40 * 1024 * 1024
HIGHEST = lax.Precision.HIGHEST


class Packing:
    def __init__(self, width, owners, capacity):
        self.width = width
        self.owners = owners
        self.capacity = capacity
        self.full = width // LANES
        self.rest = width - self.full * LANES
        assert 0 < self.rest <= LANES // SUBLANES and capacity % SUBLANES == 0
        self.shared = capacity // SUBLANES
        self.groups = self.full + 1
        self.wide = self.groups * LANES
        self.rests_at = self.full * capacity
        self.stride = -(-(self.rests_at + self.shared) // SUBLANES) * SUBLANES
        self.slots = owners * capacity
        self.rows = owners * self.stride


def compiler_params():
    return pltpu.CompilerParams(vmem_limit_bytes=VMEM_BYTES)


def vmem():
    return pl.BlockSpec(memory_space=pltpu.VMEM)


def smem():
    return pl.BlockSpec(memory_space=pltpu.SMEM)


def split(value):
    high = value.astype(jnp.bfloat16)
    low = (value - high.astype(jnp.float32)).astype(jnp.bfloat16)
    return high, low


def dot_halves(left, right, contract):
    numbers = (contract, ((), ()))

    def dot(a, b):
        return lax.dot_general(a, b, numbers, preferred_element_type=jnp.float32)

    return dot(left[0], right[0]) + (dot(left[0], right[1]) + dot(left[1], right[0]))


def loop(count, body):
    def step(index, carry):
        body(index)
        return carry

    lax.fori_loop(0, count, step, 0)


def expand_rests(pack, packed_ref, rests_ref):
    lane = lax.broadcasted_iota(jnp.int32, (pack.shared, LANES), 1)

    def body(owner):
        block = packed_ref[pl.ds(owner * pack.stride + pack.rests_at, pack.shared), :]
        for j in range(SUBLANES):
            moved = block if j == 0 else pltpu.roll(block, LANES - j * pack.rest, axis=1)
            rests_ref[pl.ds(owner * pack.capacity + j, pack.shared, stride=SUBLANES), :] = (
                jnp.where(lane < pack.rest, moved, 0.0)
            )

    loop(pack.owners, body)


def rows_kernel(pack, columns_ref, rows_ref):
    fill = jnp.zeros((pack.wide - pack.width, LANES), jnp.float32)
    for block in range(columns_ref.shape[1] // LANES):
        at = slice(block * LANES, (block + 1) * LANES)
        tile = jnp.concatenate([columns_ref[:, at], fill], axis=0)
        for c in range(pack.groups):
            rows_ref[at, c, :] = tile[c * LANES : (c + 1) * LANES].T


def to_rows(pack, columns):
    count = columns.shape[1]
    return pl.pallas_call(
        functools.partial(rows_kernel, pack),
        out_shape=jax.ShapeDtypeStruct((count, pack.groups, LANES), jnp.float32),
        in_specs=[vmem()],
        out_specs=vmem(),
        compiler_params=compiler_params(),
        name="table_rows",
    )(columns)


def serve_kernel(pack, asked_ref, table_ref, out_ref):
    lane = lax.broadcasted_iota(jnp.int32, (pack.groups, LANES), 1) // pack.rest

    def body(group):
        owner = group // pack.shared
        inner = group % pack.shared
        base = owner * pack.stride
        shared = None
        for j in range(SUBLANES):
            value = table_ref[jnp.maximum(asked_ref[group * SUBLANES + j], 0)]
            out_ref[pl.ds(base + (inner * SUBLANES + j) * pack.full, pack.full), :] = value[
                : pack.full
            ]
            if j == 0:
                shared = value
            else:
                shared = jnp.where(lane == j, pltpu.roll(value, j * pack.rest, axis=1), shared)
        out_ref[pl.ds(base + pack.rests_at + inner, 1), :] = shared[pack.full :]

    loop(pack.slots // SUBLANES, body)


def serve(pack, asked, table_rows):
    return pl.pallas_call(
        functools.partial(serve_kernel, pack),
        out_shape=jax.ShapeDtypeStruct((pack.rows, LANES), jnp.float32),
        in_specs=[smem(), vmem()],
        out_specs=vmem(),
        compiler_params=compiler_params(),
        name="serve_rows",
    )(asked, table_rows)


def unpack_kernel(
    pack, edges, address_ref, slot_ref, packed_ref, relation_ref,
    query_ref, positive_ref, negative_ref, rests_ref, rows_ref,
):
    expand_rests(pack, packed_ref, rests_ref)
    count = rows_ref.shape[0]

    def body(group):
        for j in range(SUBLANES):
            row = group * SUBLANES + j
            rows_ref[row, : pack.full, :] = packed_ref[pl.ds(address_ref[row], pack.full), :]
            rows_ref[row, pack.full :, :] = rests_ref[pl.ds(slot_ref[row], 1), :]

    loop(count // SUBLANES, body)
    for c in range(pack.groups):
        negative_ref[:, c * LANES : (c + 1) * LANES] = rows_ref[2 * edges :, c, :]

    def columns(first):
        parts = [rows_ref[first : first + edges, c, :].T for c in range(pack.groups)]
        return jnp.concatenate(parts, axis=0)[: pack.width]

    queries = columns(0) + relation_ref[...]
    residue = queries - columns(edges)
    distance = jnp.sqrt(jnp.sum(residue * residue, axis=0, keepdims=True) + EPSILON)
    query_ref[...] = queries
    positive_ref[...] = jax.nn.sigmoid(distance - MARGIN) / distance * residue


def unpack(pack, edges, negatives, address, slot, packed, relation_rows):
    shape = jax.ShapeDtypeStruct
    return pl.pallas_call(
        functools.partial(unpack_kernel, pack, edges),
        out_shape=(
            shape((pack.width, edges), jnp.float32),
            shape((pack.width, edges), jnp.float32),
            shape((negatives, pack.wide), jnp.float32),
        ),
        in_specs=[smem(), smem(), vmem(), vmem()],
        out_specs=(vmem(), vmem(), vmem()),
        scratch_shapes=[
            pltpu.VMEM((pack.slots, LANES), jnp.float32),
            pltpu.VMEM((2 * edges + negatives, pack.groups, LANES), jnp.float32),
        ],
        compiler_params=compiler_params(),
        name="unpack_rows",
    )(address, slot, packed, relation_rows)


def negatives_kernel(pack, blocks, weight, *refs):
    negative_ref = refs[0]
    query_refs = refs[1 : 1 + blocks]
    block_ref, *part_refs = refs[1 + blocks :]
    negatives = negative_ref[...]
    queries = jnp.concatenate([ref[...] for ref in query_refs], axis=1)
    queries = jnp.concatenate(
        [queries, jnp.zeros((pack.wide - pack.width, queries.shape[1]), jnp.float32)], axis=0
    )
    query_sq = jnp.sum(queries * queries, axis=0, keepdims=True)
    block_sq = jnp.sum(negatives * negatives, axis=1, keepdims=True)
    inner = jnp.dot(negatives, queries, precision=HIGHEST, preferred_element_type=jnp.float32)
    distance = jnp.sqrt(query_sq + block_sq - 2.0 * inner + EPSILON)
    coefficient = -1.0 / ((1.0 + jnp.exp(distance - MARGIN)) * (weight * distance))
    query_halves = split(queries)
    coefficient_halves = split(coefficient)
    negative_halves = split(negatives.T)
    block_ref[...] = negatives * jnp.sum(coefficient, axis=1, keepdims=True) - dot_halves(
        coefficient_halves, query_halves, ((1,), (1,))
    )
    part = queries * jnp.sum(coefficient, axis=0, keepdims=True) - dot_halves(
        negative_halves, coefficient_halves, ((1,), (0,))
    )
    width = query_refs[0].shape[1]
    for index, ref in enumerate(part_refs):
        ref[...] = part[: pack.width, index * width : (index + 1) * width]


def negative_terms(pack, weight, negatives, queries):
    shape = jax.ShapeDtypeStruct
    return pl.pallas_call(
        functools.partial(negatives_kernel, pack, len(queries), weight),
        out_shape=(shape(negatives.shape, jnp.float32),)
        + tuple(shape(q.shape, jnp.float32) for q in queries),
        in_specs=[vmem()] * (1 + len(queries)),
        out_specs=(vmem(),) * (1 + len(queries)),
        compiler_params=compiler_params(),
        name="negative_terms",
    )(negatives, *queries)


def pack_kernel(
    pack, edges, address_ref, slot_ref, query_grad_ref, positive_ref, block_ref,
    out_ref, rests_ref, rows_ref,
):
    out_ref[...] = jnp.zeros_like(out_ref)
    rests_ref[...] = jnp.zeros_like(rests_ref)
    positive = positive_ref[...]
    fill = jnp.zeros((pack.wide - pack.width, edges), jnp.float32)
    heads = jnp.concatenate([query_grad_ref[...] + positive, fill], axis=0)
    tails = jnp.concatenate([-positive, fill], axis=0)
    for c in range(pack.groups):
        at = slice(c * LANES, (c + 1) * LANES)
        rows_ref[:edges, c, :] = heads[at].T
        rows_ref[edges : 2 * edges, c, :] = tails[at].T
        rows_ref[2 * edges :, c, :] = block_ref[:, at]

    def body(group):
        for j in range(SUBLANES):
            row = group * SUBLANES + j
            value = rows_ref[row]
            out_ref[pl.ds(address_ref[row], pack.full), :] = value[: pack.full]
            rests_ref[pl.ds(slot_ref[row], 1), :] = value[pack.full :]

    loop(rows_ref.shape[0] // SUBLANES, body)

    def share(owner):
        total = None
        for j in range(SUBLANES):
            block = rests_ref[pl.ds(owner * pack.capacity + j, pack.shared, stride=SUBLANES), :]
            moved = block if j == 0 else pltpu.roll(block, j * pack.rest, axis=1)
            total = moved if total is None else total + moved
        out_ref[pl.ds(owner * pack.stride + pack.rests_at, pack.shared), :] = total

    loop(pack.owners, share)


def pack_gradients(pack, address, slot, query_grad, positive, block_grad):
    edges = positive.shape[1]
    return pl.pallas_call(
        functools.partial(pack_kernel, pack, edges),
        out_shape=jax.ShapeDtypeStruct((pack.rows, LANES), jnp.float32),
        in_specs=[smem(), smem(), vmem(), vmem(), vmem()],
        out_specs=vmem(),
        scratch_shapes=[
            pltpu.VMEM((pack.slots, LANES), jnp.float32),
            pltpu.VMEM((2 * edges + block_grad.shape[0], pack.groups, LANES), jnp.float32),
        ],
        compiler_params=compiler_params(),
        name="pack_gradients",
    )(address, slot, query_grad, positive, block_grad)


def update_kernel(
    pack, columns, asked_ref, packed_ref, sum_ref, table_ref,
    new_table_ref, new_sum_ref, rests_ref, rows_ref, high_ref, low_ref,
):
    @pl.when(pl.program_id(0) == 0)
    def _():
        expand_rests(pack, packed_ref, rests_ref)

        def body(owner):
            rows = pl.ds(owner * pack.capacity, pack.capacity)
            for c in range(pack.full):
                rows_ref[rows, c * LANES : (c + 1) * LANES] = packed_ref[
                    pl.ds(owner * pack.stride + c, pack.capacity, stride=pack.full), :
                ]
            rows_ref[rows, pack.full * LANES :] = rests_ref[rows, :]

        loop(pack.owners, body)
        high, low = split(rows_ref[...].T)
        high_ref[...] = high[: pack.width]
        low_ref[...] = low[: pack.width]

    row = lax.broadcasted_iota(jnp.int32, (columns, pack.slots), 0) + pl.program_id(0) * columns
    chosen = (row == asked_ref[...]).astype(jnp.float32).astype(jnp.bfloat16)

    def pick(half_ref):
        return lax.dot_general(
            half_ref[...], chosen, (((1,), (1,)), ((), ())), preferred_element_type=jnp.float32
        )

    summed = pick(high_ref) + pick(low_ref)
    new_sum = sum_ref[...] + jnp.sum(summed * summed, axis=0, keepdims=True) / pack.width
    new_sum_ref[...] = new_sum
    new_table_ref[...] = table_ref[...] - summed * (LEARNING_RATE / jnp.sqrt(new_sum))


def update(pack, asked, packed, adagrad_sum, table_columns):
    width, rows = table_columns.shape
    columns = 256
    shape = jax.ShapeDtypeStruct
    return pl.pallas_call(
        functools.partial(update_kernel, pack, columns),
        grid=(rows // columns,),
        out_shape=(shape((width, rows), jnp.float32), shape((1, rows), jnp.float32)),
        in_specs=[
            pl.BlockSpec((1, pack.slots), lambda i: (0, 0)),
            pl.BlockSpec((pack.rows, LANES), lambda i: (0, 0)),
            pl.BlockSpec((1, columns), lambda i: (0, i)),
            pl.BlockSpec((width, columns), lambda i: (0, i)),
        ],
        out_specs=(
            pl.BlockSpec((width, columns), lambda i: (0, i)),
            pl.BlockSpec((1, columns), lambda i: (0, i)),
        ),
        scratch_shapes=[
            pltpu.VMEM((pack.slots, LANES), jnp.float32),
            pltpu.VMEM((pack.slots, pack.wide), jnp.float32),
            pltpu.VMEM((width, pack.slots), jnp.bfloat16),
            pltpu.VMEM((width, pack.slots), jnp.bfloat16),
        ],
        compiler_params=compiler_params(),
        name="update_table",
    )(asked, packed, adagrad_sum, table_columns)


def exchange(payload):
    return lax.all_to_all(payload, ("dp", "blk"), split_axis=0, concat_axis=0, tiled=True)


def to_sibling(value, blk_count):
    return lax.ppermute(value, "blk", [(i, i ^ 1) for i in range(blk_count)])


def to_chip(value, blk_count, hops):
    return lax.ppermute(
        value, "blk", [(i, (i + 2 * hops) % blk_count) for i in range(blk_count)]
    )


def on_device(
    entity_table, adagrad_sum, relations, owner_map, head_ids, rel_ids, tail_ids, neg_ids
):
    dp_count = lax.axis_size("dp")
    blk_count = lax.axis_size("blk")
    owner_count = dp_count * blk_count
    chip_count = blk_count // 2
    rows_here, width = entity_table.shape
    edge_count = head_ids.shape[0]
    neg_count = neg_ids.shape[0]
    request_count = 2 * edge_count + neg_count
    capacity = -(-2 * request_count // owner_count // SUBLANES) * SUBLANES
    pack = Packing(width, owner_count, capacity)
    wanted = jnp.concatenate([head_ids, tail_ids, neg_ids])
    position = owner_map[wanted]
    owner_of = position // rows_here
    local_row = position % rows_here
    onehot = (owner_of[:, None] == jnp.arange(owner_count, dtype=jnp.int32)[None, :]).astype(
        jnp.int32
    )
    before = jnp.cumsum(onehot, axis=0) - onehot
    rank_in = jnp.sum(before * onehot, axis=1)
    slot_of = owner_of * capacity + rank_in
    address = owner_of * pack.stride + rank_in * pack.full
    requests = jnp.full((pack.slots,), -1, jnp.int32).at[slot_of].set(local_row)
    asked = exchange(requests.reshape(owner_count, capacity)).reshape(-1)
    served = serve(pack, asked, to_rows(pack, entity_table.T))
    fetched = exchange(served.reshape(owner_count, pack.stride, LANES))
    queries, positive, negatives = unpack(
        pack, edge_count, neg_count, address, slot_of,
        fetched.reshape(pack.rows, LANES), relations[rel_ids].T,
    )
    group = []
    for hops in range(chip_count):
        same = queries if hops == 0 else to_chip(queries, blk_count, hops)
        group += [same, to_sibling(same, blk_count)]
    weight = float(blk_count * neg_count)
    block_grad, *parts = negative_terms(pack, weight, negatives, group)
    query_grad = None
    for hops in range(chip_count):
        total = parts[2 * hops] + to_sibling(parts[2 * hops + 1], blk_count)
        if hops:
            total = to_chip(total, blk_count, chip_count - hops)
        query_grad = total if query_grad is None else query_grad + total
    outgoing = pack_gradients(pack, address, slot_of, query_grad, positive, block_grad)
    incoming = exchange(outgoing.reshape(owner_count, pack.stride, LANES))
    new_columns, new_sum = update(
        pack, asked.reshape(1, -1), incoming.reshape(pack.rows, LANES),
        adagrad_sum.reshape(1, -1), entity_table.T,
    )
    return (new_columns.T, new_sum.reshape(-1))


def solution(mesh):
    return jax.shard_map(
        on_device,
        mesh=mesh,
        in_specs=(
            P(("dp", "blk"), None),
            P(("dp", "blk")),
            P(),
            P(),
            P(("dp", "blk")),
            P(("dp", "blk")),
            P(("dp", "blk")),
            P(("dp", "blk")),
        ),
        out_specs=(P(("dp", "blk"), None), P(("dp", "blk"))),
        check_vma=False,
    )
```

```python
import functools

import jax
import jax.numpy as jnp
from jax import lax
from jax.experimental import pallas as pl
from jax.experimental.pallas import tpu as pltpu
from jax.sharding import PartitionSpec as P

MARGIN = 10.0
EPSILON = 1e-05
LEARNING_RATE = 0.1
LANES = 128
SUBLANES = 8
VMEM_BYTES = 40 * 1024 * 1024
HIGHEST = lax.Precision.HIGHEST


class Packing:
    def __init__(self, width, owners, capacity):
        self.width = width
        self.owners = owners
        self.capacity = capacity
        self.full = width // LANES
        self.rest = width - self.full * LANES
        assert 0 < self.rest <= LANES // SUBLANES and capacity % SUBLANES == 0
        self.shared = capacity // SUBLANES
        self.groups = self.full + 1
        self.wide = self.groups * LANES
        self.rests_at = self.full * capacity
        self.stride = -(-(self.rests_at + self.shared) // SUBLANES) * SUBLANES
        self.slots = owners * capacity
        self.rows = owners * self.stride


def compiler_params():
    return pltpu.CompilerParams(vmem_limit_bytes=VMEM_BYTES)


def vmem():
    return pl.BlockSpec(memory_space=pltpu.VMEM)


def smem():
    return pl.BlockSpec(memory_space=pltpu.SMEM)


def split(value):
    high = value.astype(jnp.bfloat16)
    low = (value - high.astype(jnp.float32)).astype(jnp.bfloat16)
    return high, low


def dot_halves(left, right, contract):
    numbers = (contract, ((), ()))

    def dot(a, b):
        return lax.dot_general(a, b, numbers, preferred_element_type=jnp.float32)

    return dot(left[0], right[0]) + (dot(left[0], right[1]) + dot(left[1], right[0]))


def loop(count, body):
    def step(index, carry):
        body(index)
        return carry

    lax.fori_loop(0, count, step, 0)


def expand_rests(pack, packed_ref, rests_ref):
    lane = lax.broadcasted_iota(jnp.int32, (pack.shared, LANES), 1)

    def body(owner):
        block = packed_ref[pl.ds(owner * pack.stride + pack.rests_at, pack.shared), :]
        for j in range(SUBLANES):
            moved = block if j == 0 else pltpu.roll(block, LANES - j * pack.rest, axis=1)
            rests_ref[pl.ds(owner * pack.capacity + j, pack.shared, stride=SUBLANES), :] = (
                jnp.where(lane < pack.rest, moved, 0.0)
            )

    loop(pack.owners, body)


def one_hot(mask):
    return mask.astype(jnp.float32).astype(jnp.bfloat16)


def request_kernel(
    pack, rows_here, map_ref, head_ref, tail_ref, negative_ref,
    request_ref, address_ref, slot_ref,
):
    ids = jnp.concatenate([head_ref[...], tail_ref[...], negative_ref[...]], axis=1)
    count = ids.shape[1]
    lines = map_ref.shape[0]

    def iota(rows, axis):
        return lax.broadcasted_iota(jnp.int32, (rows, count), axis)

    line_chosen = one_hot(iota(lines, 0) == ids // LANES)
    table = map_ref[...].T
    digits = [(table >> shift) & 255 for shift in range(0, 24, 8)]
    stacked = jnp.concatenate(digits, axis=0).astype(jnp.float32).astype(jnp.bfloat16)
    found = jnp.dot(stacked, line_chosen, preferred_element_type=jnp.float32)
    found = found[:LANES] + 256.0 * found[LANES : 2 * LANES] + 65536.0 * found[2 * LANES :]
    found = jnp.where(iota(LANES, 0) == ids % LANES, found, 0.0)
    position = jnp.sum(found, axis=0, keepdims=True).astype(jnp.int32)
    owner = position // rows_here
    row = position % rows_here
    to_owner = iota(pack.owners, 0) == owner
    earlier = one_hot(iota(count, 0) < iota(count, 1))
    before = jnp.dot(one_hot(to_owner), earlier, preferred_element_type=jnp.float32)
    rank = jnp.sum(jnp.where(to_owner, before, 0.0), axis=0, keepdims=True).astype(jnp.int32)
    slot_ref[...] = owner * pack.capacity + rank
    address_ref[...] = owner * pack.stride + rank * pack.full
    at_rank = one_hot(iota(pack.capacity, 0) == rank)
    absent = row - rows_here

    def place(values):
        chosen = jnp.where(to_owner, values.astype(jnp.float32), 0.0).astype(jnp.bfloat16)
        return lax.dot_general(
            chosen, at_rank, (((1,), (1,)), ((), ())), preferred_element_type=jnp.float32
        )

    high = -((-absent) // 256)
    low = absent - high * 256
    request_ref[:, 0, :] = (place(high) * 256.0 + place(low)).astype(jnp.int32) + rows_here


def build_requests(pack, rows_here, owner_map, head_ids, tail_ids, neg_ids):
    count = head_ids.shape[0] + tail_ids.shape[0] + neg_ids.shape[0]
    shape = jax.ShapeDtypeStruct
    return pl.pallas_call(
        functools.partial(request_kernel, pack, rows_here),
        out_shape=(
            shape((pack.owners, 1, pack.capacity), jnp.int32),
            shape((1, count), jnp.int32),
            shape((1, count), jnp.int32),
        ),
        in_specs=[vmem()] * 4,
        out_specs=(vmem(),) * 3,
        compiler_params=compiler_params(),
        name="build_requests",
    )(
        owner_map.reshape(-1, LANES), head_ids.reshape(1, -1), tail_ids.reshape(1, -1),
        neg_ids.reshape(1, -1),
    )


def rows_kernel(pack, columns_ref, rows_ref):
    count = columns_ref.shape[1]
    fill = jnp.zeros((pack.wide - pack.width, LANES), jnp.float32)
    for block in range(count // LANES):
        at = slice(block * LANES, (block + 1) * LANES)
        tile = jnp.concatenate([columns_ref[:, at], fill], axis=0)
        for c in range(pack.groups):
            rows_ref[at, c, :] = tile[c * LANES : (c + 1) * LANES].T
    rows_ref[count:] = jnp.zeros((SUBLANES, pack.groups, LANES), jnp.float32)


def to_rows(pack, columns):
    count = columns.shape[1]
    return pl.pallas_call(
        functools.partial(rows_kernel, pack),
        out_shape=jax.ShapeDtypeStruct((count + SUBLANES, pack.groups, LANES), jnp.float32),
        in_specs=[vmem()],
        out_specs=vmem(),
        compiler_params=compiler_params(),
        name="table_rows",
    )(columns)


def serve_kernel(pack, asked_ref, table_ref, out_ref):
    lane = lax.broadcasted_iota(jnp.int32, (pack.groups, LANES), 1) // pack.rest

    def body(owner):
        base = pl.multiple_of(owner * pack.stride, SUBLANES)
        for group in range(pack.shared):
            first = group * SUBLANES
            values = [table_ref[asked_ref[owner, 0, first + j]] for j in range(SUBLANES)]
            shared = values[0]
            for j in range(1, SUBLANES):
                moved = pltpu.roll(values[j], j * pack.rest, axis=1)
                shared = jnp.where(lane == j, moved, shared)
            for j in range(SUBLANES):
                out_ref[pl.ds(base + (first + j) * pack.full, pack.full), :] = values[j][
                    : pack.full
                ]
            out_ref[pl.ds(base + pack.rests_at + group, 1), :] = shared[pack.full :]

    loop(pack.owners, body)


def serve(pack, asked, table_rows):
    return pl.pallas_call(
        functools.partial(serve_kernel, pack),
        out_shape=jax.ShapeDtypeStruct((pack.rows, LANES), jnp.float32),
        in_specs=[smem(), vmem()],
        out_specs=vmem(),
        compiler_params=compiler_params(),
        name="serve_rows",
    )(asked, table_rows)


def unpack_kernel(
    pack, edges, address_ref, slot_ref, packed_ref, relation_ref,
    query_ref, positive_ref, negative_ref, rests_ref, rows_ref,
):
    expand_rests(pack, packed_ref, rests_ref)
    count = rows_ref.shape[0]

    def body(group):
        first = group * SUBLANES
        values = []
        for j in range(SUBLANES):
            values.append(
                (
                    packed_ref[pl.ds(address_ref[0, first + j], pack.full), :],
                    rests_ref[pl.ds(slot_ref[0, first + j], 1), :],
                )
            )
        for j, (groups, rest) in enumerate(values):
            rows_ref[first + j, : pack.full, :] = groups
            rows_ref[first + j, pack.full :, :] = rest

    loop(count // SUBLANES, body)
    for c in range(pack.groups):
        negative_ref[:, c * LANES : (c + 1) * LANES] = rows_ref[2 * edges :, c, :]

    def columns(first):
        parts = [rows_ref[first : first + edges, c, :].T for c in range(pack.groups)]
        return jnp.concatenate(parts, axis=0)[: pack.width]

    queries = columns(0) + relation_ref[...]
    residue = queries - columns(edges)
    distance = jnp.sqrt(jnp.sum(residue * residue, axis=0, keepdims=True) + EPSILON)
    query_ref[...] = queries
    positive_ref[...] = jax.nn.sigmoid(distance - MARGIN) / distance * residue


def unpack(pack, edges, negatives, address, slot, packed, relation_rows):
    shape = jax.ShapeDtypeStruct
    return pl.pallas_call(
        functools.partial(unpack_kernel, pack, edges),
        out_shape=(
            shape((pack.width, edges), jnp.float32),
            shape((pack.width, edges), jnp.float32),
            shape((negatives, pack.wide), jnp.float32),
        ),
        in_specs=[smem(), smem(), vmem(), vmem()],
        out_specs=(vmem(), vmem(), vmem()),
        scratch_shapes=[
            pltpu.VMEM((pack.slots, LANES), jnp.float32),
            pltpu.VMEM((2 * edges + negatives, pack.groups, LANES), jnp.float32),
        ],
        compiler_params=compiler_params(),
        name="unpack_rows",
    )(address, slot, packed, relation_rows)


def negatives_kernel(pack, blocks, weight, *refs):
    negative_ref = refs[0]
    query_refs = refs[1 : 1 + blocks]
    block_ref, *part_refs = refs[1 + blocks :]
    negatives = negative_ref[...]
    queries = jnp.concatenate([ref[...] for ref in query_refs], axis=1)
    queries = jnp.concatenate(
        [queries, jnp.zeros((pack.wide - pack.width, queries.shape[1]), jnp.float32)], axis=0
    )
    query_sq = jnp.sum(queries * queries, axis=0, keepdims=True)
    block_sq = jnp.sum(negatives * negatives, axis=1, keepdims=True)
    inner = jnp.dot(negatives, queries, precision=HIGHEST, preferred_element_type=jnp.float32)
    distance = jnp.sqrt(query_sq + block_sq - 2.0 * inner + EPSILON)
    coefficient = -1.0 / ((1.0 + jnp.exp(distance - MARGIN)) * (weight * distance))
    query_halves = split(queries)
    coefficient_halves = split(coefficient)
    negative_halves = split(negatives.T)
    block_ref[...] = negatives * jnp.sum(coefficient, axis=1, keepdims=True) - dot_halves(
        coefficient_halves, query_halves, ((1,), (1,))
    )
    part = queries * jnp.sum(coefficient, axis=0, keepdims=True) - dot_halves(
        negative_halves, coefficient_halves, ((1,), (0,))
    )
    width = query_refs[0].shape[1]
    for index, ref in enumerate(part_refs):
        ref[...] = part[: pack.width, index * width : (index + 1) * width]


def negative_terms(pack, weight, negatives, queries):
    shape = jax.ShapeDtypeStruct
    return pl.pallas_call(
        functools.partial(negatives_kernel, pack, len(queries), weight),
        out_shape=(shape(negatives.shape, jnp.float32),)
        + tuple(shape(q.shape, jnp.float32) for q in queries),
        in_specs=[vmem()] * (1 + len(queries)),
        out_specs=(vmem(),) * (1 + len(queries)),
        compiler_params=compiler_params(),
        name="negative_terms",
    )(negatives, *queries)


def pack_kernel(
    pack, edges, address_ref, slot_ref, query_grad_ref, positive_ref, block_ref,
    out_ref, rests_ref, rows_ref,
):
    out_ref[...] = jnp.zeros_like(out_ref)
    rests_ref[...] = jnp.zeros_like(rests_ref)
    positive = positive_ref[...]
    fill = jnp.zeros((pack.wide - pack.width, edges), jnp.float32)
    heads = jnp.concatenate([query_grad_ref[...] + positive, fill], axis=0)
    tails = jnp.concatenate([-positive, fill], axis=0)
    for c in range(pack.groups):
        at = slice(c * LANES, (c + 1) * LANES)
        rows_ref[:edges, c, :] = heads[at].T
        rows_ref[edges : 2 * edges, c, :] = tails[at].T
        rows_ref[2 * edges :, c, :] = block_ref[:, at]

    def body(group):
        first = group * SUBLANES
        values = [rows_ref[first + j] for j in range(SUBLANES)]
        for j, value in enumerate(values):
            out_ref[pl.ds(address_ref[0, first + j], pack.full), :] = value[: pack.full]
            rests_ref[pl.ds(slot_ref[0, first + j], 1), :] = value[pack.full :]

    loop(rows_ref.shape[0] // SUBLANES, body)

    def share(owner):
        total = None
        for j in range(SUBLANES):
            block = rests_ref[pl.ds(owner * pack.capacity + j, pack.shared, stride=SUBLANES), :]
            moved = block if j == 0 else pltpu.roll(block, j * pack.rest, axis=1)
            total = moved if total is None else total + moved
        out_ref[pl.ds(owner * pack.stride + pack.rests_at, pack.shared), :] = total

    loop(pack.owners, share)


def pack_gradients(pack, address, slot, query_grad, positive, block_grad):
    edges = positive.shape[1]
    return pl.pallas_call(
        functools.partial(pack_kernel, pack, edges),
        out_shape=jax.ShapeDtypeStruct((pack.rows, LANES), jnp.float32),
        in_specs=[smem(), smem(), vmem(), vmem(), vmem()],
        out_specs=vmem(),
        scratch_shapes=[
            pltpu.VMEM((pack.slots, LANES), jnp.float32),
            pltpu.VMEM((2 * edges + block_grad.shape[0], pack.groups, LANES), jnp.float32),
        ],
        compiler_params=compiler_params(),
        name="pack_gradients",
    )(address, slot, query_grad, positive, block_grad)


def update_kernel(
    pack, columns, asked_ref, packed_ref, sum_ref, table_ref,
    new_table_ref, new_sum_ref, rests_ref, rows_ref, high_ref, low_ref,
):
    @pl.when(pl.program_id(0) == 0)
    def _():
        expand_rests(pack, packed_ref, rests_ref)

        def body(owner):
            rows = pl.ds(owner * pack.capacity, pack.capacity)
            for c in range(pack.full):
                rows_ref[rows, c * LANES : (c + 1) * LANES] = packed_ref[
                    pl.ds(owner * pack.stride + c, pack.capacity, stride=pack.full), :
                ]
            rows_ref[rows, pack.full * LANES :] = rests_ref[rows, :]

        loop(pack.owners, body)
        high, low = split(rows_ref[...].T)
        high_ref[...] = high[: pack.width]
        low_ref[...] = low[: pack.width]

    row = lax.broadcasted_iota(jnp.int32, (columns, pack.slots), 0) + pl.program_id(0) * columns
    chosen = (row == asked_ref[...]).astype(jnp.float32).astype(jnp.bfloat16)

    def pick(half_ref):
        return lax.dot_general(
            half_ref[...], chosen, (((1,), (1,)), ((), ())), preferred_element_type=jnp.float32
        )

    summed = pick(high_ref) + pick(low_ref)
    new_sum = sum_ref[...] + jnp.sum(summed * summed, axis=0, keepdims=True) / pack.width
    new_sum_ref[...] = new_sum
    new_table_ref[...] = table_ref[...] - summed * (LEARNING_RATE / jnp.sqrt(new_sum))


def update(pack, asked, packed, adagrad_sum, table_columns):
    width, rows = table_columns.shape
    columns = 256
    shape = jax.ShapeDtypeStruct
    return pl.pallas_call(
        functools.partial(update_kernel, pack, columns),
        grid=(rows // columns,),
        out_shape=(shape((width, rows), jnp.float32), shape((1, rows), jnp.float32)),
        in_specs=[
            pl.BlockSpec((1, pack.slots), lambda i: (0, 0)),
            pl.BlockSpec((pack.rows, LANES), lambda i: (0, 0)),
            pl.BlockSpec((1, columns), lambda i: (0, i)),
            pl.BlockSpec((width, columns), lambda i: (0, i)),
        ],
        out_specs=(
            pl.BlockSpec((width, columns), lambda i: (0, i)),
            pl.BlockSpec((1, columns), lambda i: (0, i)),
        ),
        scratch_shapes=[
            pltpu.VMEM((pack.slots, LANES), jnp.float32),
            pltpu.VMEM((pack.slots, pack.wide), jnp.float32),
            pltpu.VMEM((width, pack.slots), jnp.bfloat16),
            pltpu.VMEM((width, pack.slots), jnp.bfloat16),
        ],
        compiler_params=compiler_params(),
        name="update_table",
    )(asked, packed, adagrad_sum, table_columns)


def exchange(payload):
    return lax.all_to_all(payload, ("dp", "blk"), split_axis=0, concat_axis=0, tiled=True)


def to_sibling(value, blk_count):
    return lax.ppermute(value, "blk", [(i, i ^ 1) for i in range(blk_count)])


def to_chip(value, blk_count, hops):
    return lax.ppermute(
        value, "blk", [(i, (i + 2 * hops) % blk_count) for i in range(blk_count)]
    )


def on_device(
    entity_table, adagrad_sum, relations, owner_map, head_ids, rel_ids, tail_ids, neg_ids
):
    dp_count = lax.axis_size("dp")
    blk_count = lax.axis_size("blk")
    owner_count = dp_count * blk_count
    chip_count = blk_count // 2
    rows_here, width = entity_table.shape
    edge_count = head_ids.shape[0]
    neg_count = neg_ids.shape[0]
    request_count = 2 * edge_count + neg_count
    capacity = -(-2 * request_count // owner_count // SUBLANES) * SUBLANES
    pack = Packing(width, owner_count, capacity)
    requests, address, slot_of = build_requests(
        pack, rows_here, owner_map, head_ids, tail_ids, neg_ids
    )
    asked = exchange(requests)
    served = serve(pack, asked, to_rows(pack, entity_table.T))
    fetched = exchange(served.reshape(owner_count, pack.stride, LANES))
    queries, positive, negatives = unpack(
        pack, edge_count, neg_count, address, slot_of,
        fetched.reshape(pack.rows, LANES), relations[rel_ids].T,
    )
    group = []
    for hops in range(chip_count):
        same = queries if hops == 0 else to_chip(queries, blk_count, hops)
        group += [same, to_sibling(same, blk_count)]
    weight = float(blk_count * neg_count)
    block_grad, *parts = negative_terms(pack, weight, negatives, group)
    query_grad = None
    for hops in range(chip_count):
        total = parts[2 * hops] + to_sibling(parts[2 * hops + 1], blk_count)
        if hops:
            total = to_chip(total, blk_count, chip_count - hops)
        query_grad = total if query_grad is None else query_grad + total
    outgoing = pack_gradients(pack, address, slot_of, query_grad, positive, block_grad)
    incoming = exchange(outgoing.reshape(owner_count, pack.stride, LANES))
    new_columns, new_sum = update(
        pack, asked.reshape(1, -1), incoming.reshape(pack.rows, LANES),
        adagrad_sum.reshape(1, -1), entity_table.T,
    )
    return (new_columns.T, new_sum.reshape(-1))


def solution(mesh):
    return jax.shard_map(
        on_device,
        mesh=mesh,
        in_specs=(
            P(("dp", "blk"), None),
            P(("dp", "blk")),
            P(),
            P(),
            P(("dp", "blk")),
            P(("dp", "blk")),
            P(("dp", "blk")),
            P(("dp", "blk")),
        ),
        out_specs=(P(("dp", "blk"), None), P(("dp", "blk"))),
        check_vma=False,
    )
```

```python
import functools

import jax
import jax.numpy as jnp
from jax import lax
from jax.experimental import pallas as pl
from jax.experimental.pallas import tpu as pltpu
from jax.sharding import PartitionSpec as P

MARGIN = 10.0
EPSILON = 1e-05
LEARNING_RATE = 0.1
LANES = 128
SUBLANES = 8
VMEM_BYTES = 24 * 1024 * 1024
HIGHEST = lax.Precision.HIGHEST


class Packing:
    def __init__(self, width, owners, capacity):
        self.width = width
        self.owners = owners
        self.capacity = capacity
        self.full = width // LANES
        self.rest = width - self.full * LANES
        assert 0 < self.rest <= LANES // SUBLANES and capacity % SUBLANES == 0
        self.shared = capacity // SUBLANES
        self.groups = self.full + 1
        self.wide = self.groups * LANES
        self.rests_at = self.full * capacity
        self.stride = -(-(self.rests_at + self.shared) // SUBLANES) * SUBLANES
        self.slots = owners * capacity
        self.rows = owners * self.stride


def compiler_params():
    return pltpu.CompilerParams(vmem_limit_bytes=VMEM_BYTES)


def vmem():
    return pl.BlockSpec(memory_space=pltpu.VMEM)


def smem():
    return pl.BlockSpec(memory_space=pltpu.SMEM)


def hbm():
    return pl.BlockSpec(memory_space=pltpu.HBM)


def in_hbm(value):
    return pltpu.with_memory_space_constraint(value, pltpu.HBM)


def split(value):
    high = value.astype(jnp.bfloat16)
    low = (value - high.astype(jnp.float32)).astype(jnp.bfloat16)
    return high, low


def dot_halves(left, right, contract):
    numbers = (contract, ((), ()))

    def dot(a, b):
        return lax.dot_general(a, b, numbers, preferred_element_type=jnp.float32)

    return dot(left[0], right[0]) + (dot(left[0], right[1]) + dot(left[1], right[0]))


def loop(count, body):
    def step(index, carry):
        body(index)
        return carry

    lax.fori_loop(0, count, step, 0)


def expand_rests(pack, packed_ref, shared_ref, rests_ref):
    for owner in range(pack.owners):
        shared_ref[owner * pack.shared : (owner + 1) * pack.shared, :] = packed_ref[
            pl.ds(owner * pack.stride + pack.rests_at, pack.shared), :
        ]
    shared = shared_ref[...]
    lane = lax.broadcasted_iota(jnp.int32, shared.shape, 1)
    for j in range(SUBLANES):
        moved = shared if j == 0 else pltpu.roll(shared, LANES - j * pack.rest, axis=1)
        rests_ref[pl.ds(j, shared.shape[0], stride=SUBLANES), :] = jnp.where(
            lane < pack.rest, moved, 0.0
        )


def rests_scratch(pack):
    return [
        pltpu.VMEM((pack.owners * pack.shared, LANES), jnp.float32),
        pltpu.VMEM((pack.slots, LANES), jnp.float32),
    ]


def row_columns(pack, rows):
    parts = [rows[:, c, :].T for c in range(pack.groups)]
    return jnp.concatenate(parts, axis=0)[: pack.width]


def one_hot(mask):
    return mask.astype(jnp.float32).astype(jnp.bfloat16)


def request_kernel(
    pack, rows_here, map_hbm, head_hbm, tail_hbm, negative_hbm,
    request_ref, address_ref, slot_ref, map_ref, ids_ref, sems,
):
    copies = [pltpu.make_async_copy(map_hbm, map_ref, sems.at[0])]
    first = 0
    for index, source in enumerate((head_hbm, tail_hbm, negative_hbm)):
        target = ids_ref.at[:, pl.ds(first, source.shape[1])]
        copies.append(pltpu.make_async_copy(source, target, sems.at[index + 1]))
        first += source.shape[1]
    for copy in copies:
        copy.start()
    for copy in copies:
        copy.wait()
    ids = ids_ref[...]
    count = ids.shape[1]
    lines = map_ref.shape[0]

    def iota(rows, axis):
        return lax.broadcasted_iota(jnp.int32, (rows, count), axis)

    line_chosen = one_hot(iota(lines, 0) == ids // LANES)
    table = map_ref[...].T
    digits = [(table >> shift) & 255 for shift in range(0, 24, 8)]
    stacked = jnp.concatenate(digits, axis=0).astype(jnp.float32).astype(jnp.bfloat16)
    found = jnp.dot(stacked, line_chosen, preferred_element_type=jnp.float32)
    found = found[:LANES] + 256.0 * found[LANES : 2 * LANES] + 65536.0 * found[2 * LANES :]
    found = jnp.where(iota(LANES, 0) == ids % LANES, found, 0.0)
    position = jnp.sum(found, axis=0, keepdims=True).astype(jnp.int32)
    owner = position // rows_here
    row = position % rows_here
    to_owner = iota(pack.owners, 0) == owner
    earlier = one_hot(iota(count, 0) < iota(count, 1))
    before = jnp.dot(one_hot(to_owner), earlier, preferred_element_type=jnp.float32)
    rank = jnp.sum(jnp.where(to_owner, before, 0.0), axis=0, keepdims=True).astype(jnp.int32)
    slot_ref[...] = owner * pack.capacity + rank
    address_ref[...] = owner * pack.stride + rank * pack.full
    at_rank = one_hot(iota(pack.capacity, 0) == rank)
    absent = row - rows_here

    def place(values):
        chosen = jnp.where(to_owner, values.astype(jnp.float32), 0.0).astype(jnp.bfloat16)
        return lax.dot_general(
            chosen, at_rank, (((1,), (1,)), ((), ())), preferred_element_type=jnp.float32
        )

    high = -((-absent) // 256)
    low = absent - high * 256
    request_ref[:, 0, :] = (place(high) * 256.0 + place(low)).astype(jnp.int32) + rows_here


def build_requests(pack, rows_here, owner_map, head_ids, tail_ids, neg_ids):
    count = head_ids.shape[0] + tail_ids.shape[0] + neg_ids.shape[0]
    shape = jax.ShapeDtypeStruct
    return pl.pallas_call(
        functools.partial(request_kernel, pack, rows_here),
        out_shape=(
            shape((pack.owners, 1, pack.capacity), jnp.int32),
            shape((1, count), jnp.int32),
            shape((1, count), jnp.int32),
        ),
        in_specs=[hbm()] * 4,
        out_specs=(vmem(),) * 3,
        scratch_shapes=[
            pltpu.VMEM((owner_map.shape[0] // LANES, LANES), jnp.int32),
            pltpu.VMEM((1, count), jnp.int32),
            pltpu.SemaphoreType.DMA((4,)),
        ],
        compiler_params=compiler_params(),
        name="build_requests",
    )(
        in_hbm(owner_map.reshape(-1, LANES)), in_hbm(head_ids.reshape(1, -1)),
        in_hbm(tail_ids.reshape(1, -1)), in_hbm(neg_ids.reshape(1, -1)),
    )


def rows_kernel(pack, columns_ref, rows_hbm, rows_ref, sem):
    count = columns_ref.shape[1]
    fill = jnp.zeros((pack.wide - pack.width, LANES), jnp.float32)
    for block in range(count // LANES):
        at = slice(block * LANES, (block + 1) * LANES)
        tile = jnp.concatenate([columns_ref[:, at], fill], axis=0)
        for c in range(pack.groups):
            rows_ref[at, c, :] = tile[c * LANES : (c + 1) * LANES].T
    rows_ref[count:] = jnp.zeros((SUBLANES, pack.groups, LANES), jnp.float32)
    copy = pltpu.make_async_copy(rows_ref, rows_hbm, sem)
    copy.start()
    copy.wait()


def to_rows(pack, columns):
    count = columns.shape[1]
    return pl.pallas_call(
        functools.partial(rows_kernel, pack),
        out_shape=pltpu.HBM((count + SUBLANES, pack.groups, LANES), jnp.float32),
        in_specs=[vmem()],
        out_specs=hbm(),
        scratch_shapes=[
            pltpu.VMEM((count + SUBLANES, pack.groups, LANES), jnp.float32),
            pltpu.SemaphoreType.DMA(()),
        ],
        compiler_params=compiler_params(),
        name="table_rows",
    )(columns)


def sends(pack, out_ref, out_hbm, sems):
    count = sems.shape[0]
    each = pack.owners // count
    copies = []
    for index in range(count):
        rows = pl.ds(index * each * pack.stride, each * pack.stride)
        copies.append(pltpu.make_async_copy(out_ref.at[rows, :], out_hbm.at[rows, :], sems.at[index]))
    return copies, each


def serve_kernel(pack, asked_ref, table_hbm, out_hbm, table_ref, out_ref, sems, table_sem):
    load = pltpu.make_async_copy(table_hbm, table_ref, table_sem)
    load.start()
    load.wait()
    lane = lax.broadcasted_iota(jnp.int32, (pack.groups, LANES), 1) // pack.rest
    copies, each = sends(pack, out_ref, out_hbm, sems)

    def body(owner):
        base = pl.multiple_of(owner * pack.stride, SUBLANES)
        for group in range(pack.shared):
            first = group * SUBLANES
            values = [table_ref[asked_ref[owner, 0, first + j]] for j in range(SUBLANES)]
            shared = values[0]
            for j in range(1, SUBLANES):
                moved = pltpu.roll(values[j], j * pack.rest, axis=1)
                shared = jnp.where(lane == j, moved, shared)
            for j in range(SUBLANES):
                out_ref[pl.ds(base + (first + j) * pack.full, pack.full), :] = values[j][
                    : pack.full
                ]
            out_ref[pl.ds(base + pack.rests_at + group, 1), :] = shared[pack.full :]

    for index, copy in enumerate(copies):
        loop(each, lambda owner: body(index * each + owner))
        copy.start()
    for copy in copies:
        copy.wait()


def serve(pack, asked, table_rows):
    return pl.pallas_call(
        functools.partial(serve_kernel, pack),
        out_shape=pltpu.HBM((pack.rows, LANES), jnp.float32),
        in_specs=[smem(), hbm()],
        out_specs=hbm(),
        scratch_shapes=[
            pltpu.VMEM(table_rows.shape, jnp.float32),
            pltpu.VMEM((pack.rows, LANES), jnp.float32),
            pltpu.SemaphoreType.DMA((8,)),
            pltpu.SemaphoreType.DMA(()),
        ],
        compiler_params=compiler_params(),
        name="serve_rows",
    )(asked, in_hbm(table_rows))


def copy_rows(pack, first_request, address_ref, slot_ref, packed_ref, rests_ref, rows_ref):
    def body(group):
        first = group * SUBLANES
        values = []
        for j in range(SUBLANES):
            request = first_request + first + j
            values.append(
                (
                    packed_ref[pl.ds(address_ref[0, request], pack.full), :],
                    rests_ref[pl.ds(slot_ref[0, request], 1), :],
                )
            )
        for j, (groups, rest) in enumerate(values):
            rows_ref[first + j, : pack.full, :] = groups
            rows_ref[first + j, pack.full :, :] = rest

    loop(rows_ref.shape[0] // SUBLANES, body)


def heads_kernel(
    pack, address_ref, slot_ref, packed_ref, relation_ref,
    query_ref, shared_ref, rests_ref, rows_ref,
):
    expand_rests(pack, packed_ref, shared_ref, rests_ref)
    copy_rows(pack, 0, address_ref, slot_ref, packed_ref, rests_ref, rows_ref)
    query_ref[...] = row_columns(pack, rows_ref[...]) + relation_ref[...]


def unpack_heads(pack, edges, address, slot, packed, relation_rows):
    return pl.pallas_call(
        functools.partial(heads_kernel, pack),
        out_shape=jax.ShapeDtypeStruct((pack.width, edges), jnp.float32),
        in_specs=[smem(), smem(), vmem(), vmem()],
        out_specs=vmem(),
        scratch_shapes=rests_scratch(pack)
        + [pltpu.VMEM((edges, pack.groups, LANES), jnp.float32)],
        compiler_params=compiler_params(),
        cost_estimate=pl.CostEstimate(flops=10**7, bytes_accessed=3 * 10**6, transcendentals=0),
        name="unpack_heads",
    )(address, slot, packed, relation_rows)


def rest_kernel(
    pack, edges, address_ref, slot_ref, packed_ref, query_ref,
    positive_ref, negative_ref, shared_ref, rests_ref, rows_ref,
):
    expand_rests(pack, packed_ref, shared_ref, rests_ref)
    copy_rows(pack, edges, address_ref, slot_ref, packed_ref, rests_ref, rows_ref)
    for c in range(pack.groups):
        negative_ref[:, c * LANES : (c + 1) * LANES] = rows_ref[edges:, c, :]
    residue = query_ref[...] - row_columns(pack, rows_ref[:edges])
    distance = jnp.sqrt(jnp.sum(residue * residue, axis=0, keepdims=True) + EPSILON)
    positive_ref[...] = jax.nn.sigmoid(distance - MARGIN) / distance * residue


def unpack_rest(pack, negatives, address, slot, packed, queries):
    edges = queries.shape[1]
    shape = jax.ShapeDtypeStruct
    return pl.pallas_call(
        functools.partial(rest_kernel, pack, edges),
        out_shape=(
            shape((pack.width, edges), jnp.float32),
            shape((negatives, pack.wide), jnp.float32),
        ),
        in_specs=[smem(), smem(), vmem(), vmem()],
        out_specs=(vmem(), vmem()),
        scratch_shapes=rests_scratch(pack)
        + [pltpu.VMEM((edges + negatives, pack.groups, LANES), jnp.float32)],
        compiler_params=compiler_params(),
        cost_estimate=pl.CostEstimate(flops=10**7, bytes_accessed=9 * 10**6, transcendentals=0),
        name="unpack_rest",
    )(address, slot, packed, queries)


def gather_queries(pack, query_refs):
    queries = jnp.concatenate([ref[...] for ref in query_refs], axis=1)
    fill = jnp.zeros((pack.wide - pack.width, queries.shape[1]), jnp.float32)
    return jnp.concatenate([queries, fill], axis=0)


def negatives_kernel(pack, blocks, weight, *refs):
    negative_ref = refs[0]
    query_refs = refs[1 : 1 + blocks]
    coefficient_ref, *part_refs = refs[1 + blocks :]
    negatives = negative_ref[...]
    queries = gather_queries(pack, query_refs)
    query_sq = jnp.sum(queries * queries, axis=0, keepdims=True)
    block_sq = jnp.sum(negatives * negatives, axis=1, keepdims=True)
    inner = jnp.dot(negatives, queries, precision=HIGHEST, preferred_element_type=jnp.float32)
    distance = jnp.sqrt(query_sq + block_sq - 2.0 * inner + EPSILON)
    coefficient = -1.0 / ((1.0 + jnp.exp(distance - MARGIN)) * (weight * distance))
    coefficient_ref[...] = coefficient
    part = queries * jnp.sum(coefficient, axis=0, keepdims=True) - dot_halves(
        split(negatives.T), split(coefficient), ((1,), (0,))
    )
    width = query_refs[0].shape[1]
    for index, ref in enumerate(part_refs):
        ref[...] = part[: pack.width, index * width : (index + 1) * width]


def negative_terms(pack, weight, negatives, queries):
    shape = jax.ShapeDtypeStruct
    count = sum(q.shape[1] for q in queries)
    rows = negatives.shape[0]
    return pl.pallas_call(
        functools.partial(negatives_kernel, pack, len(queries), weight),
        out_shape=(shape((rows, count), jnp.float32),)
        + tuple(shape(q.shape, jnp.float32) for q in queries),
        in_specs=[vmem()] * (1 + len(queries)),
        out_specs=(vmem(),) * (1 + len(queries)),
        compiler_params=compiler_params(),
        cost_estimate=pl.CostEstimate(
            flops=18 * rows * count * pack.wide, bytes_accessed=4 * 10**6, transcendentals=0
        ),
        name="negative_terms",
    )(negatives, *queries)


def store_rows(pack, first_request, address_ref, slot_ref, rows_ref, out_ref, rests_ref):
    def body(group):
        first = group * SUBLANES
        values = [rows_ref[first + j] for j in range(SUBLANES)]
        for j, value in enumerate(values):
            request = first_request + first + j
            out_ref[pl.ds(address_ref[0, request], pack.full), :] = value[: pack.full]
            rests_ref[pl.ds(slot_ref[0, request], 1), :] = value[pack.full :]

    loop(rows_ref.shape[0] // SUBLANES, body)


def store_columns(pack, columns, rows_ref):
    fill = jnp.zeros((pack.wide - pack.width, columns.shape[1]), jnp.float32)
    columns = jnp.concatenate([columns, fill], axis=0)
    for c in range(pack.groups):
        rows_ref[:, c, :] = columns[c * LANES : (c + 1) * LANES].T


def block_kernel(pack, blocks, coefficients, address_ref, slot_ref, *refs):
    positive_ref, negative_ref = refs[:2]
    query_refs = refs[2 : 2 + blocks]
    coefficient_refs = refs[2 + blocks : 2 + blocks + coefficients]
    out_ref, rests_ref, rows_ref = refs[2 + blocks + coefficients :]
    edges = positive_ref.shape[1]
    out_ref[...] = jnp.zeros_like(out_ref)
    rests_ref[...] = jnp.zeros_like(rests_ref)
    store_columns(pack, -positive_ref[...], rows_ref.at[:edges])
    coefficient = jnp.concatenate([ref[...] for ref in coefficient_refs], axis=1)
    block_grad = negative_ref[...] * jnp.sum(coefficient, axis=1, keepdims=True) - dot_halves(
        split(coefficient), split(gather_queries(pack, query_refs)), ((1,), (1,))
    )
    for c in range(pack.groups):
        rows_ref[edges:, c, :] = block_grad[:, c * LANES : (c + 1) * LANES]
    store_rows(pack, edges, address_ref, slot_ref, rows_ref, out_ref, rests_ref)


def block_gradients(pack, address, slot, positive, negatives, queries, coefficients):
    shape = jax.ShapeDtypeStruct
    rows = positive.shape[1] + negatives.shape[0]
    flops = 6 * sum(c.size for c in coefficients) * pack.wide
    return pl.pallas_call(
        functools.partial(block_kernel, pack, len(queries), len(coefficients)),
        out_shape=(
            shape((pack.rows, LANES), jnp.float32),
            shape((pack.slots, LANES), jnp.float32),
        ),
        in_specs=[smem()] * 2 + [vmem()] * (2 + len(queries) + len(coefficients)),
        out_specs=(vmem(), vmem()),
        scratch_shapes=[pltpu.VMEM((rows, pack.groups, LANES), jnp.float32)],
        compiler_params=compiler_params(),
        cost_estimate=pl.CostEstimate(
            flops=flops, bytes_accessed=10**7, transcendentals=0
        ),
        name="block_gradients",
    )(address, slot, positive, negatives, *queries, *coefficients)


def finish_kernel(pack, parts, address_ref, slot_ref, *refs):
    partial_ref, partial_rests_ref, positive_ref = refs[:3]
    part_refs = refs[3 : 3 + parts]
    out_hbm, out_ref, rests_ref, rows_ref, sems = refs[3 + parts :]
    copies, each = sends(pack, out_ref, out_hbm, sems)
    out_ref[...] = partial_ref[...]
    rests_ref[...] = partial_rests_ref[...]
    total = positive_ref[...]
    for ref in part_refs:
        total = total + ref[...]
    store_columns(pack, total, rows_ref)
    store_rows(pack, 0, address_ref, slot_ref, rows_ref, out_ref, rests_ref)
    count = each * pack.shared
    for index, copy in enumerate(copies):
        first = index * each * pack.capacity
        shared = rests_ref[pl.ds(first, count, stride=SUBLANES), :]
        for j in range(1, SUBLANES):
            block = rests_ref[pl.ds(first + j, count, stride=SUBLANES), :]
            shared = shared + pltpu.roll(block, j * pack.rest, axis=1)
        for owner in range(each):
            start = (index * each + owner) * pack.stride + pack.rests_at
            out_ref[pl.ds(start, pack.shared), :] = shared[
                owner * pack.shared : (owner + 1) * pack.shared
            ]
        copy.start()
    for copy in copies:
        copy.wait()


def finish_gradients(pack, address, slot, partial, partial_rests, positive, parts):
    edges = positive.shape[1]
    return pl.pallas_call(
        functools.partial(finish_kernel, pack, len(parts)),
        out_shape=pltpu.HBM((pack.rows, LANES), jnp.float32),
        in_specs=[smem()] * 2 + [vmem()] * (3 + len(parts)),
        out_specs=hbm(),
        scratch_shapes=[
            pltpu.VMEM((pack.rows, LANES), jnp.float32),
            pltpu.VMEM((pack.slots, LANES), jnp.float32),
            pltpu.VMEM((edges, pack.groups, LANES), jnp.float32),
            pltpu.SemaphoreType.DMA((8,)),
        ],
        compiler_params=compiler_params(),
        name="finish_gradients",
    )(address, slot, partial, partial_rests, positive, *parts)


def update_kernel(
    pack, columns, asked_ref, packed_ref, sum_ref, table_ref,
    new_table_hbm, new_sum_ref, shared_ref, rests_ref, rows_ref, halves_ref, out_ref, sems,
):
    expand_rests(pack, packed_ref, shared_ref, rests_ref)

    def body(owner):
        rows = pl.ds(pl.multiple_of(owner * pack.capacity, SUBLANES), pack.capacity)
        for c in range(pack.full):
            rows_ref[rows, c * LANES : (c + 1) * LANES] = packed_ref[
                pl.ds(owner * pack.stride + c, pack.capacity, stride=pack.full), :
            ]
        rows_ref[rows, pack.full * LANES :] = rests_ref[rows, :]

    loop(pack.owners, body)
    width = pack.width
    high, low = split(rows_ref[...].T)
    halves_ref[:width] = high[:width]
    halves_ref[width:] = low[:width]
    asked = asked_ref[...]
    row = lax.broadcasted_iota(jnp.int32, (columns, pack.slots), 0)
    copies = []
    for index in range(table_ref.shape[1] // columns):
        at = slice(index * columns, (index + 1) * columns)
        chosen = one_hot(row == asked - index * columns)
        both = lax.dot_general(
            halves_ref[...], chosen, (((1,), (1,)), ((), ())), preferred_element_type=jnp.float32
        )
        summed = both[:width] + both[width:]
        new_sum = sum_ref[:, at] + jnp.sum(summed * summed, axis=0, keepdims=True) / width
        new_sum_ref[:, at] = new_sum
        out_ref[:, at] = table_ref[:, at] - summed * (LEARNING_RATE / jnp.sqrt(new_sum))
        copies.append(
            pltpu.make_async_copy(out_ref.at[:, at], new_table_hbm.at[:, at], sems.at[index])
        )
        copies[-1].start()
    for copy in copies:
        copy.wait()


def update(pack, asked, packed, adagrad_sum, table_columns):
    width, rows = table_columns.shape
    columns = 256
    shape = jax.ShapeDtypeStruct
    return pl.pallas_call(
        functools.partial(update_kernel, pack, columns),
        out_shape=(pltpu.HBM((width, rows), jnp.float32), shape((1, rows), jnp.float32)),
        in_specs=[vmem()] * 4,
        out_specs=(hbm(), vmem()),
        scratch_shapes=rests_scratch(pack)
        + [
            pltpu.VMEM((pack.slots, pack.wide), jnp.float32),
            pltpu.VMEM((2 * width, pack.slots), jnp.bfloat16),
            pltpu.VMEM((width, rows), jnp.float32),
            pltpu.SemaphoreType.DMA((rows // columns,)),
        ],
        compiler_params=compiler_params(),
        name="update_table",
    )(asked, packed, adagrad_sum, table_columns)


def exchange(payload):
    return lax.all_to_all(payload, ("dp", "blk"), split_axis=0, concat_axis=0, tiled=True)


def to_sibling(value, blk_count):
    return lax.ppermute(value, "blk", [(i, i ^ 1) for i in range(blk_count)])


def to_chip(value, blk_count, hops):
    return lax.ppermute(
        value, "blk", [(i, (i + 2 * hops) % blk_count) for i in range(blk_count)]
    )


def on_device(
    entity_table, adagrad_sum, relations, owner_map, head_ids, rel_ids, tail_ids, neg_ids
):
    dp_count = lax.axis_size("dp")
    blk_count = lax.axis_size("blk")
    owner_count = dp_count * blk_count
    chip_count = blk_count // 2
    rows_here, width = entity_table.shape
    edge_count = head_ids.shape[0]
    neg_count = neg_ids.shape[0]
    request_count = 2 * edge_count + neg_count
    capacity = -(-2 * request_count // owner_count // SUBLANES) * SUBLANES
    pack = Packing(width, owner_count, capacity)
    requests, address, slot_of = build_requests(
        pack, rows_here, owner_map, head_ids, tail_ids, neg_ids
    )
    asked = exchange(requests)
    served = serve(pack, asked, to_rows(pack, entity_table.T))
    fetched = exchange(served.reshape(owner_count, pack.stride, LANES))
    fetched = fetched.reshape(pack.rows, LANES)
    queries = unpack_heads(pack, edge_count, address, slot_of, fetched, relations[rel_ids].T)
    weight = float(blk_count * neg_count)
    arriving = [to_chip(queries, blk_count, hops) for hops in range(1, chip_count)]
    nearby = [queries, to_sibling(queries, blk_count)]
    positive, negatives = unpack_rest(pack, neg_count, address, slot_of, fetched, queries)
    near, *near_parts = negative_terms(pack, weight, negatives, nearby)
    arriving, near, near_parts = lax.optimization_barrier((arriving, near, near_parts))
    distant = []
    for same in arriving:
        distant += [same, to_sibling(same, blk_count)]
    far, *far_parts = negative_terms(pack, weight, negatives, distant)
    group = nearby + distant
    totals = [near_parts[0], to_sibling(near_parts[1], blk_count)]
    for hops in range(1, chip_count):
        total = far_parts[2 * hops - 2] + to_sibling(far_parts[2 * hops - 1], blk_count)
        totals.append(to_chip(total, blk_count, chip_count - hops))
    partial, partial_rests = block_gradients(
        pack, address, slot_of, positive, negatives, group, (near, far)
    )
    outgoing = finish_gradients(
        pack, address, slot_of, partial, partial_rests, positive, totals
    )
    incoming = exchange(outgoing.reshape(owner_count, pack.stride, LANES))
    new_columns, new_sum = update(
        pack, asked.reshape(1, -1), incoming.reshape(pack.rows, LANES),
        adagrad_sum.reshape(1, -1), entity_table.T,
    )
    return (new_columns.T, new_sum.reshape(-1))


def solution(mesh):
    return jax.shard_map(
        on_device,
        mesh=mesh,
        in_specs=(
            P(("dp", "blk"), None),
            P(("dp", "blk")),
            P(),
            P(),
            P(("dp", "blk")),
            P(("dp", "blk")),
            P(("dp", "blk")),
            P(("dp", "blk")),
        ),
        out_specs=(P(("dp", "blk"), None), P(("dp", "blk"))),
        check_vma=False,
    )
```

```python
import functools

import jax
import jax.numpy as jnp
from jax import lax
from jax.experimental import pallas as pl
from jax.experimental.pallas import tpu as pltpu
from jax.sharding import PartitionSpec as P

MARGIN = 10.0
EPSILON = 1e-05
LEARNING_RATE = 0.1
LANES = 128
SUBLANES = 8
VMEM_BYTES = 24 * 1024 * 1024


class Packing:
    def __init__(self, width, owners, capacity):
        self.width = width
        self.owners = owners
        self.capacity = capacity
        self.full = width // LANES
        self.rest = width - self.full * LANES
        assert 0 < self.rest <= LANES // SUBLANES and capacity % SUBLANES == 0
        self.shared = capacity // SUBLANES
        self.groups = self.full + 1
        self.wide = self.groups * LANES
        self.rests_at = self.full * capacity
        self.stride = -(-(self.rests_at + self.shared) // SUBLANES) * SUBLANES
        self.slots = owners * capacity
        self.rows = owners * self.stride


def compiler_params():
    return pltpu.CompilerParams(vmem_limit_bytes=VMEM_BYTES)


def vmem():
    return pl.BlockSpec(memory_space=pltpu.VMEM)


def smem():
    return pl.BlockSpec(memory_space=pltpu.SMEM)


def hbm():
    return pl.BlockSpec(memory_space=pltpu.HBM)


def in_hbm(value):
    return pltpu.with_memory_space_constraint(value, pltpu.HBM)


def split(value):
    high = value.astype(jnp.bfloat16)
    low = (value - high.astype(jnp.float32)).astype(jnp.bfloat16)
    return high, low


def dot_halves(left, right, contract):
    numbers = (contract, ((), ()))

    def dot(a, b):
        return lax.dot_general(a, b, numbers, preferred_element_type=jnp.float32)

    return dot(left[0], right[0]) + (dot(left[0], right[1]) + dot(left[1], right[0]))


def loop(count, body):
    def step(index, carry):
        body(index)
        return carry

    lax.fori_loop(0, count, step, 0)


def expand_rests(pack, packed_ref, shared_ref, rests_ref, first_owner=0, owners=None):
    owners = pack.owners if owners is None else owners
    for owner in range(first_owner, first_owner + owners):
        shared_ref[owner * pack.shared : (owner + 1) * pack.shared, :] = packed_ref[
            pl.ds(owner * pack.stride + pack.rests_at, pack.shared), :
        ]
    first = first_owner * pack.shared
    shared = shared_ref[first : first + owners * pack.shared, :]
    lane = lax.broadcasted_iota(jnp.int32, shared.shape, 1)
    for j in range(SUBLANES):
        moved = shared if j == 0 else pltpu.roll(shared, LANES - j * pack.rest, axis=1)
        rows = pl.ds(first * SUBLANES + j, shared.shape[0], stride=SUBLANES)
        rests_ref[rows, :] = jnp.where(lane < pack.rest, moved, 0.0)


def rests_scratch(pack):
    return [
        pltpu.VMEM((pack.owners * pack.shared, LANES), jnp.float32),
        pltpu.VMEM((pack.slots, LANES), jnp.float32),
    ]


def row_columns(pack, rows):
    parts = [rows[:, c, :].T for c in range(pack.groups)]
    return jnp.concatenate(parts, axis=0)[: pack.width]


def one_hot(mask):
    return mask.astype(jnp.float32).astype(jnp.bfloat16)


def request_kernel(
    pack, rows_here, map_hbm, head_hbm, tail_hbm, negative_hbm,
    request_ref, address_ref, slot_ref, map_ref, ids_ref, sems,
):
    copies = [pltpu.make_async_copy(map_hbm, map_ref, sems.at[0])]
    first = 0
    for index, source in enumerate((head_hbm, tail_hbm, negative_hbm)):
        target = ids_ref.at[:, pl.ds(first, source.shape[1])]
        copies.append(pltpu.make_async_copy(source, target, sems.at[index + 1]))
        first += source.shape[1]
    for copy in copies:
        copy.start()
    for copy in copies:
        copy.wait()
    ids = ids_ref[...]
    count = ids.shape[1]
    lines = map_ref.shape[0]

    def iota(rows, axis):
        return lax.broadcasted_iota(jnp.int32, (rows, count), axis)

    line_chosen = one_hot(iota(lines, 0) == ids // LANES)
    table = map_ref[...].T
    digits = [(table >> shift) & 255 for shift in range(0, 24, 8)]
    stacked = jnp.concatenate(digits, axis=0).astype(jnp.float32).astype(jnp.bfloat16)
    found = jnp.dot(stacked, line_chosen, preferred_element_type=jnp.float32)
    found = found[:LANES] + 256.0 * found[LANES : 2 * LANES] + 65536.0 * found[2 * LANES :]
    found = jnp.where(iota(LANES, 0) == ids % LANES, found, 0.0)
    position = jnp.sum(found, axis=0, keepdims=True).astype(jnp.int32)
    owner = position // rows_here
    row = position % rows_here
    to_owner = iota(pack.owners, 0) == owner
    earlier = one_hot(iota(count, 0) < iota(count, 1))
    before = jnp.dot(one_hot(to_owner), earlier, preferred_element_type=jnp.float32)
    rank = jnp.sum(jnp.where(to_owner, before, 0.0), axis=0, keepdims=True).astype(jnp.int32)
    slot_ref[...] = owner * pack.capacity + rank
    address_ref[...] = owner * pack.stride + rank * pack.full
    at_rank = one_hot(iota(pack.capacity, 0) == rank)
    absent = row - rows_here

    def place(values):
        chosen = jnp.where(to_owner, values.astype(jnp.float32), 0.0).astype(jnp.bfloat16)
        return lax.dot_general(
            chosen, at_rank, (((1,), (1,)), ((), ())), preferred_element_type=jnp.float32
        )

    high = -((-absent) // 256)
    low = absent - high * 256
    request_ref[:, 0, :] = (place(high) * 256.0 + place(low)).astype(jnp.int32) + rows_here


def build_requests(pack, rows_here, owner_map, head_ids, tail_ids, neg_ids):
    count = head_ids.shape[0] + tail_ids.shape[0] + neg_ids.shape[0]
    shape = jax.ShapeDtypeStruct
    return pl.pallas_call(
        functools.partial(request_kernel, pack, rows_here),
        out_shape=(
            shape((pack.owners, 1, pack.capacity), jnp.int32),
            shape((1, count), jnp.int32),
            shape((1, count), jnp.int32),
        ),
        in_specs=[hbm()] * 4,
        out_specs=(vmem(),) * 3,
        scratch_shapes=[
            pltpu.VMEM((owner_map.shape[0] // LANES, LANES), jnp.int32),
            pltpu.VMEM((1, count), jnp.int32),
            pltpu.SemaphoreType.DMA((4,)),
        ],
        compiler_params=compiler_params(),
        name="build_requests",
    )(
        in_hbm(owner_map.reshape(-1, LANES)), in_hbm(head_ids.reshape(1, -1)),
        in_hbm(tail_ids.reshape(1, -1)), in_hbm(neg_ids.reshape(1, -1)),
    )


def rows_kernel(pack, columns_ref, rows_hbm, rows_ref, sem):
    count = columns_ref.shape[1]
    fill = jnp.zeros((pack.wide - pack.width, LANES), jnp.float32)
    for block in range(count // LANES):
        at = slice(block * LANES, (block + 1) * LANES)
        tile = jnp.concatenate([columns_ref[:, at], fill], axis=0)
        for c in range(pack.groups):
            rows_ref[at, c, :] = tile[c * LANES : (c + 1) * LANES].T
    rows_ref[count:] = jnp.zeros((SUBLANES, pack.groups, LANES), jnp.float32)
    copy = pltpu.make_async_copy(rows_ref, rows_hbm, sem)
    copy.start()
    copy.wait()


def to_rows(pack, columns):
    count = columns.shape[1]
    return pl.pallas_call(
        functools.partial(rows_kernel, pack),
        out_shape=pltpu.HBM((count + SUBLANES, pack.groups, LANES), jnp.float32),
        in_specs=[vmem()],
        out_specs=hbm(),
        scratch_shapes=[
            pltpu.VMEM((count + SUBLANES, pack.groups, LANES), jnp.float32),
            pltpu.SemaphoreType.DMA(()),
        ],
        compiler_params=compiler_params(),
        name="table_rows",
    )(columns)


def sends(pack, out_ref, out_hbm, sems):
    count = sems.shape[0]
    each = pack.owners // count
    copies = []
    for index in range(count):
        rows = pl.ds(index * each * pack.stride, each * pack.stride)
        copies.append(pltpu.make_async_copy(out_ref.at[rows, :], out_hbm.at[rows, :], sems.at[index]))
    return copies, each


def share_rests(pack, rests_ref, out_ref, first_owner, owners):
    count = owners * pack.shared
    first = first_owner * pack.capacity
    shared = rests_ref[pl.ds(first, count, stride=SUBLANES), :]
    place = lax.broadcasted_iota(jnp.int32, shared.shape, 1) // pack.rest
    for j in range(1, SUBLANES):
        block = rests_ref[pl.ds(first + j, count, stride=SUBLANES), :]
        shared = jnp.where(place == j, pltpu.roll(block, j * pack.rest, axis=1), shared)
    for owner in range(owners):
        start = (first_owner + owner) * pack.stride + pack.rests_at
        out_ref[pl.ds(start, pack.shared), :] = shared[
            owner * pack.shared : (owner + 1) * pack.shared
        ]


def serve_kernel(
    pack, asked_ref, table_hbm, out_hbm, table_ref, out_ref, rests_ref, sems, table_sems
):
    pieces = table_sems.shape[0]
    rows = table_ref.shape[0] // pieces
    loads = []
    for index in range(pieces):
        at = pl.ds(index * rows, rows)
        loads.append(
            pltpu.make_async_copy(table_hbm.at[at], table_ref.at[at], table_sems.at[index])
        )
        loads[-1].start()
    for load in loads:
        load.wait()
    copies, each = sends(pack, out_ref, out_hbm, sems)

    def body(owner):
        base = pl.multiple_of(owner * pack.stride, SUBLANES)
        slots = pl.multiple_of(owner * pack.capacity, SUBLANES)
        for first in range(0, pack.capacity, SUBLANES):
            values = [table_ref[asked_ref[owner, 0, first + j]] for j in range(SUBLANES)]
            rests_ref[pl.ds(slots + first, SUBLANES), :] = jnp.concatenate(
                [value[pack.full :] for value in values], axis=0
            )
            for j in range(SUBLANES):
                out_ref[pl.ds(base + (first + j) * pack.full, pack.full), :] = values[j][
                    : pack.full
                ]

    for index, copy in enumerate(copies):
        loop(each, lambda owner: body(index * each + owner))
        share_rests(pack, rests_ref, out_ref, index * each, each)
        copy.start()
    for copy in copies:
        copy.wait()


def serve(pack, asked, table_rows):
    return pl.pallas_call(
        functools.partial(serve_kernel, pack),
        out_shape=pltpu.HBM((pack.rows, LANES), jnp.float32),
        in_specs=[smem(), hbm()],
        out_specs=hbm(),
        scratch_shapes=[
            pltpu.VMEM(table_rows.shape, jnp.float32),
            pltpu.VMEM((pack.rows, LANES), jnp.float32),
            pltpu.VMEM((pack.slots, LANES), jnp.float32),
            pltpu.SemaphoreType.DMA((8,)),
            pltpu.SemaphoreType.DMA((8,)),
        ],
        compiler_params=compiler_params(),
        name="serve_rows",
    )(asked, in_hbm(table_rows))


def copy_rows(pack, first_request, address_ref, slot_ref, packed_ref, rests_ref, rows_ref):
    def body(group):
        first = group * SUBLANES
        values = []
        for j in range(SUBLANES):
            request = first_request + first + j
            values.append(
                (
                    packed_ref[pl.ds(address_ref[0, request], pack.full), :],
                    rests_ref[pl.ds(slot_ref[0, request], 1), :],
                )
            )
        for j, (groups, rest) in enumerate(values):
            rows_ref[first + j, : pack.full, :] = groups
            rows_ref[first + j, pack.full :, :] = rest

    loop(rows_ref.shape[0] // SUBLANES, body)


def heads_kernel(
    pack, address_ref, slot_ref, packed_ref, relation_ref,
    query_ref, shared_ref, rests_ref, rows_ref,
):
    expand_rests(pack, packed_ref, shared_ref, rests_ref)
    copy_rows(pack, 0, address_ref, slot_ref, packed_ref, rests_ref, rows_ref)
    query_ref[...] = row_columns(pack, rows_ref[...]) + relation_ref[...]


def unpack_heads(pack, edges, address, slot, packed, relation_rows):
    return pl.pallas_call(
        functools.partial(heads_kernel, pack),
        out_shape=jax.ShapeDtypeStruct((pack.width, edges), jnp.float32),
        in_specs=[smem(), smem(), vmem(), vmem()],
        out_specs=vmem(),
        scratch_shapes=rests_scratch(pack)
        + [pltpu.VMEM((edges, pack.groups, LANES), jnp.float32)],
        compiler_params=compiler_params(),
        cost_estimate=pl.CostEstimate(flops=10**7, bytes_accessed=3 * 10**6, transcendentals=0),
        name="unpack_heads",
    )(address, slot, packed, relation_rows)


def rest_kernel(
    pack, edges, address_ref, slot_ref, packed_ref, query_ref,
    positive_ref, negative_ref, high_ref, low_ref, high_columns_ref, low_columns_ref, square_ref,
    shared_ref, rests_ref, rows_ref,
):
    expand_rests(pack, packed_ref, shared_ref, rests_ref)
    copy_rows(pack, edges, address_ref, slot_ref, packed_ref, rests_ref, rows_ref)
    for c in range(pack.groups):
        negative_ref[:, c * LANES : (c + 1) * LANES] = rows_ref[edges:, c, :]
    negatives = negative_ref[...]
    high_ref[...], low_ref[...] = split(negatives)
    high_columns_ref[...], low_columns_ref[...] = split(negatives.T[: pack.width])
    square_ref[...] = jnp.sum(negatives * negatives, axis=1, keepdims=True)
    residue = query_ref[...] - row_columns(pack, rows_ref[:edges])
    distance = jnp.sqrt(jnp.sum(residue * residue, axis=0, keepdims=True) + EPSILON)
    positive_ref[...] = jax.nn.sigmoid(distance - MARGIN) / distance * residue


def unpack_rest(pack, negatives, address, slot, packed, queries):
    edges = queries.shape[1]
    shape = jax.ShapeDtypeStruct
    return pl.pallas_call(
        functools.partial(rest_kernel, pack, edges),
        out_shape=(
            shape((pack.width, edges), jnp.float32),
            shape((negatives, pack.wide), jnp.float32),
            shape((negatives, pack.wide), jnp.bfloat16),
            shape((negatives, pack.wide), jnp.bfloat16),
            shape((pack.width, negatives), jnp.bfloat16),
            shape((pack.width, negatives), jnp.bfloat16),
            shape((negatives, 1), jnp.float32),
        ),
        in_specs=[smem(), smem(), vmem(), vmem()],
        out_specs=(vmem(),) * 7,
        scratch_shapes=rests_scratch(pack)
        + [pltpu.VMEM((edges + negatives, pack.groups, LANES), jnp.float32)],
        compiler_params=compiler_params(),
        cost_estimate=pl.CostEstimate(flops=10**7, bytes_accessed=9 * 10**6, transcendentals=0),
        name="unpack_rest",
    )(address, slot, packed, queries)


def gather_queries(pack, query_refs):
    queries = jnp.concatenate([ref[...] for ref in query_refs], axis=1)
    fill = jnp.zeros((pack.wide - pack.width, queries.shape[1]), jnp.float32)
    return jnp.concatenate([queries, fill], axis=0)


def negatives_kernel(pack, blocks, weight, *refs):
    half_refs = refs[:2]
    column_refs = refs[2:4]
    square_ref = refs[4]
    query_refs = refs[5 : 5 + blocks]
    coefficient_ref, *part_refs = refs[5 + blocks :]
    queries = gather_queries(pack, query_refs)
    query_sq = jnp.sum(queries * queries, axis=0, keepdims=True)
    inner = dot_halves([ref[...] for ref in half_refs], split(queries), ((1,), (0,)))
    squared = jnp.maximum(query_sq + square_ref[...] - 2.0 * inner + EPSILON, EPSILON)
    distance = jnp.sqrt(squared)
    coefficient = -1.0 / ((1.0 + jnp.exp(distance - MARGIN)) * (weight * distance))
    coefficient_ref[...] = coefficient
    part = queries[: pack.width] * jnp.sum(coefficient, axis=0, keepdims=True) - dot_halves(
        [ref[...] for ref in column_refs], split(coefficient), ((1,), (0,))
    )
    width = query_refs[0].shape[1]
    for index, ref in enumerate(part_refs):
        ref[...] = part[:, index * width : (index + 1) * width]


def negative_terms(pack, weight, negative_parts, queries):
    shape = jax.ShapeDtypeStruct
    count = sum(q.shape[1] for q in queries)
    rows = negative_parts[0].shape[0]
    return pl.pallas_call(
        functools.partial(negatives_kernel, pack, len(queries), weight),
        out_shape=(shape((rows, count), jnp.float32),)
        + tuple(shape(q.shape, jnp.float32) for q in queries),
        in_specs=[vmem()] * (len(negative_parts) + len(queries)),
        out_specs=(vmem(),) * (1 + len(queries)),
        compiler_params=compiler_params(),
        cost_estimate=pl.CostEstimate(
            flops=12 * rows * count * pack.wide, bytes_accessed=4 * 10**6, transcendentals=0
        ),
        name="negative_terms",
    )(*negative_parts, *queries)


def store_rows(pack, first_request, address_ref, slot_ref, rows_ref, out_ref, rests_ref):
    def body(group):
        first = group * SUBLANES
        values = [rows_ref[first + j] for j in range(SUBLANES)]
        for j, value in enumerate(values):
            request = first_request + first + j
            out_ref[pl.ds(address_ref[0, request], pack.full), :] = value[: pack.full]
            rests_ref[pl.ds(slot_ref[0, request], 1), :] = value[pack.full :]

    loop(rows_ref.shape[0] // SUBLANES, body)


def store_columns(pack, columns, rows_ref):
    fill = jnp.zeros((pack.wide - pack.width, columns.shape[1]), jnp.float32)
    columns = jnp.concatenate([columns, fill], axis=0)
    for c in range(pack.groups):
        rows_ref[:, c, :] = columns[c * LANES : (c + 1) * LANES].T


def block_kernel(pack, blocks, coefficients, address_ref, slot_ref, *refs):
    positive_ref, negative_ref = refs[:2]
    query_refs = refs[2 : 2 + blocks]
    coefficient_refs = refs[2 + blocks : 2 + blocks + coefficients]
    out_ref, rests_ref, rows_ref = refs[2 + blocks + coefficients :]
    edges = positive_ref.shape[1]
    out_ref[...] = jnp.zeros_like(out_ref)
    rests_ref[...] = jnp.zeros_like(rests_ref)
    store_columns(pack, -positive_ref[...], rows_ref.at[:edges])
    coefficient = jnp.concatenate([ref[...] for ref in coefficient_refs], axis=1)
    block_grad = negative_ref[...] * jnp.sum(coefficient, axis=1, keepdims=True) - dot_halves(
        split(coefficient), split(gather_queries(pack, query_refs)), ((1,), (1,))
    )
    for c in range(pack.groups):
        rows_ref[edges:, c, :] = block_grad[:, c * LANES : (c + 1) * LANES]
    store_rows(pack, edges, address_ref, slot_ref, rows_ref, out_ref, rests_ref)


def block_gradients(pack, address, slot, positive, negatives, queries, coefficients):
    shape = jax.ShapeDtypeStruct
    rows = positive.shape[1] + negatives.shape[0]
    flops = 6 * sum(c.size for c in coefficients) * pack.wide
    return pl.pallas_call(
        functools.partial(block_kernel, pack, len(queries), len(coefficients)),
        out_shape=(
            shape((pack.rows, LANES), jnp.float32),
            shape((pack.slots, LANES), jnp.float32),
        ),
        in_specs=[smem()] * 2 + [vmem()] * (2 + len(queries) + len(coefficients)),
        out_specs=(vmem(), vmem()),
        scratch_shapes=[pltpu.VMEM((rows, pack.groups, LANES), jnp.float32)],
        compiler_params=compiler_params(),
        cost_estimate=pl.CostEstimate(
            flops=flops, bytes_accessed=10**7, transcendentals=0
        ),
        name="block_gradients",
    )(address, slot, positive, negatives, *queries, *coefficients)


def finish_kernel(pack, parts, address_ref, slot_ref, *refs):
    positive_ref = refs[2]
    part_refs = refs[3 : 3 + parts]
    out_hbm, out_ref, rests_ref, rows_ref, sems = refs[3 + parts :]
    copies, each = sends(pack, out_ref, out_hbm, sems)
    total = positive_ref[...]
    for ref in part_refs:
        total = total + ref[...]
    store_columns(pack, total, rows_ref)
    store_rows(pack, 0, address_ref, slot_ref, rows_ref, out_ref, rests_ref)
    for index, copy in enumerate(copies):
        share_rests(pack, rests_ref, out_ref, index * each, each)
        copy.start()
    for copy in copies:
        copy.wait()


def finish_gradients(pack, address, slot, partial, partial_rests, positive, parts):
    edges = positive.shape[1]
    shape = jax.ShapeDtypeStruct
    return pl.pallas_call(
        functools.partial(finish_kernel, pack, len(parts)),
        out_shape=(
            pltpu.HBM((pack.rows, LANES), jnp.float32),
            shape(partial.shape, jnp.float32),
            shape(partial_rests.shape, jnp.float32),
        ),
        in_specs=[smem()] * 2 + [vmem()] * (3 + len(parts)),
        out_specs=(hbm(), vmem(), vmem()),
        input_output_aliases={2: 1, 3: 2},
        scratch_shapes=[
            pltpu.VMEM((edges, pack.groups, LANES), jnp.float32),
            pltpu.SemaphoreType.DMA((8,)),
        ],
        compiler_params=compiler_params(),
        name="finish_gradients",
    )(address, slot, partial, partial_rests, positive, *parts)[0]


def update_kernel(
    pack, columns, asked_ref, packed_hbm, sum_ref, table_ref, new_table_hbm, new_sum_ref,
    packed_ref, shared_ref, rests_ref, rows_ref, halves_ref, out_ref, sems, packed_sems,
):
    pieces = packed_sems.shape[0]
    owners = pack.owners // pieces
    loads = []
    for index in range(pieces):
        at = pl.ds(index * owners * pack.stride, owners * pack.stride)
        loads.append(
            pltpu.make_async_copy(packed_hbm.at[at, :], packed_ref.at[at, :], packed_sems.at[index])
        )
        loads[-1].start()
    width = pack.width
    for index, load in enumerate(loads):
        load.wait()
        expand_rests(pack, packed_ref, shared_ref, rests_ref, index * owners, owners)
        for owner in range(index * owners, (index + 1) * owners):
            rows = slice(owner * pack.capacity, (owner + 1) * pack.capacity)
            for c in range(pack.full):
                rows_ref[rows, c * LANES : (c + 1) * LANES] = packed_ref[
                    pl.ds(owner * pack.stride + c, pack.capacity, stride=pack.full), :
                ]
            rows_ref[rows, pack.full * LANES :] = rests_ref[rows, :]
        slots = slice(index * owners * pack.capacity, (index + 1) * owners * pack.capacity)
        high, low = split(rows_ref[slots, :].T)
        halves_ref[:width, slots] = high[:width]
        halves_ref[width:, slots] = low[:width]
    asked = asked_ref[...]
    row = lax.broadcasted_iota(jnp.int32, (columns, pack.slots), 0)
    copies = []
    for index in range(table_ref.shape[1] // columns):
        at = slice(index * columns, (index + 1) * columns)
        chosen = one_hot(row == asked - index * columns)
        both = lax.dot_general(
            halves_ref[...], chosen, (((1,), (1,)), ((), ())), preferred_element_type=jnp.float32
        )
        summed = both[:width] + both[width:]
        new_sum = sum_ref[:, at] + jnp.sum(summed * summed, axis=0, keepdims=True) / width
        new_sum_ref[:, at] = new_sum
        out_ref[:, at] = table_ref[:, at] - summed * (LEARNING_RATE / jnp.sqrt(new_sum))
        copies.append(
            pltpu.make_async_copy(out_ref.at[:, at], new_table_hbm.at[:, at], sems.at[index])
        )
        copies[-1].start()
    for copy in copies:
        copy.wait()


def update(pack, asked, packed, adagrad_sum, table_columns):
    width, rows = table_columns.shape
    columns = 256
    shape = jax.ShapeDtypeStruct
    return pl.pallas_call(
        functools.partial(update_kernel, pack, columns),
        out_shape=(pltpu.HBM((width, rows), jnp.float32), shape((1, rows), jnp.float32)),
        in_specs=[vmem(), hbm(), vmem(), vmem()],
        out_specs=(hbm(), vmem()),
        scratch_shapes=[pltpu.VMEM((pack.rows, LANES), jnp.float32)]
        + rests_scratch(pack)
        + [
            pltpu.VMEM((pack.slots, pack.wide), jnp.float32),
            pltpu.VMEM((2 * width, pack.slots), jnp.bfloat16),
            pltpu.VMEM((width, rows), jnp.float32),
            pltpu.SemaphoreType.DMA((rows // columns,)),
            pltpu.SemaphoreType.DMA((4,)),
        ],
        compiler_params=compiler_params(),
        name="update_table",
    )(asked, in_hbm(packed), adagrad_sum, table_columns)


def exchange(payload):
    return lax.all_to_all(payload, ("dp", "blk"), split_axis=0, concat_axis=0, tiled=True)


def to_sibling(value, blk_count):
    return lax.ppermute(value, "blk", [(i, i ^ 1) for i in range(blk_count)])


def to_chip(value, blk_count, hops):
    return lax.ppermute(
        value, "blk", [(i, (i + 2 * hops) % blk_count) for i in range(blk_count)]
    )


def on_device(
    entity_table, adagrad_sum, relations, owner_map, head_ids, rel_ids, tail_ids, neg_ids
):
    dp_count = lax.axis_size("dp")
    blk_count = lax.axis_size("blk")
    owner_count = dp_count * blk_count
    chip_count = blk_count // 2
    rows_here, width = entity_table.shape
    edge_count = head_ids.shape[0]
    neg_count = neg_ids.shape[0]
    request_count = 2 * edge_count + neg_count
    capacity = -(-2 * request_count // owner_count // SUBLANES) * SUBLANES
    pack = Packing(width, owner_count, capacity)
    requests, address, slot_of = build_requests(
        pack, rows_here, owner_map, head_ids, tail_ids, neg_ids
    )
    asked = exchange(requests)
    served = serve(pack, asked, to_rows(pack, entity_table.T))
    fetched = exchange(served.reshape(owner_count, pack.stride, LANES))
    fetched = fetched.reshape(pack.rows, LANES)
    queries = unpack_heads(pack, edge_count, address, slot_of, fetched, relations[rel_ids].T)
    weight = float(blk_count * neg_count)
    arriving = [to_chip(queries, blk_count, hops) for hops in range(1, chip_count)]
    nearby = [queries, to_sibling(queries, blk_count)]
    positive, negatives, *negative_parts = unpack_rest(pack, neg_count, address, slot_of, fetched, queries)
    near, *near_parts = negative_terms(pack, weight, negative_parts, nearby)
    arriving, near, near_parts = lax.optimization_barrier((arriving, near, near_parts))
    distant = []
    for same in arriving:
        distant += [same, to_sibling(same, blk_count)]
    far, *far_parts = negative_terms(pack, weight, negative_parts, distant)
    totals = [near_parts[0], to_sibling(near_parts[1], blk_count)]
    for hops in range(1, chip_count):
        total = far_parts[2 * hops - 2] + to_sibling(far_parts[2 * hops - 1], blk_count)
        totals.append(to_chip(total, blk_count, chip_count - hops))
    partial, partial_rests = block_gradients(
        pack, address, slot_of, positive, negatives, nearby + distant, (near, far)
    )
    outgoing = finish_gradients(
        pack, address, slot_of, partial, partial_rests, positive, totals
    )
    incoming = exchange(outgoing.reshape(owner_count, pack.stride, LANES))
    new_columns, new_sum = update(
        pack, asked.reshape(1, -1), incoming.reshape(pack.rows, LANES),
        adagrad_sum.reshape(1, -1), entity_table.T,
    )
    return (new_columns.T, new_sum.reshape(-1))


def solution(mesh):
    return jax.shard_map(
        on_device,
        mesh=mesh,
        in_specs=(
            P(("dp", "blk"), None),
            P(("dp", "blk")),
            P(),
            P(),
            P(("dp", "blk")),
            P(("dp", "blk")),
            P(("dp", "blk")),
            P(("dp", "blk")),
        ),
        out_specs=(P(("dp", "blk"), None), P(("dp", "blk"))),
        check_vma=False,
    )
```

```python
import functools

import jax
import jax.numpy as jnp
from jax import lax
from jax.experimental import pallas as pl
from jax.experimental.pallas import tpu as pltpu
from jax.sharding import PartitionSpec as P

MARGIN = 10.0
EPSILON = 1e-05
LEARNING_RATE = 0.1
LANES = 128
SUBLANES = 8
VMEM_BYTES = 24 * 1024 * 1024


class Packing:
    def __init__(self, width, owners, capacity):
        self.width = width
        self.owners = owners
        self.capacity = capacity
        self.full = width // LANES
        self.rest = width - self.full * LANES
        assert 0 < self.rest <= LANES // SUBLANES and capacity % SUBLANES == 0
        self.shared = capacity // SUBLANES
        self.groups = self.full + 1
        self.wide = self.groups * LANES
        self.rests_at = self.full * capacity
        self.stride = self.rests_at + self.shared
        self.slots = owners * capacity
        self.rows = owners * self.stride


def compiler_params():
    return pltpu.CompilerParams(vmem_limit_bytes=VMEM_BYTES)


def vmem():
    return pl.BlockSpec(memory_space=pltpu.VMEM)


def smem():
    return pl.BlockSpec(memory_space=pltpu.SMEM)


def hbm():
    return pl.BlockSpec(memory_space=pltpu.HBM)


def in_hbm(value):
    return pltpu.with_memory_space_constraint(value, pltpu.HBM)


def split(value):
    high = value.astype(jnp.bfloat16)
    low = (value - high.astype(jnp.float32)).astype(jnp.bfloat16)
    return high, low


def dot_halves(left, right, contract):
    numbers = (contract, ((), ()))

    def dot(a, b):
        return lax.dot_general(a, b, numbers, preferred_element_type=jnp.float32)

    return dot(left[0], right[0]) + (dot(left[0], right[1]) + dot(left[1], right[0]))


def loop(count, body):
    def step(index, carry):
        body(index)
        return carry

    lax.fori_loop(0, count, step, 0)


def expand_rests(pack, packed_ref, shared_ref, rests_ref, first_owner=0, owners=None):
    owners = pack.owners if owners is None else owners
    for owner in range(first_owner, first_owner + owners):
        shared_ref[owner * pack.shared : (owner + 1) * pack.shared, :] = packed_ref[
            pl.ds(owner * pack.stride + pack.rests_at, pack.shared), :
        ]
    first = first_owner * pack.shared
    shared = shared_ref[first : first + owners * pack.shared, :]
    lane = lax.broadcasted_iota(jnp.int32, shared.shape, 1)
    for j in range(SUBLANES):
        moved = shared if j == 0 else pltpu.roll(shared, LANES - j * pack.rest, axis=1)
        rows = pl.ds(first * SUBLANES + j, shared.shape[0], stride=SUBLANES)
        rests_ref[rows, :] = jnp.where(lane < pack.rest, moved, 0.0)


def rests_scratch(pack):
    return [
        pltpu.VMEM((pack.owners * pack.shared, LANES), jnp.float32),
        pltpu.VMEM((pack.slots, LANES), jnp.float32),
    ]


def row_columns(pack, rows):
    parts = [rows[:, c, :].T for c in range(pack.groups)]
    return jnp.concatenate(parts, axis=0)[: pack.width]


def one_hot(mask):
    return mask.astype(jnp.float32).astype(jnp.bfloat16)


def request_kernel(
    pack, rows_here, map_hbm, head_hbm, tail_hbm, negative_hbm,
    request_ref, address_ref, slot_ref, map_ref, ids_ref, sems,
):
    copies = [pltpu.make_async_copy(map_hbm, map_ref, sems.at[0])]
    first = 0
    for index, source in enumerate((head_hbm, tail_hbm, negative_hbm)):
        target = ids_ref.at[:, pl.ds(first, source.shape[1])]
        copies.append(pltpu.make_async_copy(source, target, sems.at[index + 1]))
        first += source.shape[1]
    for copy in copies:
        copy.start()
    for copy in copies:
        copy.wait()
    ids = ids_ref[...]
    count = ids.shape[1]
    lines = map_ref.shape[0]

    def iota(rows, axis):
        return lax.broadcasted_iota(jnp.int32, (rows, count), axis)

    line_chosen = one_hot(iota(lines, 0) == ids // LANES)
    table = map_ref[...].T
    digits = [(table >> shift) & 255 for shift in range(0, 24, 8)]
    stacked = jnp.concatenate(digits, axis=0).astype(jnp.float32).astype(jnp.bfloat16)
    found = jnp.dot(stacked, line_chosen, preferred_element_type=jnp.float32)
    found = found[:LANES] + 256.0 * found[LANES : 2 * LANES] + 65536.0 * found[2 * LANES :]
    found = jnp.where(iota(LANES, 0) == ids % LANES, found, 0.0)
    position = jnp.sum(found, axis=0, keepdims=True).astype(jnp.int32)
    owner = position // rows_here
    row = position % rows_here
    to_owner = iota(pack.owners, 0) == owner
    earlier = one_hot(iota(count, 0) < iota(count, 1))
    before = jnp.dot(one_hot(to_owner), earlier, preferred_element_type=jnp.float32)
    rank = jnp.sum(jnp.where(to_owner, before, 0.0), axis=0, keepdims=True).astype(jnp.int32)
    slot_ref[...] = owner * pack.capacity + rank
    address_ref[...] = owner * pack.stride + rank * pack.full
    at_rank = one_hot(iota(pack.capacity, 0) == rank)
    absent = row - rows_here

    def place(values):
        chosen = jnp.where(to_owner, values.astype(jnp.float32), 0.0).astype(jnp.bfloat16)
        return lax.dot_general(
            chosen, at_rank, (((1,), (1,)), ((), ())), preferred_element_type=jnp.float32
        )

    high = -((-absent) // 256)
    low = absent - high * 256
    request_ref[:, 0, :] = (place(high) * 256.0 + place(low)).astype(jnp.int32) + rows_here


def build_requests(pack, rows_here, owner_map, head_ids, tail_ids, neg_ids):
    count = head_ids.shape[0] + tail_ids.shape[0] + neg_ids.shape[0]
    shape = jax.ShapeDtypeStruct
    return pl.pallas_call(
        functools.partial(request_kernel, pack, rows_here),
        out_shape=(
            shape((pack.owners, 1, pack.capacity), jnp.int32),
            shape((1, count), jnp.int32),
            shape((1, count), jnp.int32),
        ),
        in_specs=[hbm()] * 4,
        out_specs=(vmem(),) * 3,
        scratch_shapes=[
            pltpu.VMEM((owner_map.shape[0] // LANES, LANES), jnp.int32),
            pltpu.VMEM((1, count), jnp.int32),
            pltpu.SemaphoreType.DMA((4,)),
        ],
        compiler_params=compiler_params(),
        name="build_requests",
    )(
        in_hbm(owner_map.reshape(-1, LANES)), in_hbm(head_ids.reshape(1, -1)),
        in_hbm(tail_ids.reshape(1, -1)), in_hbm(neg_ids.reshape(1, -1)),
    )


def rows_kernel(pack, columns_ref, rows_ref, line_ref):
    count = columns_ref.shape[1]
    fill = jnp.zeros((pack.wide - pack.width, LANES), jnp.float32)
    place = lax.broadcasted_iota(jnp.int32, (LANES // SUBLANES, LANES), 1) // pack.rest
    for block in range(count // LANES):
        at = slice(block * LANES, (block + 1) * LANES)
        tile = jnp.concatenate([columns_ref[:, at], fill], axis=0)
        for c in range(pack.full):
            rows_ref[pl.ds(block * LANES * pack.full + c, LANES, stride=pack.full), :] = tile[
                c * LANES : (c + 1) * LANES
            ].T
        line_ref[...] = tile[pack.full * LANES :].T
        shared = line_ref[pl.ds(0, LANES // SUBLANES, stride=SUBLANES), :]
        for j in range(1, SUBLANES):
            rest = line_ref[pl.ds(j, LANES // SUBLANES, stride=SUBLANES), :]
            shared = jnp.where(place == j, pltpu.roll(rest, j * pack.rest, axis=1), shared)
        first = pack.full * (count + SUBLANES) + block * (LANES // SUBLANES)
        rows_ref[first : first + LANES // SUBLANES, :] = shared
    zeros = jnp.zeros((pack.full * SUBLANES, LANES), jnp.float32)
    rows_ref[pack.full * count : pack.full * (count + SUBLANES), :] = zeros
    rows_ref[pack.full * (count + SUBLANES) + count // SUBLANES :, :] = zeros[:SUBLANES]


def to_rows(pack, columns):
    count = columns.shape[1]
    lines = pack.full * (count + SUBLANES) + count // SUBLANES + SUBLANES
    return pl.pallas_call(
        functools.partial(rows_kernel, pack),
        out_shape=pltpu.VMEM((lines, LANES), jnp.float32),
        in_specs=[vmem()],
        out_specs=vmem(),
        scratch_shapes=[pltpu.VMEM((LANES, LANES), jnp.float32)],
        compiler_params=compiler_params(),
        name="table_rows",
    )(columns)


def sends(pack, out_ref, out_hbm, sems):
    count = sems.shape[0]
    each = pack.owners // count
    copies = []
    for index in range(count):
        rows = pl.ds(index * each * pack.stride, each * pack.stride)
        copies.append(pltpu.make_async_copy(out_ref.at[rows, :], out_hbm.at[rows, :], sems.at[index]))
    return copies, each


def share_rests(pack, rests_ref, out_ref, first_owner, owners):
    count = owners * pack.shared
    first = first_owner * pack.capacity
    shared = rests_ref[pl.ds(first, count, stride=SUBLANES), :]
    place = lax.broadcasted_iota(jnp.int32, shared.shape, 1) // pack.rest
    for j in range(1, SUBLANES):
        block = rests_ref[pl.ds(first + j, count, stride=SUBLANES), :]
        shared = jnp.where(place == j, pltpu.roll(block, j * pack.rest, axis=1), shared)
    for owner in range(owners):
        start = (first_owner + owner) * pack.stride + pack.rests_at
        out_ref[pl.ds(start, pack.shared), :] = shared[
            owner * pack.shared : (owner + 1) * pack.shared
        ]


def serve_kernel(
    pack, rows_here, asked_ref, table_ref, out_hbm, out_ref, rests_ref, table_rests_ref, sems
):
    copies, each = sends(pack, out_ref, out_hbm, sems)
    shared = table_ref[pack.full * (rows_here + SUBLANES) :, :]
    for j in range(SUBLANES):
        moved = shared if j == 0 else pltpu.roll(shared, LANES - j * pack.rest, axis=1)
        table_rests_ref[pl.ds(j, shared.shape[0], stride=SUBLANES), :] = moved

    def body(owner):
        base = owner * pack.stride
        slots = pl.multiple_of(owner * pack.capacity, SUBLANES)
        for first in range(0, pack.capacity, SUBLANES):
            rows = [asked_ref[owner, 0, first + j] for j in range(SUBLANES)]
            values = [table_ref[pl.ds(row * pack.full, pack.full), :] for row in rows]
            rests = [table_rests_ref[pl.ds(row, 1), :] for row in rows]
            for j in range(SUBLANES):
                out_ref[pl.ds(base + (first + j) * pack.full, pack.full), :] = values[j]
            rests_ref[pl.ds(slots + first, SUBLANES), :] = jnp.concatenate(rests, axis=0)

    for index, copy in enumerate(copies):
        loop(each, lambda owner: body(index * each + owner))
        share_rests(pack, rests_ref, out_ref, index * each, each)
        copy.start()
    for copy in copies:
        copy.wait()


def serve(pack, rows_here, asked, table_rows):
    return pl.pallas_call(
        functools.partial(serve_kernel, pack, rows_here),
        out_shape=pltpu.HBM((pack.rows, LANES), jnp.float32),
        in_specs=[smem(), vmem()],
        out_specs=hbm(),
        scratch_shapes=[
            pltpu.VMEM((pack.rows, LANES), jnp.float32),
            pltpu.VMEM((pack.slots, LANES), jnp.float32),
            pltpu.VMEM((rows_here + SUBLANES * SUBLANES, LANES), jnp.float32),
            pltpu.SemaphoreType.DMA((4,)),
        ],
        compiler_params=compiler_params(),
        name="serve_rows",
    )(asked, pltpu.with_memory_space_constraint(table_rows, pltpu.VMEM))


def copy_rows(pack, first_request, address_ref, slot_ref, packed_ref, rests_ref, rows_ref):
    def body(group):
        first = group * SUBLANES
        values = []
        for j in range(SUBLANES):
            request = first_request + first + j
            values.append(
                (
                    packed_ref[pl.ds(address_ref[0, request], pack.full), :],
                    rests_ref[pl.ds(slot_ref[0, request], 1), :],
                )
            )
        for j, (groups, rest) in enumerate(values):
            rows_ref[first + j, : pack.full, :] = groups
            rows_ref[first + j, pack.full :, :] = rest

    loop(rows_ref.shape[0] // SUBLANES, body)


def heads_kernel(
    pack, address_ref, slot_ref, packed_ref, relation_ref,
    query_ref, shared_ref, rests_ref, rows_ref,
):
    expand_rests(pack, packed_ref, shared_ref, rests_ref)
    copy_rows(pack, 0, address_ref, slot_ref, packed_ref, rests_ref, rows_ref)
    query_ref[...] = row_columns(pack, rows_ref[...]) + relation_ref[...]


def unpack_heads(pack, edges, address, slot, packed, relation_rows):
    return pl.pallas_call(
        functools.partial(heads_kernel, pack),
        out_shape=jax.ShapeDtypeStruct((pack.width, edges), jnp.float32),
        in_specs=[smem(), smem(), vmem(), vmem()],
        out_specs=vmem(),
        scratch_shapes=rests_scratch(pack)
        + [pltpu.VMEM((edges, pack.groups, LANES), jnp.float32)],
        compiler_params=compiler_params(),
        cost_estimate=pl.CostEstimate(flops=10**7, bytes_accessed=3 * 10**6, transcendentals=0),
        name="unpack_heads",
    )(address, slot, packed, relation_rows)


def rest_kernel(
    pack, edges, address_ref, slot_ref, packed_ref, query_ref,
    positive_ref, negative_ref, high_ref, low_ref, high_columns_ref, low_columns_ref, square_ref,
    shared_ref, rests_ref, rows_ref,
):
    expand_rests(pack, packed_ref, shared_ref, rests_ref)
    copy_rows(pack, edges, address_ref, slot_ref, packed_ref, rests_ref, rows_ref)
    for c in range(pack.groups):
        negative_ref[:, c * LANES : (c + 1) * LANES] = rows_ref[edges:, c, :]
    negatives = negative_ref[...]
    high_ref[...], low_ref[...] = split(negatives)
    high_columns_ref[...], low_columns_ref[...] = split(negatives.T[: pack.width])
    square_ref[...] = jnp.sum(negatives * negatives, axis=1, keepdims=True)
    residue = query_ref[...] - row_columns(pack, rows_ref[:edges])
    distance = jnp.sqrt(jnp.sum(residue * residue, axis=0, keepdims=True) + EPSILON)
    positive_ref[...] = jax.nn.sigmoid(distance - MARGIN) / distance * residue


def unpack_rest(pack, negatives, address, slot, packed, queries):
    edges = queries.shape[1]
    shape = jax.ShapeDtypeStruct
    return pl.pallas_call(
        functools.partial(rest_kernel, pack, edges),
        out_shape=(
            shape((pack.width, edges), jnp.float32),
            shape((negatives, pack.wide), jnp.float32),
            shape((negatives, pack.wide), jnp.bfloat16),
            shape((negatives, pack.wide), jnp.bfloat16),
            shape((pack.width, negatives), jnp.bfloat16),
            shape((pack.width, negatives), jnp.bfloat16),
            shape((negatives, 1), jnp.float32),
        ),
        in_specs=[smem(), smem(), vmem(), vmem()],
        out_specs=(vmem(),) * 7,
        scratch_shapes=rests_scratch(pack)
        + [pltpu.VMEM((edges + negatives, pack.groups, LANES), jnp.float32)],
        compiler_params=compiler_params(),
        cost_estimate=pl.CostEstimate(flops=10**7, bytes_accessed=9 * 10**6, transcendentals=0),
        name="unpack_rest",
    )(address, slot, packed, queries)


def gather_queries(pack, query_refs):
    queries = jnp.concatenate([ref[...] for ref in query_refs], axis=1)
    fill = jnp.zeros((pack.wide - pack.width, queries.shape[1]), jnp.float32)
    return jnp.concatenate([queries, fill], axis=0)


def negatives_kernel(pack, blocks, weight, *refs):
    half_refs = refs[:2]
    column_refs = refs[2:4]
    square_ref = refs[4]
    query_refs = refs[5 : 5 + blocks]
    coefficient_ref, *part_refs = refs[5 + blocks :]
    queries = gather_queries(pack, query_refs)
    query_sq = jnp.sum(queries * queries, axis=0, keepdims=True)
    inner = dot_halves([ref[...] for ref in half_refs], split(queries), ((1,), (0,)))
    squared = jnp.maximum(query_sq + square_ref[...] - 2.0 * inner + EPSILON, EPSILON)
    distance = jnp.sqrt(squared)
    coefficient = -1.0 / ((1.0 + jnp.exp(distance - MARGIN)) * (weight * distance))
    coefficient_ref[...] = coefficient
    part = queries[: pack.width] * jnp.sum(coefficient, axis=0, keepdims=True) - dot_halves(
        [ref[...] for ref in column_refs], split(coefficient), ((1,), (0,))
    )
    width = query_refs[0].shape[1]
    for index, ref in enumerate(part_refs):
        ref[...] = part[:, index * width : (index + 1) * width]


def negative_terms(pack, weight, negative_parts, queries):
    shape = jax.ShapeDtypeStruct
    count = sum(q.shape[1] for q in queries)
    rows = negative_parts[0].shape[0]
    return pl.pallas_call(
        functools.partial(negatives_kernel, pack, len(queries), weight),
        out_shape=(shape((rows, count), jnp.float32),)
        + tuple(shape(q.shape, jnp.float32) for q in queries),
        in_specs=[vmem()] * (len(negative_parts) + len(queries)),
        out_specs=(vmem(),) * (1 + len(queries)),
        compiler_params=compiler_params(),
        cost_estimate=pl.CostEstimate(
            flops=12 * rows * count * pack.wide, bytes_accessed=4 * 10**6, transcendentals=0
        ),
        name="negative_terms",
    )(*negative_parts, *queries)


def store_rows(pack, first_request, address_ref, slot_ref, rows_ref, out_ref, rests_ref):
    def body(group):
        first = group * SUBLANES
        values = [rows_ref[first + j] for j in range(SUBLANES)]
        for j, value in enumerate(values):
            request = first_request + first + j
            out_ref[pl.ds(address_ref[0, request], pack.full), :] = value[: pack.full]
            rests_ref[pl.ds(slot_ref[0, request], 1), :] = value[pack.full :]

    loop(rows_ref.shape[0] // SUBLANES, body)


def store_columns(pack, columns, rows_ref):
    fill = jnp.zeros((pack.wide - pack.width, columns.shape[1]), jnp.float32)
    columns = jnp.concatenate([columns, fill], axis=0)
    for c in range(pack.groups):
        rows_ref[:, c, :] = columns[c * LANES : (c + 1) * LANES].T


def block_kernel(pack, blocks, coefficients, address_ref, slot_ref, *refs):
    positive_ref, negative_ref = refs[:2]
    query_refs = refs[2 : 2 + blocks]
    coefficient_refs = refs[2 + blocks : 2 + blocks + coefficients]
    out_ref, rests_ref, rows_ref = refs[2 + blocks + coefficients :]
    edges = positive_ref.shape[1]
    out_ref[...] = jnp.zeros_like(out_ref)
    rests_ref[...] = jnp.zeros_like(rests_ref)
    store_columns(pack, -positive_ref[...], rows_ref.at[:edges])
    coefficient = jnp.concatenate([ref[...] for ref in coefficient_refs], axis=1)
    block_grad = negative_ref[...] * jnp.sum(coefficient, axis=1, keepdims=True) - dot_halves(
        split(coefficient), split(gather_queries(pack, query_refs)), ((1,), (1,))
    )
    for c in range(pack.groups):
        rows_ref[edges:, c, :] = block_grad[:, c * LANES : (c + 1) * LANES]
    store_rows(pack, edges, address_ref, slot_ref, rows_ref, out_ref, rests_ref)


def block_gradients(pack, address, slot, positive, negatives, queries, coefficients):
    shape = jax.ShapeDtypeStruct
    rows = positive.shape[1] + negatives.shape[0]
    flops = 6 * sum(c.size for c in coefficients) * pack.wide
    return pl.pallas_call(
        functools.partial(block_kernel, pack, len(queries), len(coefficients)),
        out_shape=(
            shape((pack.rows, LANES), jnp.float32),
            shape((pack.slots, LANES), jnp.float32),
        ),
        in_specs=[smem()] * 2 + [vmem()] * (2 + len(queries) + len(coefficients)),
        out_specs=(vmem(), vmem()),
        scratch_shapes=[pltpu.VMEM((rows, pack.groups, LANES), jnp.float32)],
        compiler_params=compiler_params(),
        cost_estimate=pl.CostEstimate(
            flops=flops, bytes_accessed=10**7, transcendentals=0
        ),
        name="block_gradients",
    )(address, slot, positive, negatives, *queries, *coefficients)


def finish_kernel(pack, parts, address_ref, slot_ref, *refs):
    positive_ref = refs[2]
    part_refs = refs[3 : 3 + parts]
    out_hbm, out_ref, rests_ref, rows_ref, sems = refs[3 + parts :]
    copies, each = sends(pack, out_ref, out_hbm, sems)
    total = positive_ref[...]
    for ref in part_refs:
        total = total + ref[...]
    store_columns(pack, total, rows_ref)
    store_rows(pack, 0, address_ref, slot_ref, rows_ref, out_ref, rests_ref)
    for index, copy in enumerate(copies):
        share_rests(pack, rests_ref, out_ref, index * each, each)
        copy.start()
    for copy in copies:
        copy.wait()


def finish_gradients(pack, address, slot, partial, partial_rests, positive, parts):
    edges = positive.shape[1]
    shape = jax.ShapeDtypeStruct
    return pl.pallas_call(
        functools.partial(finish_kernel, pack, len(parts)),
        out_shape=(
            pltpu.HBM((pack.rows, LANES), jnp.float32),
            shape(partial.shape, jnp.float32),
            shape(partial_rests.shape, jnp.float32),
        ),
        in_specs=[smem()] * 2 + [vmem()] * (3 + len(parts)),
        out_specs=(hbm(), vmem(), vmem()),
        input_output_aliases={2: 1, 3: 2},
        scratch_shapes=[
            pltpu.VMEM((edges, pack.groups, LANES), jnp.float32),
            pltpu.SemaphoreType.DMA((4,)),
        ],
        compiler_params=compiler_params(),
        name="finish_gradients",
    )(address, slot, partial, partial_rests, positive, *parts)[0]


def update_kernel(
    pack, columns, asked_ref, packed_hbm, sum_ref, table_ref, new_table_hbm, new_sum_ref,
    packed_ref, shared_ref, rests_ref, rows_ref, halves_ref, out_ref, sems, packed_sems,
):
    pieces = packed_sems.shape[0]
    owners = pack.owners // pieces
    loads = []
    for index in range(pieces):
        at = pl.ds(index * owners * pack.stride, owners * pack.stride)
        loads.append(
            pltpu.make_async_copy(packed_hbm.at[at, :], packed_ref.at[at, :], packed_sems.at[index])
        )
        loads[-1].start()
    width = pack.width
    for index, load in enumerate(loads):
        load.wait()
        expand_rests(pack, packed_ref, shared_ref, rests_ref, index * owners, owners)
        for owner in range(index * owners, (index + 1) * owners):
            rows = slice(owner * pack.capacity, (owner + 1) * pack.capacity)
            for c in range(pack.full):
                rows_ref[rows, c * LANES : (c + 1) * LANES] = packed_ref[
                    pl.ds(owner * pack.stride + c, pack.capacity, stride=pack.full), :
                ]
            rows_ref[rows, pack.full * LANES :] = rests_ref[rows, :]
        slots = slice(index * owners * pack.capacity, (index + 1) * owners * pack.capacity)
        high, low = split(rows_ref[slots, :].T)
        halves_ref[:width, slots] = high[:width]
        halves_ref[width:, slots] = low[:width]
    asked = asked_ref[...]
    row = lax.broadcasted_iota(jnp.int32, (columns, pack.slots), 0)
    copies = []
    for index in range(table_ref.shape[1] // columns):
        at = slice(index * columns, (index + 1) * columns)
        chosen = one_hot(row == asked - index * columns)
        both = lax.dot_general(
            halves_ref[...], chosen, (((1,), (1,)), ((), ())), preferred_element_type=jnp.float32
        )
        summed = both[:width] + both[width:]
        new_sum = sum_ref[:, at] + jnp.sum(summed * summed, axis=0, keepdims=True) / width
        new_sum_ref[:, at] = new_sum
        out_ref[:, at] = table_ref[:, at] - summed * (LEARNING_RATE / jnp.sqrt(new_sum))
        copies.append(
            pltpu.make_async_copy(out_ref.at[:, at], new_table_hbm.at[:, at], sems.at[index])
        )
        copies[-1].start()
    for copy in copies:
        copy.wait()


def update(pack, asked, packed, adagrad_sum, table_columns):
    width, rows = table_columns.shape
    columns = 256
    shape = jax.ShapeDtypeStruct
    return pl.pallas_call(
        functools.partial(update_kernel, pack, columns),
        out_shape=(pltpu.HBM((width, rows), jnp.float32), shape((1, rows), jnp.float32)),
        in_specs=[vmem(), hbm(), vmem(), vmem()],
        out_specs=(hbm(), vmem()),
        scratch_shapes=[pltpu.VMEM((pack.rows, LANES), jnp.float32)]
        + rests_scratch(pack)
        + [
            pltpu.VMEM((pack.slots, pack.wide), jnp.float32),
            pltpu.VMEM((2 * width, pack.slots), jnp.bfloat16),
            pltpu.VMEM((width, rows), jnp.float32),
            pltpu.SemaphoreType.DMA((rows // columns,)),
            pltpu.SemaphoreType.DMA((2,)),
        ],
        compiler_params=compiler_params(),
        name="update_table",
    )(asked, in_hbm(packed), adagrad_sum, table_columns)


def exchange(payload):
    return lax.all_to_all(payload, ("dp", "blk"), split_axis=0, concat_axis=0, tiled=True)


def to_sibling(value, blk_count):
    return lax.ppermute(value, "blk", [(i, i ^ 1) for i in range(blk_count)])


def to_chip(value, blk_count, hops):
    return lax.ppermute(
        value, "blk", [(i, (i + 2 * hops) % blk_count) for i in range(blk_count)]
    )


def on_device(
    entity_table, adagrad_sum, relations, owner_map, head_ids, rel_ids, tail_ids, neg_ids
):
    dp_count = lax.axis_size("dp")
    blk_count = lax.axis_size("blk")
    owner_count = dp_count * blk_count
    chip_count = blk_count // 2
    rows_here, width = entity_table.shape
    edge_count = head_ids.shape[0]
    neg_count = neg_ids.shape[0]
    request_count = 2 * edge_count + neg_count
    capacity = -(-2 * request_count // owner_count // SUBLANES) * SUBLANES
    pack = Packing(width, owner_count, capacity)
    requests, address, slot_of = build_requests(
        pack, rows_here, owner_map, head_ids, tail_ids, neg_ids
    )
    asked = exchange(requests)
    served = serve(pack, rows_here, asked, to_rows(pack, entity_table.T))
    fetched = exchange(served.reshape(owner_count, 1, pack.stride * LANES))
    fetched = fetched.reshape(pack.rows, LANES)
    queries = unpack_heads(pack, edge_count, address, slot_of, fetched, relations[rel_ids].T)
    weight = float(blk_count * neg_count)
    arriving = [to_chip(queries, blk_count, hops) for hops in range(1, chip_count)]
    nearby = [queries, to_sibling(queries, blk_count)]
    positive, negatives, *negative_parts = unpack_rest(pack, neg_count, address, slot_of, fetched, queries)
    near, *near_parts = negative_terms(pack, weight, negative_parts, nearby)
    arriving, near, near_parts = lax.optimization_barrier((arriving, near, near_parts))
    distant = []
    for same in arriving:
        distant += [same, to_sibling(same, blk_count)]
    far, *far_parts = negative_terms(pack, weight, negative_parts, distant)
    totals = [near_parts[0], to_sibling(near_parts[1], blk_count)]
    for hops in range(1, chip_count):
        total = far_parts[2 * hops - 2] + to_sibling(far_parts[2 * hops - 1], blk_count)
        totals.append(to_chip(total, blk_count, chip_count - hops))
    partial, partial_rests = block_gradients(
        pack, address, slot_of, positive, negatives, nearby + distant, (near, far)
    )
    outgoing = finish_gradients(
        pack, address, slot_of, partial, partial_rests, positive, totals
    )
    incoming = exchange(outgoing.reshape(owner_count, 1, pack.stride * LANES))
    new_columns, new_sum = update(
        pack, asked.reshape(1, -1), incoming.reshape(pack.rows, LANES),
        adagrad_sum.reshape(1, -1), entity_table.T,
    )
    return (new_columns.T, new_sum.reshape(-1))


def solution(mesh):
    return jax.shard_map(
        on_device,
        mesh=mesh,
        in_specs=(
            P(("dp", "blk"), None),
            P(("dp", "blk")),
            P(),
            P(),
            P(("dp", "blk")),
            P(("dp", "blk")),
            P(("dp", "blk")),
            P(("dp", "blk")),
        ),
        out_specs=(P(("dp", "blk"), None), P(("dp", "blk"))),
        check_vma=False,
    )
```

```python
import functools

import jax
import jax.numpy as jnp
from jax import lax
from jax.experimental import pallas as pl
from jax.experimental.pallas import tpu as pltpu
from jax.sharding import PartitionSpec as P

MARGIN = 10.0
EPSILON = 1e-05
LEARNING_RATE = 0.1
LANES = 128
SUBLANES = 8
SCORE_STEPS = 2
VMEM_BYTES = 24 * 1024 * 1024


class Packing:
    def __init__(self, width, owners, capacity):
        self.width = width
        self.owners = owners
        self.capacity = capacity
        self.full = width // LANES
        self.rest = width - self.full * LANES
        assert 0 < self.rest <= LANES // SUBLANES and capacity % SUBLANES == 0
        self.shared = capacity // SUBLANES
        self.groups = self.full + 1
        self.wide = self.groups * LANES
        self.rests_at = self.full * capacity
        self.stride = self.rests_at + self.shared
        self.slots = owners * capacity
        self.rest_rows = self.slots + SUBLANES
        self.rows = owners * self.stride


def compiler_params():
    return pltpu.CompilerParams(vmem_limit_bytes=VMEM_BYTES)


def vmem():
    return pl.BlockSpec(memory_space=pltpu.VMEM)


def smem():
    return pl.BlockSpec(memory_space=pltpu.SMEM)


def hbm():
    return pl.BlockSpec(memory_space=pltpu.HBM)


def in_hbm(value):
    return pltpu.with_memory_space_constraint(value, pltpu.HBM)


def split(value):
    high = value.astype(jnp.bfloat16)
    low = (value - high.astype(jnp.float32)).astype(jnp.bfloat16)
    return high, low


def dot_halves(left, right, contract):
    numbers = (contract, ((), ()))

    def dot(a, b):
        return lax.dot_general(a, b, numbers, preferred_element_type=jnp.float32)

    return dot(left[0], right[0]) + (dot(left[0], right[1]) + dot(left[1], right[0]))


def loop(count, body):
    def step(index, carry):
        body(index)
        return carry

    lax.fori_loop(0, count, step, 0)


def expand_rests(pack, packed_ref, shared_ref, rests_ref, first_owner=0, owners=None):
    owners = pack.owners if owners is None else owners
    for owner in range(first_owner, first_owner + owners):
        shared_ref[owner * pack.shared : (owner + 1) * pack.shared, :] = packed_ref[
            pl.ds(owner * pack.stride + pack.rests_at, pack.shared), :
        ]
    first = first_owner * pack.shared
    shared = shared_ref[first : first + owners * pack.shared, :]
    lane = lax.broadcasted_iota(jnp.int32, shared.shape, 1)
    for j in range(SUBLANES):
        moved = shared if j == 0 else pltpu.roll(shared, LANES - j * pack.rest, axis=1)
        rows = pl.ds(first * SUBLANES + j, shared.shape[0], stride=SUBLANES)
        rests_ref[rows, :] = jnp.where(lane < pack.rest, moved, 0.0)


def rests_scratch(pack):
    return [
        pltpu.VMEM((pack.owners * pack.shared, LANES), jnp.float32),
        pltpu.VMEM((pack.rest_rows, LANES), jnp.float32),
    ]


def row_columns(pack, rows):
    parts = [rows[:, c, :].T for c in range(pack.groups)]
    return jnp.concatenate(parts, axis=0)[: pack.width]


def one_hot(mask):
    return mask.astype(jnp.float32).astype(jnp.bfloat16)


def request_kernel(
    pack, rows_here, map_hbm, head_hbm, tail_hbm, negative_hbm,
    request_ref, address_ref, slot_ref, map_ref, ids_ref, sems,
):
    copies = [pltpu.make_async_copy(map_hbm, map_ref, sems.at[0])]
    first = 0
    for index, source in enumerate((head_hbm, tail_hbm, negative_hbm)):
        target = ids_ref.at[:, pl.ds(first, source.shape[1])]
        copies.append(pltpu.make_async_copy(source, target, sems.at[index + 1]))
        first += source.shape[1]
    for copy in copies:
        copy.start()
    for copy in copies[1:]:
        copy.wait()
    ids = ids_ref[...]
    count = ids.shape[1]
    lines = map_ref.shape[0]

    def iota(rows, axis):
        return lax.broadcasted_iota(jnp.int32, (rows, count), axis)

    line_chosen = one_hot(iota(lines, 0) == ids // LANES)
    earlier = one_hot(iota(count, 0) < iota(count, 1))
    copies[0].wait()
    table = map_ref[...].T
    digits = [(table >> shift) & 255 for shift in range(0, 24, 8)]
    stacked = jnp.concatenate(digits, axis=0).astype(jnp.float32).astype(jnp.bfloat16)
    found = jnp.dot(stacked, line_chosen, preferred_element_type=jnp.float32)
    found = found[:LANES] + 256.0 * found[LANES : 2 * LANES] + 65536.0 * found[2 * LANES :]
    found = jnp.where(iota(LANES, 0) == ids % LANES, found, 0.0)
    position = jnp.sum(found, axis=0, keepdims=True).astype(jnp.int32)
    owner = position // rows_here
    row = position % rows_here
    to_owner = iota(pack.owners, 0) == owner
    before = jnp.dot(one_hot(to_owner), earlier, preferred_element_type=jnp.float32)
    rank = jnp.sum(jnp.where(to_owner, before, 0.0), axis=0, keepdims=True).astype(jnp.int32)
    slot_ref[...] = owner * pack.capacity + rank
    address_ref[...] = owner * pack.stride + rank * pack.full
    at_rank = one_hot(iota(pack.capacity, 0) == rank)
    absent = row - rows_here

    def place(values):
        chosen = jnp.where(to_owner, values.astype(jnp.float32), 0.0).astype(jnp.bfloat16)
        return lax.dot_general(
            chosen, at_rank, (((1,), (1,)), ((), ())), preferred_element_type=jnp.float32
        )

    high = -((-absent) // 256)
    low = absent - high * 256
    request_ref[:, 0, :] = (place(high) * 256.0 + place(low)).astype(jnp.int32) + rows_here


def build_requests(pack, rows_here, owner_map, head_ids, tail_ids, neg_ids):
    count = head_ids.shape[0] + tail_ids.shape[0] + neg_ids.shape[0]
    shape = jax.ShapeDtypeStruct
    return pl.pallas_call(
        functools.partial(request_kernel, pack, rows_here),
        out_shape=(
            shape((pack.owners, 1, pack.capacity), jnp.int32),
            shape((1, count), jnp.int32),
            shape((1, count), jnp.int32),
        ),
        in_specs=[hbm()] * 4,
        out_specs=(vmem(),) * 3,
        scratch_shapes=[
            pltpu.VMEM((owner_map.shape[0] // LANES, LANES), jnp.int32),
            pltpu.VMEM((1, count), jnp.int32),
            pltpu.SemaphoreType.DMA((4,)),
        ],
        compiler_params=compiler_params(),
        name="build_requests",
    )(
        in_hbm(owner_map.reshape(-1, LANES)), in_hbm(head_ids.reshape(1, -1)),
        in_hbm(tail_ids.reshape(1, -1)), in_hbm(neg_ids.reshape(1, -1)),
    )


def rows_kernel(pack, columns_ref, rows_ref, line_ref):
    count = columns_ref.shape[1]
    fill = jnp.zeros((pack.wide - pack.width, LANES), jnp.float32)
    place = lax.broadcasted_iota(jnp.int32, (LANES // SUBLANES, LANES), 1) // pack.rest
    for block in range(count // LANES):
        at = slice(block * LANES, (block + 1) * LANES)
        tile = jnp.concatenate([columns_ref[:, at], fill], axis=0)
        for c in range(pack.full):
            rows_ref[pl.ds(block * LANES * pack.full + c, LANES, stride=pack.full), :] = tile[
                c * LANES : (c + 1) * LANES
            ].T
        line_ref[:LANES, :] = tile[pack.full * LANES :].T
        shared = line_ref[pl.ds(0, LANES // SUBLANES, stride=SUBLANES), :]
        for j in range(1, SUBLANES):
            rest = line_ref[pl.ds(j, LANES // SUBLANES, stride=SUBLANES), :]
            shared = jnp.where(place == j, pltpu.roll(rest, j * pack.rest, axis=1), shared)
        first = pack.full * (count + SUBLANES) + block * (LANES // SUBLANES)
        rows_ref[first : first + LANES // SUBLANES, :] = shared
    zeros = jnp.zeros((pack.full * SUBLANES, LANES), jnp.float32)
    rows_ref[pack.full * count : pack.full * (count + SUBLANES), :] = zeros
    rows_ref[pack.full * (count + SUBLANES) + count // SUBLANES :, :] = zeros[:SUBLANES]


def to_rows(pack, columns):
    count = columns.shape[1]
    lines = pack.full * (count + SUBLANES) + count // SUBLANES + SUBLANES
    return pl.pallas_call(
        functools.partial(rows_kernel, pack),
        out_shape=pltpu.VMEM((lines, LANES), jnp.float32),
        in_specs=[vmem()],
        out_specs=vmem(),
        scratch_shapes=[pltpu.VMEM((LANES + SUBLANES, LANES), jnp.float32)],
        compiler_params=compiler_params(),
        name="table_rows",
    )(columns)


def sends(pack, out_ref, out_hbm, sems):
    count = sems.shape[0]
    each = pack.owners // count
    copies = []
    for index in range(count):
        rows = pl.ds(index * each * pack.stride, each * pack.stride)
        copies.append(pltpu.make_async_copy(out_ref.at[rows, :], out_hbm.at[rows, :], sems.at[index]))
    return copies, each


def share_rests(pack, rests_ref, out_ref, first_owner, owners):
    count = owners * pack.shared
    first = first_owner * pack.capacity
    shared = rests_ref[pl.ds(first, count, stride=SUBLANES), :]
    place = lax.broadcasted_iota(jnp.int32, shared.shape, 1) // pack.rest
    for j in range(1, SUBLANES):
        block = rests_ref[pl.ds(first + j, count, stride=SUBLANES), :]
        shared = jnp.where(place == j, pltpu.roll(block, j * pack.rest, axis=1), shared)
    for owner in range(owners):
        start = (first_owner + owner) * pack.stride + pack.rests_at
        out_ref[pl.ds(start, pack.shared), :] = shared[
            owner * pack.shared : (owner + 1) * pack.shared
        ]


def serve_kernel(
    pack, rows_here, asked_ref, table_ref, out_hbm, out_ref, rests_ref, table_rests_ref, sems
):
    copies, each = sends(pack, out_ref, out_hbm, sems)
    shared = table_ref[pack.full * (rows_here + SUBLANES) :, :]
    for j in range(SUBLANES):
        moved = shared if j == 0 else pltpu.roll(shared, LANES - j * pack.rest, axis=1)
        table_rests_ref[pl.ds(j, shared.shape[0], stride=SUBLANES), :] = moved

    def body(owner):
        base = owner * pack.stride
        slots = pl.multiple_of(owner * pack.capacity, SUBLANES)
        for first in range(0, pack.capacity, SUBLANES):
            rows = [asked_ref[owner, 0, first + j] for j in range(SUBLANES)]
            values = [table_ref[pl.ds(row * pack.full, pack.full), :] for row in rows]
            rests = [table_rests_ref[pl.ds(row, 1), :] for row in rows]
            for j in range(SUBLANES):
                out_ref[pl.ds(base + (first + j) * pack.full, pack.full), :] = values[j]
            rests_ref[pl.ds(slots + first, SUBLANES), :] = jnp.concatenate(rests, axis=0)

    for index, copy in enumerate(copies):
        loop(each, lambda owner: body(index * each + owner))
        share_rests(pack, rests_ref, out_ref, index * each, each)
        copy.start()
    for copy in copies:
        copy.wait()


def serve(pack, rows_here, asked, table_rows):
    return pl.pallas_call(
        functools.partial(serve_kernel, pack, rows_here),
        out_shape=pltpu.HBM((pack.rows, LANES), jnp.float32),
        in_specs=[smem(), vmem()],
        out_specs=hbm(),
        scratch_shapes=[
            pltpu.VMEM((pack.rows, LANES), jnp.float32),
            pltpu.VMEM((pack.rest_rows, LANES), jnp.float32),
            pltpu.VMEM((rows_here + SUBLANES * (SUBLANES + 1), LANES), jnp.float32),
            pltpu.SemaphoreType.DMA((4,)),
        ],
        compiler_params=compiler_params(),
        name="serve_rows",
    )(asked, pltpu.with_memory_space_constraint(table_rows, pltpu.VMEM))


def copy_rows(pack, first_request, address_ref, slot_ref, packed_ref, rests_ref, rows_ref):
    def body(group):
        first = group * SUBLANES
        values = []
        for j in range(SUBLANES):
            request = first_request + first + j
            values.append(
                (
                    packed_ref[pl.ds(address_ref[0, request], pack.full), :],
                    rests_ref[pl.ds(slot_ref[0, request], 1), :],
                )
            )
        for j, (groups, rest) in enumerate(values):
            rows_ref[first + j, : pack.full, :] = groups
            rows_ref[first + j, pack.full :, :] = rest

    loop(rows_ref.shape[0] // SUBLANES, body)


def heads_kernel(
    pack, address_ref, slot_ref, packed_ref, relation_ref,
    query_ref, shared_ref, rests_ref, rows_ref,
):
    expand_rests(pack, packed_ref, shared_ref, rests_ref)
    copy_rows(pack, 0, address_ref, slot_ref, packed_ref, rests_ref, rows_ref)
    query_ref[...] = row_columns(pack, rows_ref[...]) + relation_ref[...]


def unpack_heads(pack, edges, address, slot, packed, relation_rows):
    return pl.pallas_call(
        functools.partial(heads_kernel, pack),
        out_shape=jax.ShapeDtypeStruct((pack.width, edges), jnp.float32),
        in_specs=[smem(), smem(), vmem(), vmem()],
        out_specs=vmem(),
        scratch_shapes=rests_scratch(pack)
        + [pltpu.VMEM((edges, pack.groups, LANES), jnp.float32)],
        compiler_params=compiler_params(),
        cost_estimate=pl.CostEstimate(flops=10**7, bytes_accessed=3 * 10**6, transcendentals=0),
        name="unpack_heads",
    )(address, slot, packed, relation_rows)


def rest_kernel(
    pack, edges, address_ref, slot_ref, packed_ref, query_ref,
    positive_ref, negative_ref, high_ref, low_ref, high_columns_ref, low_columns_ref, square_ref,
    shared_ref, rests_ref, rows_ref,
):
    expand_rests(pack, packed_ref, shared_ref, rests_ref)
    copy_rows(pack, edges, address_ref, slot_ref, packed_ref, rests_ref, rows_ref)
    for c in range(pack.groups):
        negative_ref[:, c * LANES : (c + 1) * LANES] = rows_ref[edges:, c, :]
    negatives = negative_ref[...]
    high_ref[...], low_ref[...] = split(negatives)
    high_columns_ref[...], low_columns_ref[...] = split(negatives.T[: pack.width])
    square_ref[...] = jnp.sum(negatives * negatives, axis=1, keepdims=True)
    residue = query_ref[...] - row_columns(pack, rows_ref[:edges])
    distance = jnp.sqrt(jnp.sum(residue * residue, axis=0, keepdims=True) + EPSILON)
    positive_ref[...] = jax.nn.sigmoid(distance - MARGIN) / distance * residue


def unpack_rest(pack, negatives, address, slot, packed, queries):
    edges = queries.shape[1]
    shape = jax.ShapeDtypeStruct
    return pl.pallas_call(
        functools.partial(rest_kernel, pack, edges),
        out_shape=(
            shape((pack.width, edges), jnp.float32),
            shape((negatives, pack.wide), jnp.float32),
            shape((negatives, pack.wide), jnp.bfloat16),
            shape((negatives, pack.wide), jnp.bfloat16),
            shape((pack.width, negatives), jnp.bfloat16),
            shape((pack.width, negatives), jnp.bfloat16),
            shape((negatives, 1), jnp.float32),
        ),
        in_specs=[smem(), smem(), vmem(), vmem()],
        out_specs=(vmem(),) * 7,
        scratch_shapes=rests_scratch(pack)
        + [pltpu.VMEM((edges + negatives, pack.groups, LANES), jnp.float32)],
        compiler_params=compiler_params(),
        cost_estimate=pl.CostEstimate(flops=10**7, bytes_accessed=9 * 10**6, transcendentals=0),
        name="unpack_rest",
    )(address, slot, packed, queries)


def gather_queries(pack, query_refs):
    queries = jnp.concatenate([ref[...] for ref in query_refs], axis=1)
    fill = jnp.zeros((pack.wide - pack.width, queries.shape[1]), jnp.float32)
    return jnp.concatenate([queries, fill], axis=0)


def negatives_kernel(pack, blocks, weight, *refs):
    half_refs = refs[:2]
    column_refs = refs[2:4]
    square_ref = refs[4]
    query_refs = refs[5 : 5 + blocks]
    coefficient_ref, *part_refs = refs[5 + blocks :]
    queries = gather_queries(pack, query_refs)
    query_sq = jnp.sum(queries * queries, axis=0, keepdims=True)
    query_halves = split(queries)
    count = square_ref.shape[0]
    weights, parts = [], []
    for first in range(0, count, count // SCORE_STEPS):
        rows = slice(first, first + count // SCORE_STEPS)
        inner = dot_halves([ref[rows, :] for ref in half_refs], query_halves, ((1,), (0,)))
        squared = jnp.maximum(query_sq + square_ref[rows, :] - 2.0 * inner + EPSILON, EPSILON)
        distance = jnp.sqrt(squared)
        coefficient = -1.0 / ((1.0 + jnp.exp(distance - MARGIN)) * (weight * distance))
        coefficient_ref[rows, :] = coefficient
        weights.append(jnp.sum(coefficient, axis=0, keepdims=True))
        parts.append(
            dot_halves([ref[:, rows] for ref in column_refs], split(coefficient), ((1,), (0,)))
        )
    part = queries[: pack.width] * sum(weights) - sum(parts)
    width = query_refs[0].shape[1]
    for index, ref in enumerate(part_refs):
        ref[...] = part[:, index * width : (index + 1) * width]


def negative_terms(pack, weight, negative_parts, queries):
    shape = jax.ShapeDtypeStruct
    count = sum(q.shape[1] for q in queries)
    rows = negative_parts[0].shape[0]
    return pl.pallas_call(
        functools.partial(negatives_kernel, pack, len(queries), weight),
        out_shape=(shape((rows, count), jnp.float32),)
        + tuple(shape(q.shape, jnp.float32) for q in queries),
        in_specs=[vmem()] * (len(negative_parts) + len(queries)),
        out_specs=(vmem(),) * (1 + len(queries)),
        compiler_params=compiler_params(),
        cost_estimate=pl.CostEstimate(
            flops=12 * rows * count * pack.wide, bytes_accessed=4 * 10**6, transcendentals=0
        ),
        name="negative_terms",
    )(*negative_parts, *queries)


def store_rows(pack, first_request, address_ref, slot_ref, rows_ref, out_ref, rests_ref):
    def body(group):
        first = group * SUBLANES
        values = [rows_ref[first + j] for j in range(SUBLANES)]
        for j, value in enumerate(values):
            request = first_request + first + j
            out_ref[pl.ds(address_ref[0, request], pack.full), :] = value[: pack.full]
            rests_ref[pl.ds(slot_ref[0, request], 1), :] = value[pack.full :]

    loop(rows_ref.shape[0] // SUBLANES, body)


def store_columns(pack, columns, rows_ref):
    fill = jnp.zeros((pack.wide - pack.width, columns.shape[1]), jnp.float32)
    columns = jnp.concatenate([columns, fill], axis=0)
    for c in range(pack.groups):
        rows_ref[:, c, :] = columns[c * LANES : (c + 1) * LANES].T


def block_kernel(pack, blocks, coefficients, address_ref, slot_ref, *refs):
    positive_ref, negative_ref = refs[:2]
    query_refs = refs[2 : 2 + blocks]
    coefficient_refs = refs[2 + blocks : 2 + blocks + coefficients]
    out_ref, rests_ref, rows_ref = refs[2 + blocks + coefficients :]
    edges = positive_ref.shape[1]
    out_ref[...] = jnp.zeros_like(out_ref)
    rests_ref[...] = jnp.zeros_like(rests_ref)
    store_columns(pack, -positive_ref[...], rows_ref.at[:edges])
    coefficient = jnp.concatenate([ref[...] for ref in coefficient_refs], axis=1)
    block_grad = negative_ref[...] * jnp.sum(coefficient, axis=1, keepdims=True) - dot_halves(
        split(coefficient), split(gather_queries(pack, query_refs)), ((1,), (1,))
    )
    for c in range(pack.groups):
        rows_ref[edges:, c, :] = block_grad[:, c * LANES : (c + 1) * LANES]
    store_rows(pack, edges, address_ref, slot_ref, rows_ref, out_ref, rests_ref)


def block_gradients(pack, address, slot, positive, negatives, queries, coefficients):
    shape = jax.ShapeDtypeStruct
    rows = positive.shape[1] + negatives.shape[0]
    flops = 6 * sum(c.size for c in coefficients) * pack.wide
    return pl.pallas_call(
        functools.partial(block_kernel, pack, len(queries), len(coefficients)),
        out_shape=(
            shape((pack.rows, LANES), jnp.float32),
            shape((pack.rest_rows, LANES), jnp.float32),
        ),
        in_specs=[smem()] * 2 + [vmem()] * (2 + len(queries) + len(coefficients)),
        out_specs=(vmem(), vmem()),
        scratch_shapes=[pltpu.VMEM((rows, pack.groups, LANES), jnp.float32)],
        compiler_params=compiler_params(),
        cost_estimate=pl.CostEstimate(
            flops=flops, bytes_accessed=10**7, transcendentals=0
        ),
        name="block_gradients",
    )(address, slot, positive, negatives, *queries, *coefficients)


def finish_kernel(pack, parts, address_ref, slot_ref, *refs):
    positive_ref = refs[2]
    part_refs = refs[3 : 3 + parts]
    out_hbm, out_ref, rests_ref, rows_ref, sems = refs[3 + parts :]
    copies, each = sends(pack, out_ref, out_hbm, sems)
    total = positive_ref[...]
    for ref in part_refs:
        total = total + ref[...]
    store_columns(pack, total, rows_ref)
    store_rows(pack, 0, address_ref, slot_ref, rows_ref, out_ref, rests_ref)
    for index, copy in enumerate(copies):
        share_rests(pack, rests_ref, out_ref, index * each, each)
        copy.start()
    for copy in copies:
        copy.wait()


def finish_gradients(pack, address, slot, partial, partial_rests, positive, parts):
    edges = positive.shape[1]
    shape = jax.ShapeDtypeStruct
    return pl.pallas_call(
        functools.partial(finish_kernel, pack, len(parts)),
        out_shape=(
            pltpu.HBM((pack.rows, LANES), jnp.float32),
            shape(partial.shape, jnp.float32),
            shape(partial_rests.shape, jnp.float32),
        ),
        in_specs=[smem()] * 2 + [vmem()] * (3 + len(parts)),
        out_specs=(hbm(), vmem(), vmem()),
        input_output_aliases={2: 1, 3: 2},
        scratch_shapes=[
            pltpu.VMEM((edges, pack.groups, LANES), jnp.float32),
            pltpu.SemaphoreType.DMA((4,)),
        ],
        compiler_params=compiler_params(),
        name="finish_gradients",
    )(address, slot, partial, partial_rests, positive, *parts)[0]


def update_kernel(
    pack, columns, asked_ref, packed_hbm, sum_ref, table_ref, new_table_hbm, new_sum_ref,
    packed_ref, shared_ref, rests_ref, rows_ref, halves_ref, out_ref, sems, packed_sems,
):
    pieces = packed_sems.shape[0]
    owners = pack.owners // pieces
    loads = []
    for index in range(pieces):
        at = pl.ds(index * owners * pack.stride, owners * pack.stride)
        loads.append(
            pltpu.make_async_copy(packed_hbm.at[at, :], packed_ref.at[at, :], packed_sems.at[index])
        )
        loads[-1].start()
    width = pack.width
    for index, load in enumerate(loads):
        load.wait()
        expand_rests(pack, packed_ref, shared_ref, rests_ref, index * owners, owners)
        for owner in range(index * owners, (index + 1) * owners):
            rows = slice(owner * pack.capacity, (owner + 1) * pack.capacity)
            for c in range(pack.full):
                rows_ref[rows, c * LANES : (c + 1) * LANES] = packed_ref[
                    pl.ds(owner * pack.stride + c, pack.capacity, stride=pack.full), :
                ]
            rows_ref[rows, pack.full * LANES :] = rests_ref[rows, :]
        slots = slice(index * owners * pack.capacity, (index + 1) * owners * pack.capacity)
        high, low = split(rows_ref[slots, :].T)
        halves_ref[:width, slots] = high[:width]
        halves_ref[width:, slots] = low[:width]
    asked = asked_ref[...]
    row = lax.broadcasted_iota(jnp.int32, (columns, pack.slots), 0)
    copies = []
    for index in range(table_ref.shape[1] // columns):
        at = slice(index * columns, (index + 1) * columns)
        chosen = one_hot(row == asked - index * columns)
        both = lax.dot_general(
            halves_ref[...], chosen, (((1,), (1,)), ((), ())), preferred_element_type=jnp.float32
        )
        summed = both[:width] + both[width:]
        new_sum = sum_ref[:, at] + jnp.sum(summed * summed, axis=0, keepdims=True) / width
        new_sum_ref[:, at] = new_sum
        out_ref[:, at] = table_ref[:, at] - summed * (LEARNING_RATE / jnp.sqrt(new_sum))
        copies.append(
            pltpu.make_async_copy(out_ref.at[:, at], new_table_hbm.at[:, at], sems.at[index])
        )
        copies[-1].start()
    for copy in copies:
        copy.wait()


def update(pack, asked, packed, adagrad_sum, table_columns):
    width, rows = table_columns.shape
    columns = 256
    shape = jax.ShapeDtypeStruct
    return pl.pallas_call(
        functools.partial(update_kernel, pack, columns),
        out_shape=(pltpu.HBM((width, rows), jnp.float32), shape((1, rows), jnp.float32)),
        in_specs=[vmem(), hbm(), vmem(), vmem()],
        out_specs=(hbm(), vmem()),
        scratch_shapes=[pltpu.VMEM((pack.rows, LANES), jnp.float32)]
        + rests_scratch(pack)
        + [
            pltpu.VMEM((pack.slots, pack.wide), jnp.float32),
            pltpu.VMEM((2 * width, pack.slots), jnp.bfloat16),
            pltpu.VMEM((width, rows), jnp.float32),
            pltpu.SemaphoreType.DMA((rows // columns,)),
            pltpu.SemaphoreType.DMA((2,)),
        ],
        compiler_params=compiler_params(),
        name="update_table",
    )(asked, in_hbm(packed), adagrad_sum, table_columns)


def exchange(payload):
    return lax.all_to_all(payload, ("dp", "blk"), split_axis=0, concat_axis=0, tiled=True)


def to_sibling(value, blk_count):
    return lax.ppermute(value, "blk", [(i, i ^ 1) for i in range(blk_count)])


def to_chip(value, blk_count, hops):
    return lax.ppermute(
        value, "blk", [(i, (i + 2 * hops) % blk_count) for i in range(blk_count)]
    )


def on_device(
    entity_table, adagrad_sum, relations, owner_map, head_ids, rel_ids, tail_ids, neg_ids
):
    dp_count = lax.axis_size("dp")
    blk_count = lax.axis_size("blk")
    owner_count = dp_count * blk_count
    chip_count = blk_count // 2
    rows_here, width = entity_table.shape
    edge_count = head_ids.shape[0]
    neg_count = neg_ids.shape[0]
    request_count = 2 * edge_count + neg_count
    capacity = -(-2 * request_count // owner_count // SUBLANES) * SUBLANES
    pack = Packing(width, owner_count, capacity)
    requests, address, slot_of = build_requests(
        pack, rows_here, owner_map, head_ids, tail_ids, neg_ids
    )
    asked = exchange(requests)
    served = serve(pack, rows_here, asked, to_rows(pack, entity_table.T))
    fetched = exchange(served.reshape(owner_count, 1, pack.stride * LANES))
    fetched = fetched.reshape(pack.rows, LANES)
    queries = unpack_heads(pack, edge_count, address, slot_of, fetched, relations[rel_ids].T)
    weight = float(blk_count * neg_count)
    arriving = [to_chip(queries, blk_count, hops) for hops in range(1, chip_count)]
    nearby = [queries, to_sibling(queries, blk_count)]
    positive, negatives, *negative_parts = unpack_rest(pack, neg_count, address, slot_of, fetched, queries)
    near, *near_parts = negative_terms(pack, weight, negative_parts, nearby)
    arriving, near, near_parts = lax.optimization_barrier((arriving, near, near_parts))
    distant = []
    for same in arriving:
        distant += [same, to_sibling(same, blk_count)]
    far, *far_parts = negative_terms(pack, weight, negative_parts, distant)
    totals = [near_parts[0], to_sibling(near_parts[1], blk_count)]
    for hops in range(1, chip_count):
        total = far_parts[2 * hops - 2] + to_sibling(far_parts[2 * hops - 1], blk_count)
        totals.append(to_chip(total, blk_count, chip_count - hops))
    partial, partial_rests = block_gradients(
        pack, address, slot_of, positive, negatives, nearby + distant, (near, far)
    )
    outgoing = finish_gradients(
        pack, address, slot_of, partial, partial_rests, positive, totals
    )
    incoming = exchange(outgoing.reshape(owner_count, 1, pack.stride * LANES))
    new_columns, new_sum = update(
        pack, asked.reshape(1, -1), incoming.reshape(pack.rows, LANES),
        adagrad_sum.reshape(1, -1), entity_table.T,
    )
    return (new_columns.T, new_sum.reshape(-1))


def solution(mesh):
    return jax.shard_map(
        on_device,
        mesh=mesh,
        in_specs=(
            P(("dp", "blk"), None),
            P(("dp", "blk")),
            P(),
            P(),
            P(("dp", "blk")),
            P(("dp", "blk")),
            P(("dp", "blk")),
            P(("dp", "blk")),
        ),
        out_specs=(P(("dp", "blk"), None), P(("dp", "blk"))),
        check_vma=False,
    )
```

```python
import functools

import jax
import jax.numpy as jnp
from jax import lax
from jax.experimental import pallas as pl
from jax.experimental.pallas import tpu as pltpu
from jax.sharding import PartitionSpec as P

MARGIN = 10.0
EPSILON = 1e-05
LEARNING_RATE = 0.1
LANES = 128
SUBLANES = 8
SCORE_STEPS = 2
SERVE_OWNERS = 4
VMEM_BYTES = 24 * 1024 * 1024


class Packing:
    def __init__(self, width, owners, capacity):
        self.width = width
        self.owners = owners
        self.capacity = capacity
        self.full = width // LANES
        self.rest = width - self.full * LANES
        assert 0 < self.rest <= LANES // SUBLANES and capacity % SUBLANES == 0
        self.shared = capacity // SUBLANES
        self.groups = self.full + 1
        self.wide = self.groups * LANES
        self.rests_at = self.full * capacity
        self.stride = self.rests_at + self.shared
        self.slots = owners * capacity
        self.rest_rows = self.slots + SUBLANES
        self.rows = owners * self.stride


def compiler_params():
    return pltpu.CompilerParams(vmem_limit_bytes=VMEM_BYTES)


def vmem():
    return pl.BlockSpec(memory_space=pltpu.VMEM)


def smem():
    return pl.BlockSpec(memory_space=pltpu.SMEM)


def hbm():
    return pl.BlockSpec(memory_space=pltpu.HBM)


def in_hbm(value):
    return pltpu.with_memory_space_constraint(value, pltpu.HBM)


def split(value):
    high = value.astype(jnp.bfloat16)
    low = (value - high.astype(jnp.float32)).astype(jnp.bfloat16)
    return high, low


def dot_halves(left, right, contract):
    numbers = (contract, ((), ()))

    def dot(a, b):
        return lax.dot_general(a, b, numbers, preferred_element_type=jnp.float32)

    return dot(left[0], right[0]) + (dot(left[0], right[1]) + dot(left[1], right[0]))


def loop(count, body):
    def step(index, carry):
        body(index)
        return carry

    lax.fori_loop(0, count, step, 0)


def expand_rests(pack, packed_ref, shared_ref, rests_ref, first_owner=0, owners=None):
    owners = pack.owners if owners is None else owners
    for owner in range(first_owner, first_owner + owners):
        shared_ref[owner * pack.shared : (owner + 1) * pack.shared, :] = packed_ref[
            pl.ds(owner * pack.stride + pack.rests_at, pack.shared), :
        ]
    first = first_owner * pack.shared
    shared = shared_ref[first : first + owners * pack.shared, :]
    lane = lax.broadcasted_iota(jnp.int32, shared.shape, 1)
    for j in range(SUBLANES):
        moved = shared if j == 0 else pltpu.roll(shared, LANES - j * pack.rest, axis=1)
        rows = pl.ds(first * SUBLANES + j, shared.shape[0], stride=SUBLANES)
        rests_ref[rows, :] = jnp.where(lane < pack.rest, moved, 0.0)


def rests_scratch(pack):
    return [
        pltpu.VMEM((pack.owners * pack.shared, LANES), jnp.float32),
        pltpu.VMEM((pack.rest_rows, LANES), jnp.float32),
    ]


def row_columns(pack, rows):
    parts = [rows[:, c, :].T for c in range(pack.groups)]
    return jnp.concatenate(parts, axis=0)[: pack.width]


def one_hot(mask):
    return mask.astype(jnp.float32).astype(jnp.bfloat16)


def request_kernel(
    pack, rows_here, map_hbm, head_hbm, tail_hbm, negative_hbm,
    request_ref, address_ref, slot_ref, map_ref, ids_ref, sems,
):
    copies = [pltpu.make_async_copy(map_hbm, map_ref, sems.at[0])]
    first = 0
    for index, source in enumerate((head_hbm, tail_hbm, negative_hbm)):
        target = ids_ref.at[:, pl.ds(first, source.shape[1])]
        copies.append(pltpu.make_async_copy(source, target, sems.at[index + 1]))
        first += source.shape[1]
    for copy in copies:
        copy.start()
    for copy in copies[1:]:
        copy.wait()
    ids = ids_ref[...]
    count = ids.shape[1]
    lines = map_ref.shape[0]

    def iota(rows, axis):
        return lax.broadcasted_iota(jnp.int32, (rows, count), axis)

    line_chosen = one_hot(iota(lines, 0) == ids // LANES)
    earlier = one_hot(iota(count, 0) < iota(count, 1))
    copies[0].wait()
    table = map_ref[...].T
    digits = [(table >> shift) & 255 for shift in range(0, 24, 8)]
    stacked = jnp.concatenate(digits, axis=0).astype(jnp.float32).astype(jnp.bfloat16)
    found = jnp.dot(stacked, line_chosen, preferred_element_type=jnp.float32)
    found = found[:LANES] + 256.0 * found[LANES : 2 * LANES] + 65536.0 * found[2 * LANES :]
    found = jnp.where(iota(LANES, 0) == ids % LANES, found, 0.0)
    position = jnp.sum(found, axis=0, keepdims=True).astype(jnp.int32)
    owner = position // rows_here
    row = position % rows_here
    to_owner = iota(pack.owners, 0) == owner
    before = jnp.dot(one_hot(to_owner), earlier, preferred_element_type=jnp.float32)
    rank = jnp.sum(jnp.where(to_owner, before, 0.0), axis=0, keepdims=True).astype(jnp.int32)
    slot_ref[...] = owner * pack.capacity + rank
    address_ref[...] = owner * pack.stride + rank * pack.full
    at_rank = one_hot(iota(pack.capacity, 0) == rank)
    absent = row - rows_here

    def place(values):
        chosen = jnp.where(to_owner, values.astype(jnp.float32), 0.0).astype(jnp.bfloat16)
        return lax.dot_general(
            chosen, at_rank, (((1,), (1,)), ((), ())), preferred_element_type=jnp.float32
        )

    high = -((-absent) // 256)
    low = absent - high * 256
    request_ref[:, 0, :] = (place(high) * 256.0 + place(low)).astype(jnp.int32) + rows_here


def build_requests(pack, rows_here, owner_map, head_ids, tail_ids, neg_ids):
    count = head_ids.shape[0] + tail_ids.shape[0] + neg_ids.shape[0]
    shape = jax.ShapeDtypeStruct
    return pl.pallas_call(
        functools.partial(request_kernel, pack, rows_here),
        out_shape=(
            shape((pack.owners, 1, pack.capacity), jnp.int32),
            shape((1, count), jnp.int32),
            shape((1, count), jnp.int32),
        ),
        in_specs=[hbm()] * 4,
        out_specs=(vmem(),) * 3,
        scratch_shapes=[
            pltpu.VMEM((owner_map.shape[0] // LANES, LANES), jnp.int32),
            pltpu.VMEM((1, count), jnp.int32),
            pltpu.SemaphoreType.DMA((4,)),
        ],
        compiler_params=compiler_params(),
        name="build_requests",
    )(
        in_hbm(owner_map.reshape(-1, LANES)), in_hbm(head_ids.reshape(1, -1)),
        in_hbm(tail_ids.reshape(1, -1)), in_hbm(neg_ids.reshape(1, -1)),
    )


def rows_kernel(pack, columns_ref, rows_ref, line_ref):
    count = columns_ref.shape[1]
    fill = jnp.zeros((pack.wide - pack.width, LANES), jnp.float32)
    place = lax.broadcasted_iota(jnp.int32, (LANES // SUBLANES, LANES), 1) // pack.rest
    for block in range(count // LANES):
        at = slice(block * LANES, (block + 1) * LANES)
        tile = jnp.concatenate([columns_ref[:, at], fill], axis=0)
        for c in range(pack.full):
            rows_ref[pl.ds(block * LANES * pack.full + c, LANES, stride=pack.full), :] = tile[
                c * LANES : (c + 1) * LANES
            ].T
        line_ref[:LANES, :] = tile[pack.full * LANES :].T
        shared = line_ref[pl.ds(0, LANES // SUBLANES, stride=SUBLANES), :]
        for j in range(1, SUBLANES):
            rest = line_ref[pl.ds(j, LANES // SUBLANES, stride=SUBLANES), :]
            shared = jnp.where(place == j, pltpu.roll(rest, j * pack.rest, axis=1), shared)
        first = pack.full * (count + SUBLANES) + block * (LANES // SUBLANES)
        rows_ref[first : first + LANES // SUBLANES, :] = shared
    zeros = jnp.zeros((pack.full * SUBLANES, LANES), jnp.float32)
    rows_ref[pack.full * count : pack.full * (count + SUBLANES), :] = zeros
    rows_ref[pack.full * (count + SUBLANES) + count // SUBLANES :, :] = zeros[:SUBLANES]


def to_rows(pack, columns):
    count = columns.shape[1]
    lines = pack.full * (count + SUBLANES) + count // SUBLANES + SUBLANES
    return pl.pallas_call(
        functools.partial(rows_kernel, pack),
        out_shape=pltpu.VMEM((lines, LANES), jnp.float32),
        in_specs=[vmem()],
        out_specs=vmem(),
        scratch_shapes=[pltpu.VMEM((LANES + SUBLANES, LANES), jnp.float32)],
        compiler_params=compiler_params(),
        name="table_rows",
    )(columns)


def sends(pack, out_ref, out_hbm, sems):
    count = sems.shape[0]
    each = pack.owners // count
    copies = []
    for index in range(count):
        rows = pl.ds(index * each * pack.stride, each * pack.stride)
        copies.append(pltpu.make_async_copy(out_ref.at[rows, :], out_hbm.at[rows, :], sems.at[index]))
    return copies, each


def share_rests(pack, rests_ref, out_ref, first_owner, owners):
    count = owners * pack.shared
    first = first_owner * pack.capacity
    shared = rests_ref[pl.ds(first, count, stride=SUBLANES), :]
    place = lax.broadcasted_iota(jnp.int32, shared.shape, 1) // pack.rest
    for j in range(1, SUBLANES):
        block = rests_ref[pl.ds(first + j, count, stride=SUBLANES), :]
        shared = jnp.where(place == j, pltpu.roll(block, j * pack.rest, axis=1), shared)
    for owner in range(owners):
        start = (first_owner + owner) * pack.stride + pack.rests_at
        out_ref[pl.ds(start, pack.shared), :] = shared[
            owner * pack.shared : (owner + 1) * pack.shared
        ]


def serve_kernel(
    pack, rows_here, asked_ref, table_ref, out_hbm, out_ref, rests_ref, table_rests_ref, sems
):
    copies, each = sends(pack, out_ref, out_hbm, sems)
    shared = table_ref[pack.full * (rows_here + SUBLANES) :, :]
    for j in range(SUBLANES):
        moved = shared if j == 0 else pltpu.roll(shared, LANES - j * pack.rest, axis=1)
        table_rests_ref[pl.ds(j, shared.shape[0], stride=SUBLANES), :] = moved

    def body(owner):
        base = owner * pack.stride
        slots = pl.multiple_of(owner * pack.capacity, SUBLANES)
        for first in range(0, pack.capacity, SUBLANES):
            rows = [asked_ref[owner, 0, first + j] for j in range(SUBLANES)]
            values = [table_ref[pl.ds(row * pack.full, pack.full), :] for row in rows]
            rests = [table_rests_ref[pl.ds(row, 1), :] for row in rows]
            for j in range(SUBLANES):
                out_ref[pl.ds(base + (first + j) * pack.full, pack.full), :] = values[j]
            rests_ref[pl.ds(slots + first, SUBLANES), :] = jnp.concatenate(rests, axis=0)

    for index, copy in enumerate(copies):
        def step(some):
            for owner in range(SERVE_OWNERS):
                body(index * each + some * SERVE_OWNERS + owner)

        loop(each // SERVE_OWNERS, step)
        share_rests(pack, rests_ref, out_ref, index * each, each)
        copy.start()
    for copy in copies:
        copy.wait()


def serve(pack, rows_here, asked, table_rows):
    return pl.pallas_call(
        functools.partial(serve_kernel, pack, rows_here),
        out_shape=pltpu.HBM((pack.rows, LANES), jnp.float32),
        in_specs=[smem(), vmem()],
        out_specs=hbm(),
        scratch_shapes=[
            pltpu.VMEM((pack.rows, LANES), jnp.float32),
            pltpu.VMEM((pack.rest_rows, LANES), jnp.float32),
            pltpu.VMEM((rows_here + SUBLANES * (SUBLANES + 1), LANES), jnp.float32),
            pltpu.SemaphoreType.DMA((4,)),
        ],
        compiler_params=compiler_params(),
        name="serve_rows",
    )(asked, pltpu.with_memory_space_constraint(table_rows, pltpu.VMEM))


def copy_rows(pack, first_request, address_ref, slot_ref, packed_ref, rests_ref, rows_ref):
    def body(group):
        first = group * 2 * SUBLANES
        values = []
        for j in range(2 * SUBLANES):
            request = first_request + first + j
            values.append(
                (
                    packed_ref[pl.ds(address_ref[0, request], pack.full), :],
                    rests_ref[pl.ds(slot_ref[0, request], 1), :],
                )
            )
        for j, (groups, rest) in enumerate(values):
            rows_ref[first + j, : pack.full, :] = groups
            rows_ref[first + j, pack.full :, :] = rest

    loop(rows_ref.shape[0] // (2 * SUBLANES), body)


def heads_kernel(
    pack, address_ref, slot_ref, packed_ref, relation_ref,
    query_ref, shared_ref, rests_ref, rows_ref,
):
    expand_rests(pack, packed_ref, shared_ref, rests_ref)
    copy_rows(pack, 0, address_ref, slot_ref, packed_ref, rests_ref, rows_ref)
    query_ref[...] = row_columns(pack, rows_ref[...]) + relation_ref[...]


def unpack_heads(pack, edges, address, slot, packed, relation_rows):
    return pl.pallas_call(
        functools.partial(heads_kernel, pack),
        out_shape=jax.ShapeDtypeStruct((pack.width, edges), jnp.float32),
        in_specs=[smem(), smem(), vmem(), vmem()],
        out_specs=vmem(),
        scratch_shapes=rests_scratch(pack)
        + [pltpu.VMEM((edges, pack.groups, LANES), jnp.float32)],
        compiler_params=compiler_params(),
        cost_estimate=pl.CostEstimate(flops=10**7, bytes_accessed=3 * 10**6, transcendentals=0),
        name="unpack_heads",
    )(address, slot, packed, relation_rows)


def rest_kernel(
    pack, edges, address_ref, slot_ref, packed_ref, query_ref,
    positive_ref, negative_ref, high_ref, low_ref, high_columns_ref, low_columns_ref, square_ref,
    shared_ref, rests_ref, rows_ref,
):
    expand_rests(pack, packed_ref, shared_ref, rests_ref)
    copy_rows(pack, edges, address_ref, slot_ref, packed_ref, rests_ref, rows_ref)
    for c in range(pack.groups):
        negative_ref[:, c * LANES : (c + 1) * LANES] = rows_ref[edges:, c, :]
    negatives = negative_ref[...]
    high_ref[...], low_ref[...] = split(negatives)
    high_columns_ref[...], low_columns_ref[...] = split(negatives.T[: pack.width])
    square_ref[...] = jnp.sum(negatives * negatives, axis=1, keepdims=True)
    residue = query_ref[...] - row_columns(pack, rows_ref[:edges])
    distance = jnp.sqrt(jnp.sum(residue * residue, axis=0, keepdims=True) + EPSILON)
    positive_ref[...] = jax.nn.sigmoid(distance - MARGIN) / distance * residue


def unpack_rest(pack, negatives, address, slot, packed, queries):
    edges = queries.shape[1]
    shape = jax.ShapeDtypeStruct
    return pl.pallas_call(
        functools.partial(rest_kernel, pack, edges),
        out_shape=(
            shape((pack.width, edges), jnp.float32),
            shape((negatives, pack.wide), jnp.float32),
            shape((negatives, pack.wide), jnp.bfloat16),
            shape((negatives, pack.wide), jnp.bfloat16),
            shape((pack.width, negatives), jnp.bfloat16),
            shape((pack.width, negatives), jnp.bfloat16),
            shape((negatives, 1), jnp.float32),
        ),
        in_specs=[smem(), smem(), vmem(), vmem()],
        out_specs=(vmem(),) * 7,
        scratch_shapes=rests_scratch(pack)
        + [pltpu.VMEM((edges + negatives, pack.groups, LANES), jnp.float32)],
        compiler_params=compiler_params(),
        cost_estimate=pl.CostEstimate(flops=10**7, bytes_accessed=9 * 10**6, transcendentals=0),
        name="unpack_rest",
    )(address, slot, packed, queries)


def gather_queries(pack, query_refs):
    queries = jnp.concatenate([ref[...] for ref in query_refs], axis=1)
    fill = jnp.zeros((pack.wide - pack.width, queries.shape[1]), jnp.float32)
    return jnp.concatenate([queries, fill], axis=0)


def negatives_kernel(pack, blocks, weight, *refs):
    half_refs = refs[:2]
    column_refs = refs[2:4]
    square_ref = refs[4]
    query_refs = refs[5 : 5 + blocks]
    coefficient_ref, *part_refs = refs[5 + blocks :]
    queries = gather_queries(pack, query_refs)
    query_sq = jnp.sum(queries * queries, axis=0, keepdims=True)
    query_halves = split(queries)
    count = square_ref.shape[0]
    weights, parts = [], []
    for first in range(0, count, count // SCORE_STEPS):
        rows = slice(first, first + count // SCORE_STEPS)
        inner = dot_halves([ref[rows, :] for ref in half_refs], query_halves, ((1,), (0,)))
        squared = jnp.maximum(query_sq + square_ref[rows, :] - 2.0 * inner + EPSILON, EPSILON)
        distance = jnp.sqrt(squared)
        coefficient = -1.0 / ((1.0 + jnp.exp(distance - MARGIN)) * (weight * distance))
        coefficient_ref[rows, :] = coefficient
        weights.append(jnp.sum(coefficient, axis=0, keepdims=True))
        parts.append(
            dot_halves([ref[:, rows] for ref in column_refs], split(coefficient), ((1,), (0,)))
        )
    part = queries[: pack.width] * sum(weights) - sum(parts)
    width = query_refs[0].shape[1]
    for index, ref in enumerate(part_refs):
        ref[...] = part[:, index * width : (index + 1) * width]


def negative_terms(pack, weight, negative_parts, queries):
    shape = jax.ShapeDtypeStruct
    count = sum(q.shape[1] for q in queries)
    rows = negative_parts[0].shape[0]
    return pl.pallas_call(
        functools.partial(negatives_kernel, pack, len(queries), weight),
        out_shape=(shape((rows, count), jnp.float32),)
        + tuple(shape(q.shape, jnp.float32) for q in queries),
        in_specs=[vmem()] * (len(negative_parts) + len(queries)),
        out_specs=(vmem(),) * (1 + len(queries)),
        compiler_params=compiler_params(),
        cost_estimate=pl.CostEstimate(
            flops=12 * rows * count * pack.wide, bytes_accessed=4 * 10**6, transcendentals=0
        ),
        name="negative_terms",
    )(*negative_parts, *queries)


def store_rows(pack, first_request, address_ref, slot_ref, rows_ref, out_ref, rests_ref):
    def body(group):
        first = group * 2 * SUBLANES
        values = [rows_ref[first + j] for j in range(2 * SUBLANES)]
        for j, value in enumerate(values):
            request = first_request + first + j
            out_ref[pl.ds(address_ref[0, request], pack.full), :] = value[: pack.full]
            rests_ref[pl.ds(slot_ref[0, request], 1), :] = value[pack.full :]

    loop(rows_ref.shape[0] // (2 * SUBLANES), body)


def store_columns(pack, columns, rows_ref):
    fill = jnp.zeros((pack.wide - pack.width, columns.shape[1]), jnp.float32)
    columns = jnp.concatenate([columns, fill], axis=0)
    for c in range(pack.groups):
        rows_ref[:, c, :] = columns[c * LANES : (c + 1) * LANES].T


def block_kernel(pack, blocks, coefficients, address_ref, slot_ref, *refs):
    positive_ref, negative_ref = refs[:2]
    query_refs = refs[2 : 2 + blocks]
    coefficient_refs = refs[2 + blocks : 2 + blocks + coefficients]
    out_ref, rests_ref, rows_ref = refs[2 + blocks + coefficients :]
    edges = positive_ref.shape[1]
    out_ref[...] = jnp.zeros_like(out_ref)
    rests_ref[...] = jnp.zeros_like(rests_ref)
    store_columns(pack, -positive_ref[...], rows_ref.at[:edges])
    coefficient = jnp.concatenate([ref[...] for ref in coefficient_refs], axis=1)
    block_grad = negative_ref[...] * jnp.sum(coefficient, axis=1, keepdims=True) - dot_halves(
        split(coefficient), split(gather_queries(pack, query_refs)), ((1,), (1,))
    )
    for c in range(pack.groups):
        rows_ref[edges:, c, :] = block_grad[:, c * LANES : (c + 1) * LANES]
    store_rows(pack, edges, address_ref, slot_ref, rows_ref, out_ref, rests_ref)


def block_gradients(pack, address, slot, positive, negatives, queries, coefficients):
    shape = jax.ShapeDtypeStruct
    rows = positive.shape[1] + negatives.shape[0]
    flops = 6 * sum(c.size for c in coefficients) * pack.wide
    return pl.pallas_call(
        functools.partial(block_kernel, pack, len(queries), len(coefficients)),
        out_shape=(
            shape((pack.rows, LANES), jnp.float32),
            shape((pack.rest_rows, LANES), jnp.float32),
        ),
        in_specs=[smem()] * 2 + [vmem()] * (2 + len(queries) + len(coefficients)),
        out_specs=(vmem(), vmem()),
        scratch_shapes=[pltpu.VMEM((rows, pack.groups, LANES), jnp.float32)],
        compiler_params=compiler_params(),
        cost_estimate=pl.CostEstimate(
            flops=flops, bytes_accessed=10**7, transcendentals=0
        ),
        name="block_gradients",
    )(address, slot, positive, negatives, *queries, *coefficients)


def finish_kernel(pack, parts, address_ref, slot_ref, *refs):
    positive_ref = refs[2]
    part_refs = refs[3 : 3 + parts]
    out_hbm, out_ref, rests_ref, rows_ref, sems = refs[3 + parts :]
    copies, each = sends(pack, out_ref, out_hbm, sems)
    total = positive_ref[...]
    for ref in part_refs:
        total = total + ref[...]
    store_columns(pack, total, rows_ref)
    store_rows(pack, 0, address_ref, slot_ref, rows_ref, out_ref, rests_ref)
    for index, copy in enumerate(copies):
        share_rests(pack, rests_ref, out_ref, index * each, each)
        copy.start()
    for copy in copies:
        copy.wait()


def finish_gradients(pack, address, slot, partial, partial_rests, positive, parts):
    edges = positive.shape[1]
    shape = jax.ShapeDtypeStruct
    return pl.pallas_call(
        functools.partial(finish_kernel, pack, len(parts)),
        out_shape=(
            pltpu.HBM((pack.rows, LANES), jnp.float32),
            shape(partial.shape, jnp.float32),
            shape(partial_rests.shape, jnp.float32),
        ),
        in_specs=[smem()] * 2 + [vmem()] * (3 + len(parts)),
        out_specs=(hbm(), vmem(), vmem()),
        input_output_aliases={2: 1, 3: 2},
        scratch_shapes=[
            pltpu.VMEM((edges, pack.groups, LANES), jnp.float32),
            pltpu.SemaphoreType.DMA((4,)),
        ],
        compiler_params=compiler_params(),
        name="finish_gradients",
    )(address, slot, partial, partial_rests, positive, *parts)[0]


def update_kernel(
    pack, columns, asked_ref, packed_hbm, sum_ref, table_ref, new_table_hbm, new_sum_ref,
    packed_ref, shared_ref, rests_ref, rows_ref, halves_ref, out_ref, sems, packed_sems,
):
    pieces = packed_sems.shape[0]
    owners = pack.owners // pieces
    loads = []
    for index in range(pieces):
        at = pl.ds(index * owners * pack.stride, owners * pack.stride)
        loads.append(
            pltpu.make_async_copy(packed_hbm.at[at, :], packed_ref.at[at, :], packed_sems.at[index])
        )
        loads[-1].start()
    width = pack.width
    for index, load in enumerate(loads):
        load.wait()
        expand_rests(pack, packed_ref, shared_ref, rests_ref, index * owners, owners)
        for owner in range(index * owners, (index + 1) * owners):
            rows = slice(owner * pack.capacity, (owner + 1) * pack.capacity)
            for c in range(pack.full):
                rows_ref[rows, c * LANES : (c + 1) * LANES] = packed_ref[
                    pl.ds(owner * pack.stride + c, pack.capacity, stride=pack.full), :
                ]
            rows_ref[rows, pack.full * LANES :] = rests_ref[rows, :]
        slots = slice(index * owners * pack.capacity, (index + 1) * owners * pack.capacity)
        high, low = split(rows_ref[slots, :].T)
        halves_ref[:width, slots] = high[:width]
        halves_ref[width:, slots] = low[:width]
    asked = asked_ref[...]
    row = lax.broadcasted_iota(jnp.int32, (columns, pack.slots), 0)
    copies = []
    for index in range(table_ref.shape[1] // columns):
        at = slice(index * columns, (index + 1) * columns)
        chosen = one_hot(row == asked - index * columns)
        both = lax.dot_general(
            halves_ref[...], chosen, (((1,), (1,)), ((), ())), preferred_element_type=jnp.float32
        )
        summed = both[:width] + both[width:]
        new_sum = sum_ref[:, at] + jnp.sum(summed * summed, axis=0, keepdims=True) / width
        new_sum_ref[:, at] = new_sum
        out_ref[:, at] = table_ref[:, at] - summed * (LEARNING_RATE / jnp.sqrt(new_sum))
        copies.append(
            pltpu.make_async_copy(out_ref.at[:, at], new_table_hbm.at[:, at], sems.at[index])
        )
        copies[-1].start()
    for copy in copies:
        copy.wait()


def update(pack, asked, packed, adagrad_sum, table_columns):
    width, rows = table_columns.shape
    columns = 256
    shape = jax.ShapeDtypeStruct
    return pl.pallas_call(
        functools.partial(update_kernel, pack, columns),
        out_shape=(pltpu.HBM((width, rows), jnp.float32), shape((1, rows), jnp.float32)),
        in_specs=[vmem(), hbm(), vmem(), vmem()],
        out_specs=(hbm(), vmem()),
        scratch_shapes=[pltpu.VMEM((pack.rows, LANES), jnp.float32)]
        + rests_scratch(pack)
        + [
            pltpu.VMEM((pack.slots, pack.wide), jnp.float32),
            pltpu.VMEM((2 * width, pack.slots), jnp.bfloat16),
            pltpu.VMEM((width, rows), jnp.float32),
            pltpu.SemaphoreType.DMA((rows // columns,)),
            pltpu.SemaphoreType.DMA((2,)),
        ],
        compiler_params=compiler_params(),
        name="update_table",
    )(asked, in_hbm(packed), adagrad_sum, table_columns)


def exchange(payload):
    return lax.all_to_all(payload, ("dp", "blk"), split_axis=0, concat_axis=0, tiled=True)


def to_sibling(value, blk_count):
    return lax.ppermute(value, "blk", [(i, i ^ 1) for i in range(blk_count)])


def to_chip(value, blk_count, hops):
    return lax.ppermute(
        value, "blk", [(i, (i + 2 * hops) % blk_count) for i in range(blk_count)]
    )


def on_device(
    entity_table, adagrad_sum, relations, owner_map, head_ids, rel_ids, tail_ids, neg_ids
):
    dp_count = lax.axis_size("dp")
    blk_count = lax.axis_size("blk")
    owner_count = dp_count * blk_count
    chip_count = blk_count // 2
    rows_here, width = entity_table.shape
    edge_count = head_ids.shape[0]
    neg_count = neg_ids.shape[0]
    request_count = 2 * edge_count + neg_count
    capacity = -(-2 * request_count // owner_count // SUBLANES) * SUBLANES
    pack = Packing(width, owner_count, capacity)
    requests, address, slot_of = build_requests(
        pack, rows_here, owner_map, head_ids, tail_ids, neg_ids
    )
    asked = exchange(requests)
    served = serve(pack, rows_here, asked, to_rows(pack, entity_table.T))
    fetched = exchange(served.reshape(owner_count, 1, pack.stride * LANES))
    fetched = fetched.reshape(pack.rows, LANES)
    queries = unpack_heads(pack, edge_count, address, slot_of, fetched, relations[rel_ids].T)
    weight = float(blk_count * neg_count)
    arriving = [to_chip(queries, blk_count, hops) for hops in range(1, chip_count)]
    nearby = [queries, to_sibling(queries, blk_count)]
    positive, negatives, *negative_parts = unpack_rest(pack, neg_count, address, slot_of, fetched, queries)
    near, *near_parts = negative_terms(pack, weight, negative_parts, nearby)
    arriving, near, near_parts = lax.optimization_barrier((arriving, near, near_parts))
    distant = []
    for same in arriving:
        distant += [same, to_sibling(same, blk_count)]
    far, *far_parts = negative_terms(pack, weight, negative_parts, distant)
    totals = [near_parts[0], to_sibling(near_parts[1], blk_count)]
    for hops in range(1, chip_count):
        total = far_parts[2 * hops - 2] + to_sibling(far_parts[2 * hops - 1], blk_count)
        totals.append(to_chip(total, blk_count, chip_count - hops))
    partial, partial_rests = block_gradients(
        pack, address, slot_of, positive, negatives, nearby + distant, (near, far)
    )
    outgoing = finish_gradients(
        pack, address, slot_of, partial, partial_rests, positive, totals
    )
    incoming = exchange(outgoing.reshape(owner_count, 1, pack.stride * LANES))
    new_columns, new_sum = update(
        pack, asked.reshape(1, -1), incoming.reshape(pack.rows, LANES),
        adagrad_sum.reshape(1, -1), entity_table.T,
    )
    return (new_columns.T, new_sum.reshape(-1))


def solution(mesh):
    return jax.shard_map(
        on_device,
        mesh=mesh,
        in_specs=(
            P(("dp", "blk"), None),
            P(("dp", "blk")),
            P(),
            P(),
            P(("dp", "blk")),
            P(("dp", "blk")),
            P(("dp", "blk")),
            P(("dp", "blk")),
        ),
        out_specs=(P(("dp", "blk"), None), P(("dp", "blk"))),
        check_vma=False,
    )
```

```python
import functools

import jax
import jax.numpy as jnp
from jax import lax
from jax.experimental import pallas as pl
from jax.experimental.pallas import tpu as pltpu
from jax.sharding import PartitionSpec as P

MARGIN = 10.0
EPSILON = 1e-05
LEARNING_RATE = 0.1
LANES = 128
SUBLANES = 8
SCORE_STEPS = 2
SERVE_OWNERS = 4
VMEM_BYTES = 24 * 1024 * 1024


class Packing:
    def __init__(self, width, owners, capacity):
        self.width = width
        self.owners = owners
        self.capacity = capacity
        self.full = width // LANES
        self.rest = width - self.full * LANES
        assert 0 < self.rest <= LANES // SUBLANES and capacity % SUBLANES == 0
        self.shared = capacity // SUBLANES
        self.groups = self.full + 1
        self.wide = self.groups * LANES
        self.rests_at = self.full * capacity
        self.stride = self.rests_at + self.shared
        self.slots = owners * capacity
        self.rest_rows = self.slots + SUBLANES
        self.rows = owners * self.stride


def compiler_params():
    return pltpu.CompilerParams(vmem_limit_bytes=VMEM_BYTES)


def vmem():
    return pl.BlockSpec(memory_space=pltpu.VMEM)


def smem():
    return pl.BlockSpec(memory_space=pltpu.SMEM)


def hbm():
    return pl.BlockSpec(memory_space=pltpu.HBM)


def in_hbm(value):
    return pltpu.with_memory_space_constraint(value, pltpu.HBM)


def split(value):
    high = value.astype(jnp.bfloat16)
    low = (value - high.astype(jnp.float32)).astype(jnp.bfloat16)
    return high, low


def dot_halves(left, right, contract):
    numbers = (contract, ((), ()))

    def dot(a, b):
        return lax.dot_general(a, b, numbers, preferred_element_type=jnp.float32)

    return dot(left[0], right[0]) + (dot(left[0], right[1]) + dot(left[1], right[0]))


def loop(count, body):
    def step(index, carry):
        body(index)
        return carry

    lax.fori_loop(0, count, step, 0)


def expand_rests(pack, packed_ref, shared_ref, rests_ref, first_owner=0, owners=None):
    owners = pack.owners if owners is None else owners
    for owner in range(first_owner, first_owner + owners):
        shared_ref[owner * pack.shared : (owner + 1) * pack.shared, :] = packed_ref[
            pl.ds(owner * pack.stride + pack.rests_at, pack.shared), :
        ]
    first = first_owner * pack.shared
    shared = shared_ref[first : first + owners * pack.shared, :]
    lane = lax.broadcasted_iota(jnp.int32, shared.shape, 1)
    for j in range(SUBLANES):
        moved = shared if j == 0 else pltpu.roll(shared, LANES - j * pack.rest, axis=1)
        rows = pl.ds(first * SUBLANES + j, shared.shape[0], stride=SUBLANES)
        rests_ref[rows, :] = jnp.where(lane < pack.rest, moved, 0.0)


def rests_scratch(pack):
    return [
        pltpu.VMEM((pack.owners * pack.shared, LANES), jnp.float32),
        pltpu.VMEM((pack.rest_rows, LANES), jnp.float32),
    ]


def row_columns(pack, rows):
    parts = [rows[:, c, :].T for c in range(pack.groups)]
    return jnp.concatenate(parts, axis=0)[: pack.width]


def one_hot(mask):
    return mask.astype(jnp.float32).astype(jnp.bfloat16)


def request_kernel(
    pack, rows_here, map_hbm, head_hbm, tail_hbm, negative_hbm,
    request_ref, address_ref, slot_ref, map_ref, ids_ref, sems,
):
    copies = [pltpu.make_async_copy(map_hbm, map_ref, sems.at[0])]
    first = 0
    for index, source in enumerate((head_hbm, tail_hbm, negative_hbm)):
        target = ids_ref.at[:, pl.ds(first, source.shape[1])]
        copies.append(pltpu.make_async_copy(source, target, sems.at[index + 1]))
        first += source.shape[1]
    for copy in copies:
        copy.start()
    for copy in copies[1:]:
        copy.wait()
    ids = ids_ref[...]
    count = ids.shape[1]
    lines = map_ref.shape[0]

    def iota(rows, axis):
        return lax.broadcasted_iota(jnp.int32, (rows, count), axis)

    line_chosen = one_hot(iota(lines, 0) == ids // LANES)
    earlier = one_hot(iota(count, 0) < iota(count, 1))
    copies[0].wait()
    table = map_ref[...].T
    digits = [(table >> shift) & 255 for shift in range(0, 24, 8)]
    stacked = jnp.concatenate(digits, axis=0).astype(jnp.float32).astype(jnp.bfloat16)
    found = jnp.dot(stacked, line_chosen, preferred_element_type=jnp.float32)
    found = found[:LANES] + 256.0 * found[LANES : 2 * LANES] + 65536.0 * found[2 * LANES :]
    found = jnp.where(iota(LANES, 0) == ids % LANES, found, 0.0)
    position = jnp.sum(found, axis=0, keepdims=True).astype(jnp.int32)
    owner = position // rows_here
    row = position % rows_here
    to_owner = iota(pack.owners, 0) == owner
    before = jnp.dot(one_hot(to_owner), earlier, preferred_element_type=jnp.float32)
    rank = jnp.sum(jnp.where(to_owner, before, 0.0), axis=0, keepdims=True).astype(jnp.int32)
    slot_ref[...] = owner * pack.capacity + rank
    address_ref[...] = owner * pack.stride + rank * pack.full
    at_rank = one_hot(iota(pack.capacity, 0) == rank)
    absent = row - rows_here

    def place(values):
        chosen = jnp.where(to_owner, values.astype(jnp.float32), 0.0).astype(jnp.bfloat16)
        return lax.dot_general(
            chosen, at_rank, (((1,), (1,)), ((), ())), preferred_element_type=jnp.float32
        )

    high = -((-absent) // 256)
    low = absent - high * 256
    request_ref[:, 0, :] = (place(high) * 256.0 + place(low)).astype(jnp.int32) + rows_here


def build_requests(pack, rows_here, owner_map, head_ids, tail_ids, neg_ids):
    count = head_ids.shape[0] + tail_ids.shape[0] + neg_ids.shape[0]
    shape = jax.ShapeDtypeStruct
    return pl.pallas_call(
        functools.partial(request_kernel, pack, rows_here),
        out_shape=(
            shape((pack.owners, 1, pack.capacity), jnp.int32),
            shape((1, count), jnp.int32),
            shape((1, count), jnp.int32),
        ),
        in_specs=[hbm()] * 4,
        out_specs=(vmem(),) * 3,
        scratch_shapes=[
            pltpu.VMEM((owner_map.shape[0] // LANES, LANES), jnp.int32),
            pltpu.VMEM((1, count), jnp.int32),
            pltpu.SemaphoreType.DMA((4,)),
        ],
        compiler_params=compiler_params(),
        name="build_requests",
    )(
        in_hbm(owner_map.reshape(-1, LANES)), in_hbm(head_ids.reshape(1, -1)),
        in_hbm(tail_ids.reshape(1, -1)), in_hbm(neg_ids.reshape(1, -1)),
    )


def rows_kernel(pack, columns_ref, rows_ref, line_ref):
    count = columns_ref.shape[1]
    fill = jnp.zeros((pack.wide - pack.width, LANES), jnp.float32)
    place = lax.broadcasted_iota(jnp.int32, (LANES // SUBLANES, LANES), 1) // pack.rest
    for block in range(count // LANES):
        at = slice(block * LANES, (block + 1) * LANES)
        tile = jnp.concatenate([columns_ref[:, at], fill], axis=0)
        for c in range(pack.full):
            rows_ref[pl.ds(block * LANES * pack.full + c, LANES, stride=pack.full), :] = tile[
                c * LANES : (c + 1) * LANES
            ].T
        line_ref[:LANES, :] = tile[pack.full * LANES :].T
        shared = line_ref[pl.ds(0, LANES // SUBLANES, stride=SUBLANES), :]
        for j in range(1, SUBLANES):
            rest = line_ref[pl.ds(j, LANES // SUBLANES, stride=SUBLANES), :]
            shared = jnp.where(place == j, pltpu.roll(rest, j * pack.rest, axis=1), shared)
        first = pack.full * (count + SUBLANES) + block * (LANES // SUBLANES)
        rows_ref[first : first + LANES // SUBLANES, :] = shared
    zeros = jnp.zeros((pack.full * SUBLANES, LANES), jnp.float32)
    rows_ref[pack.full * count : pack.full * (count + SUBLANES), :] = zeros
    rows_ref[pack.full * (count + SUBLANES) + count // SUBLANES :, :] = zeros[:SUBLANES]


def to_rows(pack, columns):
    count = columns.shape[1]
    lines = pack.full * (count + SUBLANES) + count // SUBLANES + SUBLANES
    return pl.pallas_call(
        functools.partial(rows_kernel, pack),
        out_shape=pltpu.VMEM((lines, LANES), jnp.float32),
        in_specs=[vmem()],
        out_specs=vmem(),
        scratch_shapes=[pltpu.VMEM((LANES + SUBLANES, LANES), jnp.float32)],
        compiler_params=compiler_params(),
        name="table_rows",
    )(columns)


def sends(pack, out_ref, out_hbm, sems):
    count = sems.shape[0]
    each = pack.owners // count
    copies = []
    for index in range(count):
        rows = pl.ds(index * each * pack.stride, each * pack.stride)
        copies.append(pltpu.make_async_copy(out_ref.at[rows, :], out_hbm.at[rows, :], sems.at[index]))
    return copies, each


def share_rests(pack, rests_ref, out_ref, first_owner, owners):
    count = owners * pack.shared
    first = first_owner * pack.capacity
    shared = rests_ref[pl.ds(first, count, stride=SUBLANES), :]
    place = lax.broadcasted_iota(jnp.int32, shared.shape, 1) // pack.rest
    for j in range(1, SUBLANES):
        block = rests_ref[pl.ds(first + j, count, stride=SUBLANES), :]
        shared = jnp.where(place == j, pltpu.roll(block, j * pack.rest, axis=1), shared)
    for owner in range(owners):
        start = (first_owner + owner) * pack.stride + pack.rests_at
        out_ref[pl.ds(start, pack.shared), :] = shared[
            owner * pack.shared : (owner + 1) * pack.shared
        ]


def serve_kernel(
    pack, rows_here, asked_ref, table_ref, out_hbm, out_ref, rests_ref, table_rests_ref, sems
):
    copies, each = sends(pack, out_ref, out_hbm, sems)
    shared = table_ref[pack.full * (rows_here + SUBLANES) :, :]
    for j in range(SUBLANES):
        moved = shared if j == 0 else pltpu.roll(shared, LANES - j * pack.rest, axis=1)
        table_rests_ref[pl.ds(j, shared.shape[0], stride=SUBLANES), :] = moved

    def body(owner):
        base = owner * pack.stride
        slots = pl.multiple_of(owner * pack.capacity, SUBLANES)
        for first in range(0, pack.capacity, SUBLANES):
            rows = [asked_ref[owner, 0, first + j] for j in range(SUBLANES)]
            values = [table_ref[pl.ds(row * pack.full, pack.full), :] for row in rows]
            rests = [table_rests_ref[pl.ds(row, 1), :] for row in rows]
            for j in range(SUBLANES):
                out_ref[pl.ds(base + (first + j) * pack.full, pack.full), :] = values[j]
            rests_ref[pl.ds(slots + first, SUBLANES), :] = jnp.concatenate(rests, axis=0)

    for index, copy in enumerate(copies):
        def step(some):
            for owner in range(SERVE_OWNERS):
                body(index * each + some * SERVE_OWNERS + owner)

        loop(each // SERVE_OWNERS, step)
        share_rests(pack, rests_ref, out_ref, index * each, each)
        copy.start()
    for copy in copies:
        copy.wait()


def serve(pack, rows_here, asked, table_rows):
    return pl.pallas_call(
        functools.partial(serve_kernel, pack, rows_here),
        out_shape=pltpu.HBM((pack.rows, LANES), jnp.float32),
        in_specs=[smem(), vmem()],
        out_specs=hbm(),
        scratch_shapes=[
            pltpu.VMEM((pack.rows, LANES), jnp.float32),
            pltpu.VMEM((pack.rest_rows, LANES), jnp.float32),
            pltpu.VMEM((rows_here + SUBLANES * (SUBLANES + 1), LANES), jnp.float32),
            pltpu.SemaphoreType.DMA((4,)),
        ],
        compiler_params=compiler_params(),
        name="serve_rows",
    )(asked, pltpu.with_memory_space_constraint(table_rows, pltpu.VMEM))


def copy_rows(pack, first_request, address_ref, slot_ref, packed_ref, rests_ref, rows_ref):
    def body(group):
        first = group * 2 * SUBLANES
        values = []
        for j in range(2 * SUBLANES):
            request = first_request + first + j
            values.append(
                (
                    packed_ref[pl.ds(address_ref[request], pack.full), :],
                    rests_ref[pl.ds(slot_ref[request], 1), :],
                )
            )
        for j, (groups, rest) in enumerate(values):
            rows_ref[first + j, : pack.full, :] = groups
            rows_ref[first + j, pack.full :, :] = rest

    loop(rows_ref.shape[0] // (2 * SUBLANES), body)


def heads_kernel(
    pack, address_ref, slot_ref, packed_ref, relation_ref,
    query_ref, shared_ref, rests_ref, rows_ref,
):
    expand_rests(pack, packed_ref, shared_ref, rests_ref)
    copy_rows(pack, 0, address_ref, slot_ref, packed_ref, rests_ref, rows_ref)
    query_ref[...] = row_columns(pack, rows_ref[...]) + relation_ref[...]


def unpack_heads(pack, edges, address, slot, packed, relation_rows):
    return pl.pallas_call(
        functools.partial(heads_kernel, pack),
        out_shape=jax.ShapeDtypeStruct((pack.width, edges), jnp.float32),
        in_specs=[smem(), smem(), vmem(), vmem()],
        out_specs=vmem(),
        scratch_shapes=rests_scratch(pack)
        + [pltpu.VMEM((edges, pack.groups, LANES), jnp.float32)],
        compiler_params=compiler_params(),
        cost_estimate=pl.CostEstimate(flops=10**7, bytes_accessed=3 * 10**6, transcendentals=0),
        name="unpack_heads",
    )(address, slot, packed, relation_rows)


def rest_kernel(
    pack, edges, address_ref, slot_ref, packed_ref, query_ref,
    positive_ref, negative_ref, high_ref, low_ref, high_columns_ref, low_columns_ref, square_ref,
    shared_ref, rests_ref, rows_ref,
):
    expand_rests(pack, packed_ref, shared_ref, rests_ref)
    copy_rows(pack, edges, address_ref, slot_ref, packed_ref, rests_ref, rows_ref)
    for c in range(pack.groups):
        negative_ref[:, c * LANES : (c + 1) * LANES] = rows_ref[edges:, c, :]
    negatives = negative_ref[...]
    high_ref[...], low_ref[...] = split(negatives)
    high_columns_ref[...], low_columns_ref[...] = split(negatives.T[: pack.width])
    square_ref[...] = jnp.sum(negatives * negatives, axis=1, keepdims=True)
    residue = query_ref[...] - row_columns(pack, rows_ref[:edges])
    distance = jnp.sqrt(jnp.sum(residue * residue, axis=0, keepdims=True) + EPSILON)
    positive_ref[...] = jax.nn.sigmoid(distance - MARGIN) / distance * residue


def unpack_rest(pack, negatives, address, slot, packed, queries):
    edges = queries.shape[1]
    shape = jax.ShapeDtypeStruct
    return pl.pallas_call(
        functools.partial(rest_kernel, pack, edges),
        out_shape=(
            shape((pack.width, edges), jnp.float32),
            shape((negatives, pack.wide), jnp.float32),
            shape((negatives, pack.wide), jnp.bfloat16),
            shape((negatives, pack.wide), jnp.bfloat16),
            shape((pack.width, negatives), jnp.bfloat16),
            shape((pack.width, negatives), jnp.bfloat16),
            shape((negatives, 1), jnp.float32),
        ),
        in_specs=[smem(), smem(), vmem(), vmem()],
        out_specs=(vmem(),) * 7,
        scratch_shapes=rests_scratch(pack)
        + [pltpu.VMEM((edges + negatives, pack.groups, LANES), jnp.float32)],
        compiler_params=compiler_params(),
        cost_estimate=pl.CostEstimate(flops=10**7, bytes_accessed=9 * 10**6, transcendentals=0),
        name="unpack_rest",
    )(address, slot, packed, queries)


def gather_queries(pack, query_refs):
    queries = jnp.concatenate([ref[...] for ref in query_refs], axis=1)
    fill = jnp.zeros((pack.wide - pack.width, queries.shape[1]), jnp.float32)
    return jnp.concatenate([queries, fill], axis=0)


def negatives_kernel(pack, blocks, weight, *refs):
    half_refs = refs[:2]
    column_refs = refs[2:4]
    square_ref = refs[4]
    query_refs = refs[5 : 5 + blocks]
    coefficient_ref, *part_refs = refs[5 + blocks :]
    queries = gather_queries(pack, query_refs)
    query_sq = jnp.sum(queries * queries, axis=0, keepdims=True)
    query_halves = split(queries)
    count = square_ref.shape[0]
    weights, parts = [], []
    for first in range(0, count, count // SCORE_STEPS):
        rows = slice(first, first + count // SCORE_STEPS)
        inner = dot_halves([ref[rows, :] for ref in half_refs], query_halves, ((1,), (0,)))
        squared = jnp.maximum(query_sq + square_ref[rows, :] - 2.0 * inner + EPSILON, EPSILON)
        distance = jnp.sqrt(squared)
        coefficient = -1.0 / ((1.0 + jnp.exp(distance - MARGIN)) * (weight * distance))
        coefficient_ref[rows, :] = coefficient
        weights.append(jnp.sum(coefficient, axis=0, keepdims=True))
        parts.append(
            dot_halves([ref[:, rows] for ref in column_refs], split(coefficient), ((1,), (0,)))
        )
    part = queries[: pack.width] * sum(weights) - sum(parts)
    width = query_refs[0].shape[1]
    for index, ref in enumerate(part_refs):
        ref[...] = part[:, index * width : (index + 1) * width]


def negative_terms(pack, weight, negative_parts, queries):
    shape = jax.ShapeDtypeStruct
    count = sum(q.shape[1] for q in queries)
    rows = negative_parts[0].shape[0]
    return pl.pallas_call(
        functools.partial(negatives_kernel, pack, len(queries), weight),
        out_shape=(shape((rows, count), jnp.float32),)
        + tuple(shape(q.shape, jnp.float32) for q in queries),
        in_specs=[vmem()] * (len(negative_parts) + len(queries)),
        out_specs=(vmem(),) * (1 + len(queries)),
        compiler_params=compiler_params(),
        cost_estimate=pl.CostEstimate(
            flops=12 * rows * count * pack.wide, bytes_accessed=4 * 10**6, transcendentals=0
        ),
        name="negative_terms",
    )(*negative_parts, *queries)


def store_rows(pack, first_request, address_ref, slot_ref, rows_ref, out_ref, rests_ref):
    def body(group):
        first = group * 2 * SUBLANES
        values = [rows_ref[first + j] for j in range(2 * SUBLANES)]
        for j, value in enumerate(values):
            request = first_request + first + j
            out_ref[pl.ds(address_ref[request], pack.full), :] = value[: pack.full]
            rests_ref[pl.ds(slot_ref[request], 1), :] = value[pack.full :]

    loop(rows_ref.shape[0] // (2 * SUBLANES), body)


def store_columns(pack, columns, rows_ref):
    fill = jnp.zeros((pack.wide - pack.width, columns.shape[1]), jnp.float32)
    columns = jnp.concatenate([columns, fill], axis=0)
    for c in range(pack.groups):
        rows_ref[:, c, :] = columns[c * LANES : (c + 1) * LANES].T


def block_kernel(pack, blocks, coefficients, address_ref, slot_ref, *refs):
    positive_ref, negative_ref = refs[:2]
    query_refs = refs[2 : 2 + blocks]
    coefficient_refs = refs[2 + blocks : 2 + blocks + coefficients]
    out_ref, rests_ref, rows_ref = refs[2 + blocks + coefficients :]
    edges = positive_ref.shape[1]
    out_ref[...] = jnp.zeros_like(out_ref)
    rests_ref[...] = jnp.zeros_like(rests_ref)
    store_columns(pack, -positive_ref[...], rows_ref.at[:edges])
    coefficient = jnp.concatenate([ref[...] for ref in coefficient_refs], axis=1)
    block_grad = negative_ref[...] * jnp.sum(coefficient, axis=1, keepdims=True) - dot_halves(
        split(coefficient), split(gather_queries(pack, query_refs)), ((1,), (1,))
    )
    for c in range(pack.groups):
        rows_ref[edges:, c, :] = block_grad[:, c * LANES : (c + 1) * LANES]
    store_rows(pack, edges, address_ref, slot_ref, rows_ref, out_ref, rests_ref)


def block_gradients(pack, address, slot, positive, negatives, queries, coefficients):
    shape = jax.ShapeDtypeStruct
    rows = positive.shape[1] + negatives.shape[0]
    flops = 6 * sum(c.size for c in coefficients) * pack.wide
    return pl.pallas_call(
        functools.partial(block_kernel, pack, len(queries), len(coefficients)),
        out_shape=(
            shape((pack.rows, LANES), jnp.float32),
            shape((pack.rest_rows, LANES), jnp.float32),
        ),
        in_specs=[smem()] * 2 + [vmem()] * (2 + len(queries) + len(coefficients)),
        out_specs=(vmem(), vmem()),
        scratch_shapes=[pltpu.VMEM((rows, pack.groups, LANES), jnp.float32)],
        compiler_params=compiler_params(),
        cost_estimate=pl.CostEstimate(
            flops=flops, bytes_accessed=10**7, transcendentals=0
        ),
        name="block_gradients",
    )(address, slot, positive, negatives, *queries, *coefficients)


def finish_kernel(pack, parts, address_ref, slot_ref, *refs):
    positive_ref = refs[2]
    part_refs = refs[3 : 3 + parts]
    out_hbm, out_ref, rests_ref, rows_ref, sems = refs[3 + parts :]
    copies, each = sends(pack, out_ref, out_hbm, sems)
    total = positive_ref[...]
    for ref in part_refs:
        total = total + ref[...]
    store_columns(pack, total, rows_ref)
    store_rows(pack, 0, address_ref, slot_ref, rows_ref, out_ref, rests_ref)
    for index, copy in enumerate(copies):
        share_rests(pack, rests_ref, out_ref, index * each, each)
        copy.start()
    for copy in copies:
        copy.wait()


def finish_gradients(pack, address, slot, partial, partial_rests, positive, parts):
    edges = positive.shape[1]
    shape = jax.ShapeDtypeStruct
    return pl.pallas_call(
        functools.partial(finish_kernel, pack, len(parts)),
        out_shape=(
            pltpu.HBM((pack.rows, LANES), jnp.float32),
            shape(partial.shape, jnp.float32),
            shape(partial_rests.shape, jnp.float32),
        ),
        in_specs=[smem()] * 2 + [vmem()] * (3 + len(parts)),
        out_specs=(hbm(), vmem(), vmem()),
        input_output_aliases={2: 1, 3: 2},
        scratch_shapes=[
            pltpu.VMEM((edges, pack.groups, LANES), jnp.float32),
            pltpu.SemaphoreType.DMA((4,)),
        ],
        compiler_params=compiler_params(),
        name="finish_gradients",
    )(address, slot, partial, partial_rests, positive, *parts)[0]


def update_kernel(
    pack, columns, asked_ref, packed_hbm, sum_ref, table_ref, new_table_hbm, new_sum_ref,
    packed_ref, shared_ref, rests_ref, rows_ref, halves_ref, out_ref, sems, packed_sems,
):
    pieces = packed_sems.shape[0]
    owners = pack.owners // pieces
    loads = []
    for index in range(pieces):
        at = pl.ds(index * owners * pack.stride, owners * pack.stride)
        loads.append(
            pltpu.make_async_copy(packed_hbm.at[at, :], packed_ref.at[at, :], packed_sems.at[index])
        )
        loads[-1].start()
    width = pack.width
    for index, load in enumerate(loads):
        load.wait()
        expand_rests(pack, packed_ref, shared_ref, rests_ref, index * owners, owners)
        for owner in range(index * owners, (index + 1) * owners):
            rows = slice(owner * pack.capacity, (owner + 1) * pack.capacity)
            for c in range(pack.full):
                rows_ref[rows, c * LANES : (c + 1) * LANES] = packed_ref[
                    pl.ds(owner * pack.stride + c, pack.capacity, stride=pack.full), :
                ]
            rows_ref[rows, pack.full * LANES :] = rests_ref[rows, :]
        slots = slice(index * owners * pack.capacity, (index + 1) * owners * pack.capacity)
        high, low = split(rows_ref[slots, :].T)
        halves_ref[:width, slots] = high[:width]
        halves_ref[width:, slots] = low[:width]
    asked = asked_ref[...]
    row = lax.broadcasted_iota(jnp.int32, (columns, pack.slots), 0)
    copies = []
    for index in range(table_ref.shape[1] // columns):
        at = slice(index * columns, (index + 1) * columns)
        chosen = one_hot(row == asked - index * columns)
        both = lax.dot_general(
            halves_ref[...], chosen, (((1,), (1,)), ((), ())), preferred_element_type=jnp.float32
        )
        summed = both[:width] + both[width:]
        new_sum = sum_ref[:, at] + jnp.sum(summed * summed, axis=0, keepdims=True) / width
        new_sum_ref[:, at] = new_sum
        out_ref[:, at] = table_ref[:, at] - summed * (LEARNING_RATE / jnp.sqrt(new_sum))
        copies.append(
            pltpu.make_async_copy(out_ref.at[:, at], new_table_hbm.at[:, at], sems.at[index])
        )
        copies[-1].start()
    for copy in copies:
        copy.wait()


def update(pack, asked, packed, adagrad_sum, table_columns):
    width, rows = table_columns.shape
    columns = 256
    shape = jax.ShapeDtypeStruct
    return pl.pallas_call(
        functools.partial(update_kernel, pack, columns),
        out_shape=(pltpu.HBM((width, rows), jnp.float32), shape((1, rows), jnp.float32)),
        in_specs=[vmem(), hbm(), vmem(), vmem()],
        out_specs=(hbm(), vmem()),
        scratch_shapes=[pltpu.VMEM((pack.rows, LANES), jnp.float32)]
        + rests_scratch(pack)
        + [
            pltpu.VMEM((pack.slots, pack.wide), jnp.float32),
            pltpu.VMEM((2 * width, pack.slots), jnp.bfloat16),
            pltpu.VMEM((width, rows), jnp.float32),
            pltpu.SemaphoreType.DMA((rows // columns,)),
            pltpu.SemaphoreType.DMA((2,)),
        ],
        compiler_params=compiler_params(),
        name="update_table",
    )(asked, in_hbm(packed), adagrad_sum, table_columns)


def exchange(payload):
    return lax.all_to_all(payload, ("dp", "blk"), split_axis=0, concat_axis=0, tiled=True)


def to_sibling(value, blk_count):
    return lax.ppermute(value, "blk", [(i, i ^ 1) for i in range(blk_count)])


def to_chip(value, blk_count, hops):
    return lax.ppermute(
        value, "blk", [(i, (i + 2 * hops) % blk_count) for i in range(blk_count)]
    )


def on_device(
    entity_table, adagrad_sum, relations, owner_map, head_ids, rel_ids, tail_ids, neg_ids
):
    dp_count = lax.axis_size("dp")
    blk_count = lax.axis_size("blk")
    owner_count = dp_count * blk_count
    chip_count = blk_count // 2
    rows_here, width = entity_table.shape
    edge_count = head_ids.shape[0]
    neg_count = neg_ids.shape[0]
    request_count = 2 * edge_count + neg_count
    capacity = -(-2 * request_count // owner_count // SUBLANES) * SUBLANES
    pack = Packing(width, owner_count, capacity)
    requests, address, slot_of = build_requests(
        pack, rows_here, owner_map, head_ids, tail_ids, neg_ids
    )
    asked = exchange(requests)
    address, slot_of = address.reshape(-1), slot_of.reshape(-1)
    served = serve(pack, rows_here, asked, to_rows(pack, entity_table.T))
    fetched = exchange(served.reshape(owner_count, 1, pack.stride * LANES))
    fetched = fetched.reshape(pack.rows, LANES)
    queries = unpack_heads(pack, edge_count, address, slot_of, fetched, relations[rel_ids].T)
    weight = float(blk_count * neg_count)
    arriving = [to_chip(queries, blk_count, hops) for hops in range(1, chip_count)]
    nearby = [queries, to_sibling(queries, blk_count)]
    positive, negatives, *negative_parts = unpack_rest(pack, neg_count, address, slot_of, fetched, queries)
    near, *near_parts = negative_terms(pack, weight, negative_parts, nearby)
    arriving, near, near_parts = lax.optimization_barrier((arriving, near, near_parts))
    distant = []
    for same in arriving:
        distant += [same, to_sibling(same, blk_count)]
    far, *far_parts = negative_terms(pack, weight, negative_parts, distant)
    totals = [near_parts[0], to_sibling(near_parts[1], blk_count)]
    for hops in range(1, chip_count):
        total = far_parts[2 * hops - 2] + to_sibling(far_parts[2 * hops - 1], blk_count)
        totals.append(to_chip(total, blk_count, chip_count - hops))
    partial, partial_rests = block_gradients(
        pack, address, slot_of, positive, negatives, nearby + distant, (near, far)
    )
    outgoing = finish_gradients(
        pack, address, slot_of, partial, partial_rests, positive, totals
    )
    incoming = exchange(outgoing.reshape(owner_count, 1, pack.stride * LANES))
    new_columns, new_sum = update(
        pack, asked.reshape(1, -1), incoming.reshape(pack.rows, LANES),
        adagrad_sum.reshape(1, -1), entity_table.T,
    )
    return (new_columns.T, new_sum.reshape(-1))


def solution(mesh):
    return jax.shard_map(
        on_device,
        mesh=mesh,
        in_specs=(
            P(("dp", "blk"), None),
            P(("dp", "blk")),
            P(),
            P(),
            P(("dp", "blk")),
            P(("dp", "blk")),
            P(("dp", "blk")),
            P(("dp", "blk")),
        ),
        out_specs=(P(("dp", "blk"), None), P(("dp", "blk"))),
        check_vma=False,
    )
```

```python
import functools

import jax
import jax.numpy as jnp
from jax import lax
from jax.experimental import pallas as pl
from jax.experimental.pallas import tpu as pltpu
from jax.sharding import PartitionSpec as P

MARGIN = 10.0
EPSILON = 1e-05
LEARNING_RATE = 0.1
LANES = 128
SUBLANES = 8
SCORE_STEPS = 2
SERVE_OWNERS = 4
VMEM_BYTES = 24 * 1024 * 1024


class Packing:
    def __init__(self, width, owners, capacity):
        self.width = width
        self.owners = owners
        self.capacity = capacity
        self.full = width // LANES
        self.rest = width - self.full * LANES
        assert 0 < self.rest <= LANES // SUBLANES and capacity % SUBLANES == 0
        self.shared = capacity // SUBLANES
        self.groups = self.full + 1
        self.wide = self.groups * LANES
        self.rests_at = self.full * capacity
        self.stride = self.rests_at + self.shared
        self.slots = owners * capacity
        self.rest_rows = self.slots + SUBLANES
        self.rows = owners * self.stride


def compiler_params():
    return pltpu.CompilerParams(vmem_limit_bytes=VMEM_BYTES)


def vmem():
    return pl.BlockSpec(memory_space=pltpu.VMEM)


def smem():
    return pl.BlockSpec(memory_space=pltpu.SMEM)


def hbm():
    return pl.BlockSpec(memory_space=pltpu.HBM)


def in_hbm(value):
    return pltpu.with_memory_space_constraint(value, pltpu.HBM)


def split(value):
    high = value.astype(jnp.bfloat16)
    low = (value - high.astype(jnp.float32)).astype(jnp.bfloat16)
    return high, low


def dot_halves(left, right, contract):
    numbers = (contract, ((), ()))

    def dot(a, b):
        return lax.dot_general(a, b, numbers, preferred_element_type=jnp.float32)

    return dot(left[0], right[0]) + (dot(left[0], right[1]) + dot(left[1], right[0]))


def loop(count, body):
    def step(index, carry):
        body(index)
        return carry

    lax.fori_loop(0, count, step, 0)


def expand_rests(pack, packed_ref, shared_ref, rests_ref, first_owner=0, owners=None):
    owners = pack.owners if owners is None else owners
    for owner in range(first_owner, first_owner + owners):
        shared_ref[owner * pack.shared : (owner + 1) * pack.shared, :] = packed_ref[
            pl.ds(owner * pack.stride + pack.rests_at, pack.shared), :
        ]
    first = first_owner * pack.shared
    shared = shared_ref[first : first + owners * pack.shared, :]
    lane = lax.broadcasted_iota(jnp.int32, shared.shape, 1)
    for j in range(SUBLANES):
        moved = shared if j == 0 else pltpu.roll(shared, LANES - j * pack.rest, axis=1)
        rows = pl.ds(first * SUBLANES + j, shared.shape[0], stride=SUBLANES)
        rests_ref[rows, :] = jnp.where(lane < pack.rest, moved, 0.0)


def rests_scratch(pack):
    return [
        pltpu.VMEM((pack.owners * pack.shared, LANES), jnp.float32),
        pltpu.VMEM((pack.rest_rows, LANES), jnp.float32),
    ]


def row_columns(pack, rows):
    parts = [rows[:, c, :].T for c in range(pack.groups)]
    return jnp.concatenate(parts, axis=0)[: pack.width]


def one_hot(mask):
    return mask.astype(jnp.float32).astype(jnp.bfloat16)


def request_kernel(
    pack, rows_here, map_hbm, head_hbm, tail_hbm, negative_hbm,
    request_ref, address_ref, slot_ref, map_ref, ids_ref, sems,
):
    copies = [pltpu.make_async_copy(map_hbm, map_ref, sems.at[0])]
    first = 0
    for index, source in enumerate((head_hbm, tail_hbm, negative_hbm)):
        target = ids_ref.at[:, pl.ds(first, source.shape[1])]
        copies.append(pltpu.make_async_copy(source, target, sems.at[index + 1]))
        first += source.shape[1]
    for copy in copies:
        copy.start()
    for copy in copies[1:]:
        copy.wait()
    ids = ids_ref[...]
    count = ids.shape[1]
    lines = map_ref.shape[0]

    def iota(rows, axis):
        return lax.broadcasted_iota(jnp.int32, (rows, count), axis)

    line_chosen = one_hot(iota(lines, 0) == ids // LANES)
    earlier = one_hot(iota(count, 0) < iota(count, 1))
    copies[0].wait()
    table = map_ref[...].T
    digits = [(table >> shift) & 255 for shift in range(0, 24, 8)]
    stacked = jnp.concatenate(digits, axis=0).astype(jnp.float32).astype(jnp.bfloat16)
    found = jnp.dot(stacked, line_chosen, preferred_element_type=jnp.float32)
    found = found[:LANES] + 256.0 * found[LANES : 2 * LANES] + 65536.0 * found[2 * LANES :]
    found = jnp.where(iota(LANES, 0) == ids % LANES, found, 0.0)
    position = jnp.sum(found, axis=0, keepdims=True).astype(jnp.int32)
    owner = position // rows_here
    row = position % rows_here
    to_owner = iota(pack.owners, 0) == owner
    before = jnp.dot(one_hot(to_owner), earlier, preferred_element_type=jnp.float32)
    rank = jnp.sum(jnp.where(to_owner, before, 0.0), axis=0, keepdims=True).astype(jnp.int32)
    slot_ref[...] = owner * pack.capacity + rank
    address_ref[...] = owner * pack.stride + rank * pack.full
    at_rank = one_hot(iota(pack.capacity, 0) == rank)
    absent = row - rows_here

    def place(values):
        chosen = jnp.where(to_owner, values.astype(jnp.float32), 0.0).astype(jnp.bfloat16)
        return lax.dot_general(
            chosen, at_rank, (((1,), (1,)), ((), ())), preferred_element_type=jnp.float32
        )

    high = -((-absent) // 256)
    low = absent - high * 256
    request_ref[:, 0, :] = (place(high) * 256.0 + place(low)).astype(jnp.int32) + rows_here


def build_requests(pack, rows_here, owner_map, head_ids, tail_ids, neg_ids):
    count = head_ids.shape[0] + tail_ids.shape[0] + neg_ids.shape[0]
    shape = jax.ShapeDtypeStruct
    return pl.pallas_call(
        functools.partial(request_kernel, pack, rows_here),
        out_shape=(
            shape((pack.owners, 1, pack.capacity), jnp.int32),
            shape((1, count), jnp.int32),
            shape((1, count), jnp.int32),
        ),
        in_specs=[hbm()] * 4,
        out_specs=(vmem(),) * 3,
        scratch_shapes=[
            pltpu.VMEM((owner_map.shape[0] // LANES, LANES), jnp.int32),
            pltpu.VMEM((1, count), jnp.int32),
            pltpu.SemaphoreType.DMA((4,)),
        ],
        compiler_params=compiler_params(),
        name="build_requests",
    )(
        in_hbm(owner_map.reshape(-1, LANES)), in_hbm(head_ids.reshape(1, -1)),
        in_hbm(tail_ids.reshape(1, -1)), in_hbm(neg_ids.reshape(1, -1)),
    )


def rows_kernel(pack, columns_ref, rows_ref, line_ref):
    count = columns_ref.shape[1]
    fill = jnp.zeros((pack.wide - pack.width, LANES), jnp.float32)
    place = lax.broadcasted_iota(jnp.int32, (LANES // SUBLANES, LANES), 1) // pack.rest
    for block in range(count // LANES):
        at = slice(block * LANES, (block + 1) * LANES)
        tile = jnp.concatenate([columns_ref[:, at], fill], axis=0)
        for c in range(pack.full):
            rows_ref[pl.ds(block * LANES * pack.full + c, LANES, stride=pack.full), :] = tile[
                c * LANES : (c + 1) * LANES
            ].T
        line_ref[:LANES, :] = tile[pack.full * LANES :].T
        shared = line_ref[pl.ds(0, LANES // SUBLANES, stride=SUBLANES), :]
        for j in range(1, SUBLANES):
            rest = line_ref[pl.ds(j, LANES // SUBLANES, stride=SUBLANES), :]
            shared = jnp.where(place == j, pltpu.roll(rest, j * pack.rest, axis=1), shared)
        first = pack.full * (count + SUBLANES) + block * (LANES // SUBLANES)
        rows_ref[first : first + LANES // SUBLANES, :] = shared
    zeros = jnp.zeros((pack.full * SUBLANES, LANES), jnp.float32)
    rows_ref[pack.full * count : pack.full * (count + SUBLANES), :] = zeros
    rows_ref[pack.full * (count + SUBLANES) + count // SUBLANES :, :] = zeros[:SUBLANES]


def to_rows(pack, columns):
    count = columns.shape[1]
    lines = pack.full * (count + SUBLANES) + count // SUBLANES + SUBLANES
    return pl.pallas_call(
        functools.partial(rows_kernel, pack),
        out_shape=pltpu.VMEM((lines, LANES), jnp.float32),
        in_specs=[vmem()],
        out_specs=vmem(),
        scratch_shapes=[pltpu.VMEM((LANES + SUBLANES, LANES), jnp.float32)],
        compiler_params=compiler_params(),
        name="table_rows",
    )(columns)


def sends(pack, out_ref, out_hbm, sems):
    count = sems.shape[0]
    each = pack.owners // count
    copies = []
    for index in range(count):
        rows = pl.ds(index * each * pack.stride, each * pack.stride)
        copies.append(pltpu.make_async_copy(out_ref.at[rows, :], out_hbm.at[rows, :], sems.at[index]))
    return copies, each


def share_rests(pack, rests_ref, out_ref, first_owner, owners):
    count = owners * pack.shared
    first = first_owner * pack.capacity
    shared = rests_ref[pl.ds(first, count, stride=SUBLANES), :]
    place = lax.broadcasted_iota(jnp.int32, shared.shape, 1) // pack.rest
    for j in range(1, SUBLANES):
        block = rests_ref[pl.ds(first + j, count, stride=SUBLANES), :]
        shared = jnp.where(place == j, pltpu.roll(block, j * pack.rest, axis=1), shared)
    for owner in range(owners):
        start = (first_owner + owner) * pack.stride + pack.rests_at
        out_ref[pl.ds(start, pack.shared), :] = shared[
            owner * pack.shared : (owner + 1) * pack.shared
        ]


def serve_kernel(
    pack, rows_here, asked_ref, table_ref, out_hbm, out_ref, rests_ref, table_rests_ref, sems
):
    copies, each = sends(pack, out_ref, out_hbm, sems)
    shared = table_ref[pack.full * (rows_here + SUBLANES) :, :]
    for j in range(SUBLANES):
        moved = shared if j == 0 else pltpu.roll(shared, LANES - j * pack.rest, axis=1)
        table_rests_ref[pl.ds(j, shared.shape[0], stride=SUBLANES), :] = moved

    def body(owner):
        base = owner * pack.stride
        slots = pl.multiple_of(owner * pack.capacity, SUBLANES)
        for first in range(0, pack.capacity, SUBLANES):
            rows = [asked_ref[owner, 0, first + j] for j in range(SUBLANES)]
            values = [table_ref[pl.ds(row * pack.full, pack.full), :] for row in rows]
            rests = [table_rests_ref[pl.ds(row, 1), :] for row in rows]
            for j in range(SUBLANES):
                out_ref[pl.ds(base + (first + j) * pack.full, pack.full), :] = values[j]
            rests_ref[pl.ds(slots + first, SUBLANES), :] = jnp.concatenate(rests, axis=0)

    for index, copy in enumerate(copies):
        def step(some):
            for owner in range(SERVE_OWNERS):
                body(index * each + some * SERVE_OWNERS + owner)

        loop(each // SERVE_OWNERS, step)
        share_rests(pack, rests_ref, out_ref, index * each, each)
        copy.start()
    for copy in copies:
        copy.wait()


def serve(pack, rows_here, asked, table_rows):
    return pl.pallas_call(
        functools.partial(serve_kernel, pack, rows_here),
        out_shape=pltpu.HBM((pack.rows, LANES), jnp.float32),
        in_specs=[smem(), vmem()],
        out_specs=hbm(),
        scratch_shapes=[
            pltpu.VMEM((pack.rows, LANES), jnp.float32),
            pltpu.VMEM((pack.rest_rows, LANES), jnp.float32),
            pltpu.VMEM((rows_here + SUBLANES * (SUBLANES + 1), LANES), jnp.float32),
            pltpu.SemaphoreType.DMA((4,)),
        ],
        compiler_params=compiler_params(),
        name="serve_rows",
    )(asked, pltpu.with_memory_space_constraint(table_rows, pltpu.VMEM))


def copy_rows(pack, first_request, address_ref, slot_ref, packed_ref, rests_ref, rows_ref):
    def body(group):
        first = group * 2 * SUBLANES
        values = []
        for j in range(2 * SUBLANES):
            request = first_request + first + j
            values.append(
                (
                    packed_ref[pl.ds(address_ref[request], pack.full), :],
                    rests_ref[pl.ds(slot_ref[request], 1), :],
                )
            )
        for j, (groups, rest) in enumerate(values):
            rows_ref[first + j, : pack.full, :] = groups
            rows_ref[first + j, pack.full :, :] = rest

    loop(rows_ref.shape[0] // (2 * SUBLANES), body)


def heads_kernel(
    pack, address_ref, slot_ref, packed_ref, relation_ref,
    query_ref, shared_ref, rests_ref, rows_ref,
):
    expand_rests(pack, packed_ref, shared_ref, rests_ref)
    copy_rows(pack, 0, address_ref, slot_ref, packed_ref, rests_ref, rows_ref)
    query_ref[...] = row_columns(pack, rows_ref[...]) + relation_ref[...]


def unpack_heads(pack, edges, address, slot, packed, relation_rows):
    return pl.pallas_call(
        functools.partial(heads_kernel, pack),
        out_shape=jax.ShapeDtypeStruct((pack.width, edges), jnp.float32),
        in_specs=[smem(), smem(), vmem(), vmem()],
        out_specs=vmem(),
        scratch_shapes=rests_scratch(pack)
        + [pltpu.VMEM((edges, pack.groups, LANES), jnp.float32)],
        compiler_params=compiler_params(),
        cost_estimate=pl.CostEstimate(flops=10**7, bytes_accessed=3 * 10**6, transcendentals=0),
        name="unpack_heads",
    )(address, slot, packed, relation_rows)


def rest_kernel(
    pack, edges, address_ref, slot_ref, packed_ref, query_ref,
    positive_ref, negative_ref, high_ref, low_ref, high_columns_ref, low_columns_ref, square_ref,
    shared_ref, rests_ref, rows_ref,
):
    expand_rests(pack, packed_ref, shared_ref, rests_ref)
    copy_rows(pack, edges, address_ref, slot_ref, packed_ref, rests_ref, rows_ref)
    for c in range(pack.groups):
        negative_ref[:, c * LANES : (c + 1) * LANES] = rows_ref[edges:, c, :]
    negatives = negative_ref[...]
    high_ref[...], low_ref[...] = split(negatives)
    high_columns_ref[...], low_columns_ref[...] = split(negatives.T[: pack.width])
    square_ref[...] = jnp.sum(negatives * negatives, axis=1, keepdims=True)
    residue = query_ref[...] - row_columns(pack, rows_ref[:edges])
    distance = jnp.sqrt(jnp.sum(residue * residue, axis=0, keepdims=True) + EPSILON)
    positive_ref[...] = jax.nn.sigmoid(distance - MARGIN) / distance * residue


def unpack_rest(pack, negatives, address, slot, packed, queries):
    edges = queries.shape[1]
    shape = jax.ShapeDtypeStruct
    return pl.pallas_call(
        functools.partial(rest_kernel, pack, edges),
        out_shape=(
            shape((pack.width, edges), jnp.float32),
            shape((negatives, pack.wide), jnp.float32),
            shape((negatives, pack.wide), jnp.bfloat16),
            shape((negatives, pack.wide), jnp.bfloat16),
            shape((pack.width, negatives), jnp.bfloat16),
            shape((pack.width, negatives), jnp.bfloat16),
            shape((negatives, 1), jnp.float32),
        ),
        in_specs=[smem(), smem(), vmem(), vmem()],
        out_specs=(vmem(),) * 7,
        scratch_shapes=rests_scratch(pack)
        + [pltpu.VMEM((edges + negatives, pack.groups, LANES), jnp.float32)],
        compiler_params=compiler_params(),
        cost_estimate=pl.CostEstimate(flops=10**7, bytes_accessed=9 * 10**6, transcendentals=0),
        name="unpack_rest",
    )(address, slot, packed, queries)


def gather_queries(pack, query_refs):
    queries = jnp.concatenate([ref[...] for ref in query_refs], axis=1)
    fill = jnp.zeros((pack.wide - pack.width, queries.shape[1]), jnp.float32)
    return jnp.concatenate([queries, fill], axis=0)


def negatives_kernel(pack, blocks, weight, *refs):
    half_refs = refs[:2]
    column_refs = refs[2:4]
    square_ref = refs[4]
    query_refs = refs[5 : 5 + blocks]
    coefficient_ref, *part_refs = refs[5 + blocks :]
    queries = gather_queries(pack, query_refs)
    query_sq = jnp.sum(queries * queries, axis=0, keepdims=True)
    query_halves = split(queries)
    count = square_ref.shape[0]
    weights, parts = [], []
    for first in range(0, count, count // SCORE_STEPS):
        rows = slice(first, first + count // SCORE_STEPS)
        inner = dot_halves([ref[rows, :] for ref in half_refs], query_halves, ((1,), (0,)))
        squared = jnp.maximum(query_sq + square_ref[rows, :] - 2.0 * inner + EPSILON, EPSILON)
        distance = jnp.sqrt(squared)
        coefficient = -1.0 / ((1.0 + jnp.exp(distance - MARGIN)) * (weight * distance))
        coefficient_ref[rows, :] = coefficient
        weights.append(jnp.sum(coefficient, axis=0, keepdims=True))
        parts.append(
            dot_halves([ref[:, rows] for ref in column_refs], split(coefficient), ((1,), (0,)))
        )
    part = queries[: pack.width] * sum(weights) - sum(parts)
    width = query_refs[0].shape[1]
    for index, ref in enumerate(part_refs):
        ref[...] = part[:, index * width : (index + 1) * width]


def negative_terms(pack, weight, negative_parts, queries):
    shape = jax.ShapeDtypeStruct
    count = sum(q.shape[1] for q in queries)
    rows = negative_parts[0].shape[0]
    return pl.pallas_call(
        functools.partial(negatives_kernel, pack, len(queries), weight),
        out_shape=(shape((rows, count), jnp.float32),)
        + tuple(shape(q.shape, jnp.float32) for q in queries),
        in_specs=[vmem()] * (len(negative_parts) + len(queries)),
        out_specs=(vmem(),) * (1 + len(queries)),
        compiler_params=compiler_params(),
        cost_estimate=pl.CostEstimate(
            flops=12 * rows * count * pack.wide, bytes_accessed=4 * 10**6, transcendentals=0
        ),
        name="negative_terms",
    )(*negative_parts, *queries)


def store_rows(pack, first_request, address_ref, slot_ref, rows_ref, out_ref, rests_ref):
    def body(group):
        first = group * 2 * SUBLANES
        values = [rows_ref[first + j] for j in range(2 * SUBLANES)]
        for j, value in enumerate(values):
            request = first_request + first + j
            out_ref[pl.ds(address_ref[request], pack.full), :] = value[: pack.full]
            rests_ref[pl.ds(slot_ref[request], 1), :] = value[pack.full :]

    loop(rows_ref.shape[0] // (2 * SUBLANES), body)


def store_columns(pack, columns, rows_ref):
    fill = jnp.zeros((pack.wide - pack.width, columns.shape[1]), jnp.float32)
    columns = jnp.concatenate([columns, fill], axis=0)
    for c in range(pack.groups):
        rows_ref[:, c, :] = columns[c * LANES : (c + 1) * LANES].T


def block_kernel(pack, blocks, coefficients, address_ref, slot_ref, *refs):
    positive_ref, negative_ref = refs[:2]
    query_refs = refs[2 : 2 + blocks]
    coefficient_refs = refs[2 + blocks : 2 + blocks + coefficients]
    out_ref, rests_ref, rows_ref = refs[2 + blocks + coefficients :]
    edges = positive_ref.shape[1]
    out_ref[...] = jnp.zeros_like(out_ref)
    rests_ref[...] = jnp.zeros_like(rests_ref)
    store_columns(pack, -positive_ref[...], rows_ref.at[:edges])
    coefficient = jnp.concatenate([ref[...] for ref in coefficient_refs], axis=1)
    block_grad = negative_ref[...] * jnp.sum(coefficient, axis=1, keepdims=True) - dot_halves(
        split(coefficient), split(gather_queries(pack, query_refs)), ((1,), (1,))
    )
    for c in range(pack.groups):
        rows_ref[edges:, c, :] = block_grad[:, c * LANES : (c + 1) * LANES]
    store_rows(pack, edges, address_ref, slot_ref, rows_ref, out_ref, rests_ref)


def block_gradients(pack, address, slot, positive, negatives, queries, coefficients):
    shape = jax.ShapeDtypeStruct
    rows = positive.shape[1] + negatives.shape[0]
    flops = 6 * sum(c.size for c in coefficients) * pack.wide
    return pl.pallas_call(
        functools.partial(block_kernel, pack, len(queries), len(coefficients)),
        out_shape=(
            shape((pack.rows, LANES), jnp.float32),
            shape((pack.rest_rows, LANES), jnp.float32),
        ),
        in_specs=[smem()] * 2 + [vmem()] * (2 + len(queries) + len(coefficients)),
        out_specs=(vmem(), vmem()),
        scratch_shapes=[pltpu.VMEM((rows, pack.groups, LANES), jnp.float32)],
        compiler_params=compiler_params(),
        cost_estimate=pl.CostEstimate(
            flops=flops, bytes_accessed=10**7, transcendentals=0
        ),
        name="block_gradients",
    )(address, slot, positive, negatives, *queries, *coefficients)


def finish_kernel(pack, parts, address_ref, slot_ref, *refs):
    positive_ref = refs[2]
    part_refs = refs[3 : 3 + parts]
    out_hbm, out_ref, rests_ref, rows_ref, sems = refs[3 + parts :]
    copies, each = sends(pack, out_ref, out_hbm, sems)
    total = positive_ref[...]
    for ref in part_refs:
        total = total + ref[...]
    store_columns(pack, total, rows_ref)
    store_rows(pack, 0, address_ref, slot_ref, rows_ref, out_ref, rests_ref)
    for index, copy in enumerate(copies):
        share_rests(pack, rests_ref, out_ref, index * each, each)
        copy.start()
    for copy in copies:
        copy.wait()


def finish_gradients(pack, address, slot, partial, partial_rests, positive, parts):
    edges = positive.shape[1]
    shape = jax.ShapeDtypeStruct
    return pl.pallas_call(
        functools.partial(finish_kernel, pack, len(parts)),
        out_shape=(
            pltpu.HBM((pack.rows, LANES), jnp.float32),
            shape(partial.shape, jnp.float32),
            shape(partial_rests.shape, jnp.float32),
        ),
        in_specs=[smem()] * 2 + [vmem()] * (3 + len(parts)),
        out_specs=(hbm(), vmem(), vmem()),
        input_output_aliases={2: 1, 3: 2},
        scratch_shapes=[
            pltpu.VMEM((edges, pack.groups, LANES), jnp.float32),
            pltpu.SemaphoreType.DMA((4,)),
        ],
        compiler_params=compiler_params(),
        name="finish_gradients",
    )(address, slot, partial, partial_rests, positive, *parts)[0]


def update_kernel(
    pack, columns, asked_ref, packed_hbm, sum_ref, table_ref, new_table_hbm, new_sum_ref,
    packed_ref, shared_ref, rests_ref, rows_ref, halves_ref, out_ref, sems, packed_sems,
):
    pieces = packed_sems.shape[0]
    owners = pack.owners // pieces
    loads = []
    for index in range(pieces):
        at = pl.ds(index * owners * pack.stride, owners * pack.stride)
        loads.append(
            pltpu.make_async_copy(packed_hbm.at[at, :], packed_ref.at[at, :], packed_sems.at[index])
        )
        loads[-1].start()
    width = pack.width
    for index, load in enumerate(loads):
        load.wait()
        expand_rests(pack, packed_ref, shared_ref, rests_ref, index * owners, owners)
        for owner in range(index * owners, (index + 1) * owners):
            rows = slice(owner * pack.capacity, (owner + 1) * pack.capacity)
            for c in range(pack.full):
                rows_ref[rows, c * LANES : (c + 1) * LANES] = packed_ref[
                    pl.ds(owner * pack.stride + c, pack.capacity, stride=pack.full), :
                ]
            rows_ref[rows, pack.full * LANES :] = rests_ref[rows, :]
        slots = slice(index * owners * pack.capacity, (index + 1) * owners * pack.capacity)
        high, low = split(rows_ref[slots, :])
        halves_ref[:width, slots] = high.T[:width]
        halves_ref[width:, slots] = low.T[:width]
    asked = asked_ref[...]
    row = lax.broadcasted_iota(jnp.int32, (columns, pack.slots), 0)
    copies = []
    for index in range(table_ref.shape[1] // columns):
        at = slice(index * columns, (index + 1) * columns)
        chosen = one_hot(row == asked - index * columns)
        both = lax.dot_general(
            halves_ref[...], chosen, (((1,), (1,)), ((), ())), preferred_element_type=jnp.float32
        )
        summed = both[:width] + both[width:]
        new_sum = sum_ref[:, at] + jnp.sum(summed * summed, axis=0, keepdims=True) / width
        new_sum_ref[:, at] = new_sum
        out_ref[:, at] = table_ref[:, at] - summed * (LEARNING_RATE / jnp.sqrt(new_sum))
        copies.append(
            pltpu.make_async_copy(out_ref.at[:, at], new_table_hbm.at[:, at], sems.at[index])
        )
        copies[-1].start()
    for copy in copies:
        copy.wait()


def update(pack, asked, packed, adagrad_sum, table_columns):
    width, rows = table_columns.shape
    columns = 256
    shape = jax.ShapeDtypeStruct
    return pl.pallas_call(
        functools.partial(update_kernel, pack, columns),
        out_shape=(pltpu.HBM((width, rows), jnp.float32), shape((1, rows), jnp.float32)),
        in_specs=[vmem(), hbm(), vmem(), vmem()],
        out_specs=(hbm(), vmem()),
        scratch_shapes=[pltpu.VMEM((pack.rows, LANES), jnp.float32)]
        + rests_scratch(pack)
        + [
            pltpu.VMEM((pack.slots, pack.wide), jnp.float32),
            pltpu.VMEM((2 * width, pack.slots), jnp.bfloat16),
            pltpu.VMEM((width, rows), jnp.float32),
            pltpu.SemaphoreType.DMA((rows // columns,)),
            pltpu.SemaphoreType.DMA((2,)),
        ],
        compiler_params=compiler_params(),
        name="update_table",
    )(asked, in_hbm(packed), adagrad_sum, table_columns)


def exchange(payload):
    return lax.all_to_all(payload, ("dp", "blk"), split_axis=0, concat_axis=0, tiled=True)


def to_sibling(value, blk_count):
    return lax.ppermute(value, "blk", [(i, i ^ 1) for i in range(blk_count)])


def to_chip(value, blk_count, hops):
    return lax.ppermute(
        value, "blk", [(i, (i + 2 * hops) % blk_count) for i in range(blk_count)]
    )


def on_device(
    entity_table, adagrad_sum, relations, owner_map, head_ids, rel_ids, tail_ids, neg_ids
):
    dp_count = lax.axis_size("dp")
    blk_count = lax.axis_size("blk")
    owner_count = dp_count * blk_count
    chip_count = blk_count // 2
    rows_here, width = entity_table.shape
    edge_count = head_ids.shape[0]
    neg_count = neg_ids.shape[0]
    request_count = 2 * edge_count + neg_count
    capacity = -(-2 * request_count // owner_count // SUBLANES) * SUBLANES
    pack = Packing(width, owner_count, capacity)
    requests, address, slot_of = build_requests(
        pack, rows_here, owner_map, head_ids, tail_ids, neg_ids
    )
    asked = exchange(requests)
    address, slot_of = address.reshape(-1), slot_of.reshape(-1)
    served = serve(pack, rows_here, asked, to_rows(pack, entity_table.T))
    fetched = exchange(served.reshape(owner_count, 1, pack.stride * LANES))
    fetched = fetched.reshape(pack.rows, LANES)
    queries = unpack_heads(pack, edge_count, address, slot_of, fetched, relations[rel_ids].T)
    weight = float(blk_count * neg_count)
    arriving = [to_chip(queries, blk_count, hops) for hops in range(1, chip_count)]
    nearby = [queries, to_sibling(queries, blk_count)]
    positive, negatives, *negative_parts = unpack_rest(pack, neg_count, address, slot_of, fetched, queries)
    near, *near_parts = negative_terms(pack, weight, negative_parts, nearby)
    arriving, near, near_parts = lax.optimization_barrier((arriving, near, near_parts))
    distant = []
    for same in arriving:
        distant += [same, to_sibling(same, blk_count)]
    far, *far_parts = negative_terms(pack, weight, negative_parts, distant)
    totals = [near_parts[0], to_sibling(near_parts[1], blk_count)]
    for hops in range(1, chip_count):
        total = far_parts[2 * hops - 2] + to_sibling(far_parts[2 * hops - 1], blk_count)
        totals.append(to_chip(total, blk_count, chip_count - hops))
    partial, partial_rests = block_gradients(
        pack, address, slot_of, positive, negatives, nearby + distant, (near, far)
    )
    outgoing = finish_gradients(
        pack, address, slot_of, partial, partial_rests, positive, totals
    )
    incoming = exchange(outgoing.reshape(owner_count, 1, pack.stride * LANES))
    new_columns, new_sum = update(
        pack, asked.reshape(1, -1), incoming.reshape(pack.rows, LANES),
        adagrad_sum.reshape(1, -1), entity_table.T,
    )
    return (new_columns.T, new_sum.reshape(-1))


def solution(mesh):
    return jax.shard_map(
        on_device,
        mesh=mesh,
        in_specs=(
            P(("dp", "blk"), None),
            P(("dp", "blk")),
            P(),
            P(),
            P(("dp", "blk")),
            P(("dp", "blk")),
            P(("dp", "blk")),
            P(("dp", "blk")),
        ),
        out_specs=(P(("dp", "blk"), None), P(("dp", "blk"))),
        check_vma=False,
    )
```
